32 devices in a mesh: ctx: 8 (over z, y), head: 4 (over x, core).
Axes of the slice: x: 2, y: 2, z: 4, core: 2. Of those that a mesh axis runs over, the one named last changes fastest.
Arguments:
- features: bfloat16 [2048, 1024], P('ctx', 'head'), may hold values from -30 to 30
- w_qkv: bfloat16 [1024, 3, 1024], P(None, None, 'head'), may hold values from -1 to 1
- block_links: int32 [16, 9], P('ctx'), may hold values from -1 to 15, as said below
- d_out: bfloat16 [2048, 1024], P('ctx', 'head'), may hold values from -6 to 6
Outputs:
- attended: bfloat16 [2048, 1024], P('ctx', 'head')
- grad_features: bfloat16 [2048, 1024], P('ctx', 'head')
The draws below stay inside these ranges and needn't reach their ends.
Inputs may be any that keep to these rules, and one draw needn't show every extreme that they name: `block_links`: row q lists in order the key blocks q - 1 to q + 1; then p - 1 to p + 1, p being the block on the previous coil turn; then n - 1 to n + 1, n being the block on the next coil turn. q - p and n - q lie between 3 and 5, and a distance of 5 occurs in both directions in every draw. A coil neighbour may be absent; the entries of an absent neighbour and entries outside the sequence are -1. Live entries of a row are distinct.
All inputs are finite; a program needn't handle non-finite values.
Results may differ from the reference program's by a relative error of at most 0.025.
Values may be sent and summed in bfloat16 or wider, within the bound.
No kernel may reach another device: no remote copies, remote signals or barrier semaphores. Data moves between devices by JAX's collectives and lax.ppermute only.
A program may use at most 64 MiB of HBM per device.

```python
import jax
import jax.numpy as jnp
from jax import lax

D = 1024
HEADS = 8
HD = 128
BLK = 128
BPD = 2
TURN = 4
JIT = 1
BAND = 1
WIN = 1
TOKENS = 2048
NBLK = 16
NB = 9
REACH = 6


def draw_features(key, part):
    key_base = jax.random.fold_in(jax.random.fold_in(key, 11), 0)
    drawn = jnp.clip(jax.random.normal(key_base, (NBLK, BLK, D), jnp.float32), -6.0, 6.0)
    return drawn.reshape(NBLK * BLK, D).astype(jnp.bfloat16)


def draw_w_qkv(key, part):
    key_base = jax.random.fold_in(jax.random.fold_in(key, 23), 0)
    fan_scale = D ** (-0.5)
    base = jnp.clip(jax.random.normal(key_base, (D, 3, D), jnp.float32), -6.0, 6.0)
    return (base * fan_scale).astype(jnp.bfloat16)


def draw_block_links(key, part):
    key_back, key_ahead, key_back_live, key_ahead_live = jax.random.split(jax.random.fold_in(key, 37), 4)
    rows_all = jnp.arange(NBLK, dtype=jnp.int32)
    back = jax.random.randint(key_back, (NBLK,), TURN - JIT, TURN + JIT + 1).astype(jnp.int32)
    ahead = jax.random.randint(key_ahead, (NBLK,), TURN - JIT, TURN + JIT + 1).astype(jnp.int32)
    back_live = jax.random.randint(key_back_live, (NBLK,), 0, 4) > 0
    ahead_live = jax.random.randint(key_ahead_live, (NBLK,), 0, 4) > 0
    ahead = ahead.at[BPD - 1].set(TURN + JIT)
    ahead_live = ahead_live.at[BPD - 1].set(True)
    back = back.at[NBLK - BPD].set(TURN + JIT)
    back_live = back_live.at[NBLK - BPD].set(True)
    band_steps = jnp.arange(-BAND, BAND + 1, dtype=jnp.int32)[None, :]
    window_steps = jnp.arange(-WIN, WIN + 1, dtype=jnp.int32)[None, :]
    band_links = rows_all[:, None] + band_steps
    prior_links = jnp.where(back_live[:, None], (rows_all - back)[:, None] + window_steps, -1)
    later_links = jnp.where(ahead_live[:, None], (rows_all + ahead)[:, None] + window_steps, -1)
    links_all = jnp.concatenate([band_links, prior_links, later_links], axis=1)
    links_all = jnp.where((links_all >= 0) & (links_all < NBLK), links_all, -1)
    return links_all.astype(jnp.int32)


def shard_levels(stream_key, extent, pieces, low, top_value):
    def one(position, blocks):
        steps = jax.random.uniform(jax.random.fold_in(jax.random.fold_in(stream_key, 6), position), (blocks,), jnp.float32, low / len(pieces), top_value / len(pieces))
        return jnp.repeat(jnp.exp(steps), extent[position] // blocks).reshape((-1,) + (1,) * (len(extent) - position - 1))

    level = one(*pieces[0])
    for cut in pieces[1:]:
        level = level * one(*cut)
    return level


def scatter_about(stream_key, extent, deviation, bound, cuts=(), kind=jnp.bfloat16):
    values = deviation * jax.random.normal(stream_key, extent, jnp.float32)
    if cuts:
        values = values * shard_levels(stream_key, extent, cuts, -0.22, 0.18)
    return jnp.clip(values, -bound, bound).astype(kind)


def setup_inputs(seed: int = 0) -> dict:
    arg_keys = jax.random.split(jax.random.key(seed), 5)
    return {
        "features": draw_features(jax.random.fold_in(arg_keys[4], 71), 0),
        "w_qkv": draw_w_qkv(jax.random.fold_in(arg_keys[4], 71), 0),
        "block_links": draw_block_links(jax.random.fold_in(arg_keys[4], 71), 0),
        "d_out": scatter_about(arg_keys[3], (TOKENS, D), 1.0, 6.0, ((0, 8), (1, 4))),
    }


def rounded(values):
    return lax.optimization_barrier(values.astype(jnp.bfloat16)).astype(jnp.float32)


def reference(features, w_qkv, block_links, d_out):
    model_width = features.shape[1]
    w_flat = w_qkv.reshape(model_width, 3 * model_width)
    projected = jnp.dot(features, w_flat, preferred_element_type=jnp.float32).astype(jnp.bfloat16)
    block_shape = (NBLK, BLK, HEADS, HD)
    queries = projected[:, :model_width].reshape(block_shape)
    keys = projected[:, model_width:2 * model_width].reshape(block_shape)
    values = projected[:, 2 * model_width:].reshape(block_shape)
    grads = d_out.reshape(block_shape)
    score_scale = HD ** -0.5
    window_len = BPD + 2 * REACH
    window_shape = (window_len, BLK, HEADS, HD)
    group_count = NBLK // BPD

    def visit_group(running, inputs):
        key_acc, value_acc = running
        query_group, grad_group, link_group, group_index = inputs
        window_base = group_index * BPD - REACH

        def visit(window_sums, inner):
            key_win, value_win = window_sums
            query_block, grad_block, link_row = inner
            live_slot = link_row >= 0
            slot_index = jnp.where(live_slot, link_row, 0).astype(jnp.int32)
            local_index = jnp.where(live_slot, link_row - window_base, 0).astype(jnp.int32)
            picked_lookup_rows = keys[slot_index].reshape(NB * BLK, HEADS, HD).astype(jnp.float32)
            picked_content_rows = values[slot_index].reshape(NB * BLK, HEADS, HD).astype(jnp.float32)
            query_f = query_block.astype(jnp.float32)
            grad_f = grad_block.astype(jnp.float32)
            scores = jnp.einsum("qhd,khd->hqk", query_f, picked_lookup_rows) * score_scale
            key_mask = jnp.repeat(live_slot, BLK)[None, None, :]
            largest = jnp.max(jnp.where(key_mask, scores, -1e30), axis=-1, keepdims=True)
            exp_terms = jnp.where(key_mask, jnp.exp(scores - largest), 0.0)
            normalized = exp_terms / jnp.sum(exp_terms, axis=-1, keepdims=True)
            softmax_share = rounded(normalized)
            attended = jnp.einsum("hqk,khd->qhd", softmax_share, picked_content_rows).astype(jnp.bfloat16)
            row_dot = jnp.sum(grad_f * attended.astype(jnp.float32), axis=-1)
            value_part = jnp.einsum("hqk,qhd->khd", softmax_share, grad_f)
            probability_gradient = jnp.einsum("qhd,khd->hqk", grad_f, picked_content_rows)
            score_derivative = rounded(normalized * (probability_gradient - row_dot.T[:, :, None]))
            query_grad = (jnp.einsum("hqk,khd->qhd", score_derivative, picked_lookup_rows) * score_scale).astype(jnp.bfloat16)
            key_part = jnp.einsum("hqk,qhd->khd", score_derivative, query_f) * score_scale
            live_gate = live_slot.astype(key_part.dtype)[:, None, None, None]
            key_part = key_part.reshape(NB, BLK, HEADS, HD) * live_gate
            value_part = value_part.reshape(NB, BLK, HEADS, HD) * live_gate
            key_win = key_win.at[local_index].add(key_part)
            value_win = value_win.at[local_index].add(value_part)
            return (key_win, value_win), (attended, query_grad)

        start_win = (jnp.zeros(window_shape, jnp.float32), jnp.zeros(window_shape, jnp.float32))
        (key_win, value_win), (attended, query_grad) = lax.scan(
            visit, start_win, (query_group, grad_group, link_group))
        acc_start = (group_index * BPD).astype(jnp.int32)
        zero_index = jnp.zeros((), jnp.int32)
        starts = (acc_start, zero_index, zero_index, zero_index)
        key_old = lax.dynamic_slice(key_acc, starts, window_shape)
        value_old = lax.dynamic_slice(value_acc, starts, window_shape)
        key_acc = lax.dynamic_update_slice(key_acc, key_old + rounded(key_win), starts)
        value_acc = lax.dynamic_update_slice(value_acc, value_old + rounded(value_win), starts)
        return (key_acc, value_acc), (attended, query_grad)

    padded_shape = (NBLK + 2 * REACH, BLK, HEADS, HD)
    start_sums = (jnp.zeros(padded_shape, jnp.float32), jnp.zeros(padded_shape, jnp.float32))
    group_shape = (group_count, BPD, BLK, HEADS, HD)
    (key_acc, value_acc), (attended, query_grad) = lax.scan(
        visit_group, start_sums,
        (queries.reshape(group_shape), grads.reshape(group_shape),
         block_links.reshape(group_count, BPD, NB), jnp.arange(group_count, dtype=jnp.int32)))
    key_acc = key_acc[REACH:REACH + NBLK]
    value_acc = value_acc[REACH:REACH + NBLK]
    total_rows = NBLK * BLK
    grad_projected = jnp.concatenate([
        query_grad.reshape(total_rows, model_width),
        key_acc.astype(jnp.bfloat16).reshape(total_rows, model_width),
        value_acc.astype(jnp.bfloat16).reshape(total_rows, model_width)], axis=1)
    grad_features = jnp.dot(grad_projected, w_flat.T, preferred_element_type=jnp.float32).astype(jnp.bfloat16)
    return attended.reshape(total_rows, model_width), grad_features
```

```python
import functools

import jax
import jax.numpy as jnp
from jax import lax
from jax.experimental import pallas as pl
from jax.experimental.pallas import tpu as pltpu
from jax.sharding import PartitionSpec as P

HD = 128
BLK = 128
REACH = 6
SPAN = 3
LOG2E = 1.4426950408889634
DEAD = -1e30
BF = jnp.bfloat16
F32 = jnp.float32

GROUP = 4
ROWS = GROUP * BLK
HALF = ROWS // 2
WINDOW = GROUP + 2 * REACH
NEAR_LEFT = (REACH - GROUP) * BLK
OWN = REACH * BLK
NEAR_RIGHT = OWN + ROWS
FAR_RIGHT = NEAR_RIGHT + ROWS


def params(flops, moved):
    return dict(
        compiler_params=pltpu.CompilerParams(vmem_limit_bytes=48 * 1024 * 1024),
        cost_estimate=pl.CostEstimate(flops=flops, bytes_accessed=moved, transcendentals=0),
    )


VMEM = pl.BlockSpec(memory_space=pltpu.VMEM)
SMEM = pl.BlockSpec(memory_space=pltpu.SMEM)


def dot(a, b, dims):
    return lax.dot_general(a, b, (dims, ((), ())), preferred_element_type=F32)


def project_kernel(place, f, sx, sy, sd, other, w, q_out, kv_out):
    side, head = place[0], place[3]
    width = f.shape[1]
    for group, near, far in ((0, f, sx), (1, sy, sd)):
        total = None
        pieces = (
            (head, near[...]),
            (head ^ 2, far[...]),
            (head ^ 1, other[2 * group * HALF : (2 * group + 1) * HALF]),
            (head ^ 3, other[(2 * group + 1) * HALF : (2 * group + 2) * HALF]),
        )
        for source, piece in pieces:
            term = dot(piece, w[pl.ds(pl.multiple_of(source * width, width), width), :], ((1,), (0,)))
            total = term if total is None else total + term
        rows = pl.ds(pl.multiple_of((side ^ group) * HALF, HALF), HALF)
        q_out[rows, :] = total[:, :HD].astype(BF)
        kv_out[rows, :] = total[:, HD:].astype(BF)


def attend_kernel(
    place, links, q, kv, near_a, near_b, far_a, far_b, d_own, d_other,
    att_own, att_other, dq_out, own_out, a_out, b_out, far_a_out, far_b_out,
    win, acc, att,
):
    side, odd, first = place[0], place[1], place[2]
    scale = HD ** -0.5
    even = 1 - odd
    at_a = pl.multiple_of(even * NEAR_RIGHT + odd * NEAR_LEFT, BLK)
    at_b = pl.multiple_of(odd * NEAR_RIGHT + even * NEAR_LEFT, BLK)
    at_far_a = pl.multiple_of(even * FAR_RIGHT, BLK)
    at_far_b = pl.multiple_of(odd * FAR_RIGHT, BLK)
    win[OWN : OWN + ROWS, :] = kv[...]
    win[pl.ds(at_a, ROWS), :] = near_a[...]
    win[pl.ds(at_b, ROWS), :] = near_b[...]
    win[pl.ds(at_far_a, HALF), :] = far_a[...]
    win[pl.ds(at_far_b, HALF), :] = far_b[...]
    acc[...] = jnp.zeros_like(acc)
    zeros = jnp.zeros((BLK, HD), BF)
    own_cols = pl.ds(pl.multiple_of(side * HD, HD), HD)
    for i in range(GROUP):
        rows = slice(i * BLK, (i + 1) * BLK)
        here = slice((i % 2) * BLK, (i % 2 + 1) * BLK)
        d_blk = jnp.where(side == i // 2, d_own[here, own_cols], d_other[here, :])
        pair = jnp.concatenate(
            [
                jnp.concatenate([q[rows, :], zeros], axis=1),
                jnp.concatenate([zeros, d_blk], axis=1),
            ],
            axis=0,
        )
        starts, both, scores = [], [], []
        for t in range(3):
            if t == 0:
                start = (REACH + i - 1) * BLK
            else:
                base = jnp.int32(-(1 << 20))
                for j in range(SPAN):
                    entry = links[i, SPAN * t + j]
                    base = jnp.maximum(base, jnp.where(entry >= 0, entry - j, -(1 << 20)))
                base = jnp.where(base > -(1 << 19), base - first + REACH, REACH + i)
                base = jnp.clip(base, 0, WINDOW - SPAN)
                start = pl.multiple_of(base * BLK, BLK)
            starts.append(start)
            product = dot(win[pl.ds(start, SPAN * BLK), :], pair, ((1,), (1,)))
            both.append(product[:, BLK:])
            for j in range(SPAN):
                bias = jnp.where(links[i, SPAN * t + j] >= 0, 0.0, DEAD).astype(F32)
                scores.append(product[j * BLK : (j + 1) * BLK, :BLK] + bias)
        scores = jnp.concatenate(scores, axis=0)
        largest = jnp.max(scores, axis=0, keepdims=True)
        terms = jnp.exp2((scores - largest) * (scale * LOG2E))
        share = terms * (1.0 / jnp.sum(terms, axis=0, keepdims=True))
        prob_grad = jnp.concatenate(both, axis=0)
        row_dot = jnp.sum(share * prob_grad, axis=0, keepdims=True)
        score_grad = share * (prob_grad - row_dot)
        mixed = jnp.concatenate([score_grad.astype(BF), share.astype(BF)], axis=1)
        out = None
        for t in range(3):
            part = mixed[t * SPAN * BLK : (t + 1) * SPAN * BLK, :]
            keys = win[pl.ds(starts[t], SPAN * BLK), :]
            term = dot(part, keys, ((0,), (0,)))
            out = term if out is None else out + term
            acc[pl.ds(starts[t], SPAN * BLK), :] += dot(part, pair, ((1,), (0,)))
        att[rows, :] = out[BLK:, HD:].astype(BF)
        dq_out[rows, :] = (out[:BLK, :HD] * scale).astype(BF)
    att_own[...] = att[pl.ds(pl.multiple_of(side * HALF, HALF), HALF), :]
    att_other[...] = att[pl.ds(pl.multiple_of((1 - side) * HALF, HALF), HALF), :]
    factor = jnp.where(lax.broadcasted_iota(jnp.int32, (1, 2 * HD), 1) < HD, scale, 1.0).astype(F32)
    own_out[...] = acc[OWN : OWN + ROWS, :] * factor
    a_out[...] = (acc[pl.ds(at_a, ROWS), :] * factor).astype(BF)
    b_out[...] = (acc[pl.ds(at_b, ROWS), :] * factor).astype(BF)
    far_a_out[...] = (acc[pl.ds(at_far_a, HALF), :] * factor).astype(BF)
    far_b_out[...] = (acc[pl.ds(at_far_b, HALF), :] * factor).astype(BF)


def spread_kernel(place, own, from_a, from_b, dq, w, keep, send):
    side, head = place[0], place[3]
    width = 2 * HD
    dkv = (own[...] + from_a[...].astype(F32) + from_b[...].astype(F32)).astype(BF)
    grads = jnp.concatenate([dq[...], dkv], axis=1)
    for step in range(4):
        dest = head ^ step
        out = dot(grads, w[pl.ds(pl.multiple_of(dest * width, width), width), :], ((1,), (1,))).astype(BF)
        target = keep if step % 2 == 0 else send
        for group in range(2):
            index = 2 * group + step // 2
            part = jnp.where(side == group, out[:HALF], out[HALF:])
            target[index * HALF : (index + 1) * HALF, :] = part


def body(features, w_qkv, block_links, d_out, n_ctx, n_head):
    ctx, head = lax.axis_index("ctx"), lax.axis_index("head")
    side = ctx % 2
    group = ctx // 2
    odd = group % 2
    n_group = n_ctx // 2
    place = jnp.stack([side, odd, group * GROUP, head]).astype(jnp.int32)

    def across(value, flip_ctx, flip_head):
        pairs = [
            (c * n_head + h, (c ^ flip_ctx) * n_head + (h ^ flip_head))
            for c in range(n_ctx)
            for h in range(n_head)
        ]
        return lax.ppermute(value, ("ctx", "head"), pairs)

    def group_swap(value, offset):
        pairs = []
        for low in range(offset, n_group - 1, 2):
            for s in range(2):
                pairs.append((2 * low + s, 2 * low + 2 + s))
                pairs.append((2 * low + 2 + s, 2 * low + s))
        return lax.ppermute(value, "ctx", pairs)

    f = features
    sx = across(f, 0, 2)
    sy = across(f, 1, 0)
    sd = across(f, 1, 2)
    w_sel = lax.dynamic_slice_in_dim(w_qkv, side * HD, HD, axis=2).reshape(w_qkv.shape[0], 3 * HD)
    other = across(jnp.concatenate([f, sx, sy, sd], axis=0), 0, 1)

    q, kv = pl.pallas_call(
        project_kernel,
        name="project",
        out_shape=[
            jax.ShapeDtypeStruct((ROWS, HD), BF),
            jax.ShapeDtypeStruct((ROWS, 2 * HD), BF),
        ],
        in_specs=[SMEM] + [VMEM] * 6,
        out_specs=[VMEM] * 2,
        **params(2 * ROWS * 1024 * 3 * HD, 4 << 20),
    )(place, f, sx, sy, sd, other, w_sel)

    near_a = group_swap(kv, 0)
    near_b = group_swap(kv, 1)
    far_b = group_swap(lax.dynamic_slice_in_dim(near_a, odd * HALF, HALF, axis=0), 1)
    far_a = group_swap(lax.dynamic_slice_in_dim(near_b, (1 - odd) * HALF, HALF, axis=0), 0)

    link_rows = jnp.zeros((16, HD), BF).at[: block_links.shape[0], : block_links.shape[1]].set(
        block_links.astype(BF)
    )
    d_payload = jnp.concatenate(
        [lax.dynamic_slice_in_dim(d_out, (1 - side) * HD, HD, axis=1), link_rows], axis=0
    )
    d_other = across(d_payload, 1, 0)
    other_links = d_other[HALF : HALF + block_links.shape[0], : block_links.shape[1]].astype(jnp.int32)
    links = jnp.where(
        side == 0,
        jnp.concatenate([block_links, other_links], axis=0),
        jnp.concatenate([other_links, block_links], axis=0),
    )

    att_own, att_other, dq, own, near_a_grad, near_b_grad, far_a_grad, far_b_grad = pl.pallas_call(
        attend_kernel,
        name="attend",
        out_shape=[
            jax.ShapeDtypeStruct((HALF, HD), BF),
            jax.ShapeDtypeStruct((HALF, HD), BF),
            jax.ShapeDtypeStruct((ROWS, HD), BF),
            jax.ShapeDtypeStruct((ROWS, 2 * HD), F32),
            jax.ShapeDtypeStruct((ROWS, 2 * HD), BF),
            jax.ShapeDtypeStruct((ROWS, 2 * HD), BF),
            jax.ShapeDtypeStruct((HALF, 2 * HD), BF),
            jax.ShapeDtypeStruct((HALF, 2 * HD), BF),
        ],
        in_specs=[SMEM] * 2 + [VMEM] * 8,
        out_specs=[VMEM] * 8,
        scratch_shapes=[
            pltpu.VMEM((WINDOW * BLK, 2 * HD), BF),
            pltpu.VMEM((WINDOW * BLK, 2 * HD), F32),
            pltpu.VMEM((ROWS, HD), BF),
        ],
        **params(6 * 2 * GROUP * 9 * BLK * BLK * 2 * HD, 4 << 20),
    )(place, links, q, kv, near_a, near_b, far_a, far_b, d_out, d_other[:HALF])

    back_a = group_swap(far_a_grad, 0)
    back_b = group_swap(far_b_grad, 1)

    def add_half(whole, part, start):
        old = lax.dynamic_slice_in_dim(whole, start, HALF, axis=0)
        new = (old.astype(F32) + part.astype(F32)).astype(BF)
        return lax.dynamic_update_slice_in_dim(whole, new, start, axis=0)

    from_b = group_swap(add_half(near_b_grad, back_a, (1 - odd) * HALF), 1)
    from_a = group_swap(add_half(near_a_grad, back_b, odd * HALF), 0)
    att_back = across(att_other, 1, 0)
    attended = jnp.where(
        side == 0,
        jnp.concatenate([att_own, att_back], axis=1),
        jnp.concatenate([att_back, att_own], axis=1),
    )

    keep, send = pl.pallas_call(
        spread_kernel,
        name="spread",
        out_shape=[jax.ShapeDtypeStruct((4 * HALF, 2 * HD), BF)] * 2,
        in_specs=[SMEM] + [VMEM] * 5,
        out_specs=[VMEM] * 2,
        **params(2 * ROWS * 1024 * 3 * HD, 4 << 20),
    )(place, own, from_a, from_b, dq, w_sel)

    arrived = across(send, 0, 1)
    chip = (keep.astype(F32) + arrived.astype(F32)).astype(BF)
    gx = across(chip[HALF : 2 * HALF], 0, 2)
    gy = across(chip[2 * HALF : 3 * HALF], 1, 0)
    gd = across(chip[3 * HALF :], 1, 2)
    grad_features = (
        chip[:HALF].astype(F32) + gx.astype(F32) + gy.astype(F32) + gd.astype(F32)
    ).astype(BF)
    return attended, grad_features


def solution(mesh):
    sizes = dict(mesh.shape)
    return jax.shard_map(
        functools.partial(body, n_ctx=sizes["ctx"], n_head=sizes["head"]),
        mesh=mesh,
        in_specs=(P("ctx", "head"), P(None, None, "head"), P("ctx", None), P("ctx", "head")),
        out_specs=(P("ctx", "head"), P("ctx", "head")),
        check_vma=False,
    )
```

```python
import functools

import jax
import jax.numpy as jnp
from jax import lax
from jax.experimental import pallas as pl
from jax.experimental.pallas import tpu as pltpu
from jax.sharding import PartitionSpec as P

HD = 128
BLK = 128
REACH = 6
SPAN = 3
LOG2E = 1.4426950408889634
DEAD = -1e30
BF = jnp.bfloat16
F32 = jnp.float32

GROUP = 4
ROWS = GROUP * BLK
HALF = ROWS // 2
WINDOW = GROUP + 2 * REACH
NEAR_LEFT = (REACH - GROUP) * BLK
OWN = REACH * BLK
NEAR_RIGHT = OWN + ROWS
FAR_RIGHT = NEAR_RIGHT + ROWS


def params(flops, moved, mebibytes):
    return dict(
        compiler_params=pltpu.CompilerParams(vmem_limit_bytes=mebibytes * 1024 * 1024),
        cost_estimate=pl.CostEstimate(flops=flops, bytes_accessed=moved, transcendentals=0),
    )


VMEM = pl.BlockSpec(memory_space=pltpu.VMEM)
SMEM = pl.BlockSpec(memory_space=pltpu.SMEM)


def dot(a, b, dims):
    return lax.dot_general(a, b, (dims, ((), ())), preferred_element_type=F32)


def pack_kernel(f, sx, sy, sd, out):
    for index, piece in enumerate((f, sx, sy, sd)):
        out[index * HALF : (index + 1) * HALF, :] = piece[...]


def weight_rows(w, source, side, groups):
    width = w.shape[2]
    rows = pl.ds(pl.multiple_of(source * width, width), width)
    cols = pl.ds(pl.multiple_of(side * HD, HD), HD)
    return jnp.concatenate([w[g, rows, cols] for g in groups], axis=1)


def project_kernel(place, pack, other, w, q_out, kv_out):
    side, head = place[0], place[3]
    total = None
    for source, store, index in ((head, pack, 0), (head ^ 2, pack, 1), (head ^ 1, other, 0), (head ^ 3, other, 1)):
        rows = [store[(2 * group + index) * HALF : (2 * group + index + 1) * HALF, :] for group in range(2)]
        term = dot(jnp.concatenate(rows, axis=0), weight_rows(w, source, side, (0, 1, 2)), ((1,), (0,)))
        total = term if total is None else total + term
    for group in range(2):
        rows = pl.ds(pl.multiple_of((side ^ group) * HALF, HALF), HALF)
        part = total[group * HALF : (group + 1) * HALF]
        q_out[rows, :] = part[:, :HD].astype(BF)
        kv_out[rows, :] = part[:, HD:].astype(BF)


def attend_kernel(
    place, links, q, kv, near_a, near_b, far_a, far_b, d_own, d_other,
    att_own, att_other, dq_out, own_out, a_out, b_out, far_a_out, far_b_out,
    win, acc, att,
):
    side, odd, first = place[0], place[1], place[2]
    scale = HD ** -0.5
    even = 1 - odd
    at_a = pl.multiple_of(even * NEAR_RIGHT + odd * NEAR_LEFT, BLK)
    at_b = pl.multiple_of(odd * NEAR_RIGHT + even * NEAR_LEFT, BLK)
    at_far_a = pl.multiple_of(even * FAR_RIGHT, BLK)
    at_far_b = pl.multiple_of(odd * FAR_RIGHT, BLK)
    win[OWN : OWN + ROWS, :] = kv[...]
    win[pl.ds(at_a, ROWS), :] = near_a[...]
    win[pl.ds(at_b, ROWS), :] = near_b[...]
    win[pl.ds(at_far_a, HALF), :] = far_a[...]
    win[pl.ds(at_far_b, HALF), :] = far_b[...]
    acc[...] = jnp.zeros_like(acc)
    zeros = jnp.zeros((BLK, HD), BF)
    own_cols = pl.ds(pl.multiple_of(side * HD, HD), HD)
    for i in range(GROUP):
        rows = slice(i * BLK, (i + 1) * BLK)
        here = slice((i % 2) * BLK, (i % 2 + 1) * BLK)
        d_blk = jnp.where(side == i // 2, d_own[here, own_cols], d_other[here, :])
        pair = jnp.concatenate(
            [
                jnp.concatenate([q[rows, :], zeros], axis=1),
                jnp.concatenate([zeros, d_blk], axis=1),
            ],
            axis=0,
        )
        starts, scores, prob_grads, peaks, biases = [], [], [], [], []
        for t in range(3):
            if t == 0:
                start = (REACH + i - 1) * BLK
            else:
                base = jnp.int32(-(1 << 20))
                for j in range(SPAN):
                    entry = links[i, SPAN * t + j]
                    base = jnp.maximum(base, jnp.where(entry >= 0, entry - j, -(1 << 20)))
                base = jnp.where(base > -(1 << 19), base - first + REACH, REACH + i)
                base = jnp.clip(base, 0, WINDOW - SPAN)
                start = pl.multiple_of(base * BLK, BLK)
            starts.append(start)
            product = dot(win[pl.ds(start, SPAN * BLK), :], pair, ((1,), (1,)))
            for j in range(SPAN):
                block = product[j * BLK : (j + 1) * BLK]
                bias = jnp.where(links[i, SPAN * t + j] >= 0, 0.0, DEAD).astype(F32)
                scores.append(block[:, :BLK])
                prob_grads.append(block[:, BLK:])
                biases.append(bias)
                peaks.append(jnp.max(block[:, :BLK].reshape(BLK // 8, 8, BLK), axis=0) + bias)
        largest = peaks[0]
        for peak in peaks[1:]:
            largest = jnp.maximum(largest, peak)
        largest = jnp.max(largest, axis=0, keepdims=True)
        terms = []
        total = jnp.zeros((8, BLK), F32)
        weighted = jnp.zeros((8, BLK), F32)
        for n in range(3 * SPAN):
            term = jnp.exp2((scores[n] - (largest - biases[n])) * (scale * LOG2E))
            terms.append(term)
            total = total + jnp.sum(term.reshape(BLK // 8, 8, BLK), axis=0)
            weighted = weighted + jnp.sum((term * prob_grads[n]).reshape(BLK // 8, 8, BLK), axis=0)
        inverse = 1.0 / jnp.sum(total, axis=0, keepdims=True)
        row_dot = jnp.sum(weighted, axis=0, keepdims=True) * inverse
        out = None
        for t in range(3):
            parts = []
            for n in range(SPAN * t, SPAN * t + SPAN):
                share = terms[n] * inverse
                grad = share * (prob_grads[n] - row_dot)
                parts.append(jnp.concatenate([grad.astype(BF), share.astype(BF)], axis=1))
            part = jnp.concatenate(parts, axis=0)
            keys = win[pl.ds(starts[t], SPAN * BLK), :]
            term = dot(part, keys, ((0,), (0,)))
            out = term if out is None else out + term
            acc[pl.ds(starts[t], SPAN * BLK), :] += dot(part, pair, ((1,), (0,)))
        att[rows, :] = out[BLK:, HD:].astype(BF)
        dq_out[rows, :] = (out[:BLK, :HD] * scale).astype(BF)
    att_own[...] = att[pl.ds(pl.multiple_of(side * HALF, HALF), HALF), :]
    att_other[...] = att[pl.ds(pl.multiple_of((1 - side) * HALF, HALF), HALF), :]
    factor = jnp.where(lax.broadcasted_iota(jnp.int32, (1, 2 * HD), 1) < HD, scale, 1.0).astype(F32)
    own_out[...] = acc[OWN : OWN + ROWS, :] * factor
    a_out[...] = (acc[pl.ds(at_a, ROWS), :] * factor).astype(BF)
    b_out[...] = (acc[pl.ds(at_b, ROWS), :] * factor).astype(BF)
    far_a_out[...] = (acc[pl.ds(at_far_a, HALF), :] * factor).astype(BF)
    far_b_out[...] = (acc[pl.ds(at_far_b, HALF), :] * factor).astype(BF)


def spread_kernel(place, own, from_a, from_b, dq, w, keep, send):
    side, head = place[0], place[3]
    dkv = (own[...] + from_a[...].astype(F32) + from_b[...].astype(F32)).astype(BF)
    grads = jnp.concatenate([dq[...], dkv], axis=1)
    for step in range(4):
        dest = head ^ step
        out = dot(grads, weight_rows(w, dest, side, (0, 1, 2)), ((1,), (1,))).astype(BF)
        target = keep if step % 2 == 0 else send
        for group in range(2):
            index = 2 * group + step // 2
            part = jnp.where(side == group, out[:HALF], out[HALF:])
            target[index * HALF : (index + 1) * HALF, :] = part


def body(features, w_qkv, block_links, d_out, n_ctx, n_head):
    ctx, head = lax.axis_index("ctx"), lax.axis_index("head")
    side = ctx % 2
    group = ctx // 2
    odd = group % 2
    n_group = n_ctx // 2
    place = jnp.stack([side, odd, group * GROUP, head]).astype(jnp.int32)

    def across(value, flip_ctx, flip_head):
        pairs = [
            (c * n_head + h, (c ^ flip_ctx) * n_head + (h ^ flip_head))
            for c in range(n_ctx)
            for h in range(n_head)
        ]
        return lax.ppermute(value, ("ctx", "head"), pairs)

    def group_swap(value, offset):
        pairs = []
        for low in range(offset, n_group - 1, 2):
            for s in range(2):
                pairs.append((2 * low + s, 2 * low + 2 + s))
                pairs.append((2 * low + 2 + s, 2 * low + s))
        return lax.ppermute(value, "ctx", pairs)

    f = features
    sx = across(f, 0, 2)
    sy = across(f, 1, 0)
    sd = across(f, 1, 2)
    w = jnp.transpose(w_qkv, (1, 0, 2))
    pack = pl.pallas_call(
        pack_kernel,
        name="pack",
        out_shape=jax.ShapeDtypeStruct((4 * f.shape[0], f.shape[1]), BF),
        in_specs=[VMEM] * 4,
        out_specs=VMEM,
        **params(0, 1 << 20, 4),
    )(f, sx, sy, sd)
    other = across(pack, 0, 1)

    q, kv = pl.pallas_call(
        project_kernel,
        name="project",
        out_shape=[
            jax.ShapeDtypeStruct((ROWS, HD), BF),
            jax.ShapeDtypeStruct((ROWS, 2 * HD), BF),
        ],
        in_specs=[SMEM] + [VMEM] * 3,
        out_specs=[VMEM] * 2,
        **params(2 * ROWS * 1024 * 3 * HD, 4 << 20, 8),
    )(place, pack, other, w)

    near_a = group_swap(kv, 0)
    near_b = group_swap(kv, 1)
    far_b = group_swap(lax.dynamic_slice_in_dim(near_a, odd * HALF, HALF, axis=0), 1)
    far_a = group_swap(lax.dynamic_slice_in_dim(near_b, (1 - odd) * HALF, HALF, axis=0), 0)

    link_rows = jnp.zeros((16, HD), BF).at[: block_links.shape[0], : block_links.shape[1]].set(
        block_links.astype(BF)
    )
    d_payload = jnp.concatenate(
        [lax.dynamic_slice_in_dim(d_out, (1 - side) * HD, HD, axis=1), link_rows], axis=0
    )
    d_other = across(d_payload, 1, 0)
    other_links = d_other[HALF : HALF + block_links.shape[0], : block_links.shape[1]].astype(jnp.int32)
    links = jnp.where(
        side == 0,
        jnp.concatenate([block_links, other_links], axis=0),
        jnp.concatenate([other_links, block_links], axis=0),
    )

    att_own, att_other, dq, own, near_a_grad, near_b_grad, far_a_grad, far_b_grad = pl.pallas_call(
        attend_kernel,
        name="attend",
        out_shape=[
            jax.ShapeDtypeStruct((HALF, HD), BF),
            jax.ShapeDtypeStruct((HALF, HD), BF),
            jax.ShapeDtypeStruct((ROWS, HD), BF),
            jax.ShapeDtypeStruct((ROWS, 2 * HD), F32),
            jax.ShapeDtypeStruct((ROWS, 2 * HD), BF),
            jax.ShapeDtypeStruct((ROWS, 2 * HD), BF),
            jax.ShapeDtypeStruct((HALF, 2 * HD), BF),
            jax.ShapeDtypeStruct((HALF, 2 * HD), BF),
        ],
        in_specs=[SMEM] * 2 + [VMEM] * 8,
        out_specs=[VMEM] * 8,
        scratch_shapes=[
            pltpu.VMEM((WINDOW * BLK, 2 * HD), BF),
            pltpu.VMEM((WINDOW * BLK, 2 * HD), F32),
            pltpu.VMEM((ROWS, HD), BF),
        ],
        **params(6 * 2 * GROUP * 9 * BLK * BLK * 2 * HD, 4 << 20, 16),
    )(place, links, q, kv, near_a, near_b, far_a, far_b, d_out, d_other[:HALF])

    back_a = group_swap(far_a_grad, 0)
    back_b = group_swap(far_b_grad, 1)

    def add_half(whole, part, start):
        old = lax.dynamic_slice_in_dim(whole, start, HALF, axis=0)
        new = (old.astype(F32) + part.astype(F32)).astype(BF)
        return lax.dynamic_update_slice_in_dim(whole, new, start, axis=0)

    from_b = group_swap(add_half(near_b_grad, back_a, (1 - odd) * HALF), 1)
    from_a = group_swap(add_half(near_a_grad, back_b, odd * HALF), 0)
    att_back = across(att_other, 1, 0)
    attended = jnp.where(
        side == 0,
        jnp.concatenate([att_own, att_back], axis=1),
        jnp.concatenate([att_back, att_own], axis=1),
    )

    keep, send = pl.pallas_call(
        spread_kernel,
        name="spread",
        out_shape=[jax.ShapeDtypeStruct((4 * HALF, 2 * HD), BF)] * 2,
        in_specs=[SMEM] + [VMEM] * 5,
        out_specs=[VMEM] * 2,
        **params(2 * ROWS * 1024 * 3 * HD, 4 << 20, 8),
    )(place, own, from_a, from_b, dq, w)

    arrived = across(send, 0, 1)
    chip = (keep.astype(F32) + arrived.astype(F32)).astype(BF)
    gx = across(chip[HALF : 2 * HALF], 0, 2)
    gy = across(chip[2 * HALF : 3 * HALF], 1, 0)
    gd = across(chip[3 * HALF :], 1, 2)
    grad_features = (
        chip[:HALF].astype(F32) + gx.astype(F32) + gy.astype(F32) + gd.astype(F32)
    ).astype(BF)
    return attended, grad_features


def solution(mesh):
    sizes = dict(mesh.shape)
    return jax.shard_map(
        functools.partial(body, n_ctx=sizes["ctx"], n_head=sizes["head"]),
        mesh=mesh,
        in_specs=(P("ctx", "head"), P(None, None, "head"), P("ctx", None), P("ctx", "head")),
        out_specs=(P("ctx", "head"), P("ctx", "head")),
        check_vma=False,
    )
```

```python
import functools

import jax
import jax.numpy as jnp
from jax import lax
from jax.experimental import pallas as pl
from jax.experimental.pallas import tpu as pltpu
from jax.sharding import PartitionSpec as P

HD = 128
BLK = 128
REACH = 6
SPAN = 3
LOG2E = 1.4426950408889634
DEAD = -1e30
BF = jnp.bfloat16
F32 = jnp.float32

GROUP = 4
ROWS = GROUP * BLK
HALF = ROWS // 2
WINDOW = GROUP + 2 * REACH
NEAR_LEFT = (REACH - GROUP) * BLK
OWN = REACH * BLK
NEAR_RIGHT = OWN + ROWS
FAR_RIGHT = NEAR_RIGHT + ROWS


def params(flops, moved, mebibytes):
    return dict(
        compiler_params=pltpu.CompilerParams(vmem_limit_bytes=mebibytes * 1024 * 1024),
        cost_estimate=pl.CostEstimate(flops=flops, bytes_accessed=moved, transcendentals=0),
    )


VMEM = pl.BlockSpec(memory_space=pltpu.VMEM)
SMEM = pl.BlockSpec(memory_space=pltpu.SMEM)


def dot(a, b, dims):
    return lax.dot_general(a, b, (dims, ((), ())), preferred_element_type=F32)


def pack_kernel(near, far, begun, out):
    out[:HALF, :] = begun[:HALF, :]
    out[HALF : 2 * HALF, :] = near[...]
    out[2 * HALF : 3 * HALF, :] = begun[HALF:, :]
    out[3 * HALF :, :] = far[...]


def weight_rows(w, source, side, groups):
    width = w.shape[2]
    rows = pl.ds(pl.multiple_of(source * width, width), width)
    cols = pl.ds(pl.multiple_of(side * HD, HD), HD)
    return jnp.concatenate([w[g, rows, cols] for g in groups], axis=1)


def project_near_kernel(place, near, far, w, total, pack):
    rows = jnp.concatenate([near[...], far[...]], axis=0)
    pack[...] = rows
    total[...] = dot(rows, weight_rows(w, place[3], place[0], (0, 1, 2)), ((1,), (0,)))


def project_across_kernel(place, near, far, before, w, total):
    rows = jnp.concatenate([near[...], far[...]], axis=0)
    total[...] = before[...] + dot(rows, weight_rows(w, place[3] ^ 2, place[0], (0, 1, 2)), ((1,), (0,)))


def sibling_product(place, other, w, groups):
    total = None
    for index in range(2):
        rows = [other[(2 * group + index) * HALF : (2 * group + index + 1) * HALF, :] for group in range(2)]
        source = place[3] ^ (1 + 2 * index)
        term = dot(jnp.concatenate(rows, axis=0), weight_rows(w, source, place[0], groups), ((1,), (0,)))
        total = term if total is None else total + term
    return total


def project_kv_kernel(place, other, before, w, first_out, second_out, kv):
    kv[...] = (before[:, HD:] + sibling_product(place, other, w, (1, 2))).astype(BF)
    start = (place[0] ^ (1 - place[1])) * HALF
    first_out[...] = kv[pl.ds(pl.multiple_of(start, HALF), HALF), :]
    second_out[...] = kv[pl.ds(pl.multiple_of(HALF - start, HALF), HALF), :]


def project_q_kernel(place, other, before, w, q_out):
    total = (before[:, :HD] + sibling_product(place, other, w, (0,))).astype(BF)
    for group in range(2):
        rows = pl.ds(pl.multiple_of((place[0] ^ group) * HALF, HALF), HALF)
        q_out[rows, :] = total[group * HALF : (group + 1) * HALF]


def regions(odd):
    even = 1 - odd
    left_lo, left_hi = NEAR_LEFT, NEAR_LEFT + HALF
    right_lo, right_hi = NEAR_RIGHT, NEAR_RIGHT + HALF
    pick = lambda at_even, at_odd: pl.multiple_of(even * at_even + odd * at_odd, HALF)
    return (
        pick(OWN + HALF, OWN),
        pick(OWN, OWN + HALF),
        pick(right_lo, left_hi),
        pick(right_hi, left_lo),
        pick(left_hi, right_lo),
        pick(left_lo, right_hi),
        pick(FAR_RIGHT, 0),
        pick(0, FAR_RIGHT),
    )


def attend_kernel(
    place, links, q, first_kv, second_kv, a1, a2, b1, b2, far_a, far_b, d_own, d_other,
    att_own, att_other, dq_out, first_out, second_out, a1_out, a2_out, b1_out, b2_out, far_a_out, far_b_out,
    win, acc, att,
):
    side, odd, first = place[0], place[1], place[2]
    scale = HD ** -0.5
    places = regions(odd)
    for at, source in zip(places, (first_kv, second_kv, a1, a2, b1, b2, far_a, far_b)):
        win[pl.ds(at, HALF), :] = source[...]
    acc[...] = jnp.zeros_like(acc)
    zeros = jnp.zeros((BLK, HD), BF)
    own_cols = pl.ds(pl.multiple_of(side * HD, HD), HD)
    for i in range(GROUP):
        rows = slice(i * BLK, (i + 1) * BLK)
        here = slice((i % 2) * BLK, (i % 2 + 1) * BLK)
        d_blk = jnp.where(side == i // 2, d_own[here, own_cols], d_other[here, :])
        pair = jnp.concatenate(
            [
                jnp.concatenate([q[rows, :], zeros], axis=1),
                jnp.concatenate([zeros, d_blk], axis=1),
            ],
            axis=0,
        )
        starts, scores, prob_grads, peaks, biases = [], [], [], [], []
        for t in range(3):
            if t == 0:
                start = (REACH + i - 1) * BLK
            else:
                base = jnp.int32(-(1 << 20))
                for j in range(SPAN):
                    entry = links[i, SPAN * t + j]
                    base = jnp.maximum(base, jnp.where(entry >= 0, entry - j, -(1 << 20)))
                base = jnp.where(base > -(1 << 19), base - first + REACH, REACH + i)
                base = jnp.clip(base, 0, WINDOW - SPAN)
                start = pl.multiple_of(base * BLK, BLK)
            starts.append(start)
            product = dot(win[pl.ds(start, SPAN * BLK), :], pair, ((1,), (1,)))
            for j in range(SPAN):
                block = product[j * BLK : (j + 1) * BLK]
                bias = jnp.where(links[i, SPAN * t + j] >= 0, 0.0, DEAD).astype(F32)
                scores.append(block[:, :BLK])
                prob_grads.append(block[:, BLK:])
                biases.append(bias)
                peaks.append(jnp.max(block[:, :BLK].reshape(BLK // 8, 8, BLK), axis=0) + bias)
        largest = peaks[0]
        for peak in peaks[1:]:
            largest = jnp.maximum(largest, peak)
        largest = jnp.max(largest, axis=0, keepdims=True)
        terms = []
        total = jnp.zeros((8, BLK), F32)
        weighted = jnp.zeros((8, BLK), F32)
        for n in range(3 * SPAN):
            term = jnp.exp2((scores[n] - (largest - biases[n])) * (scale * LOG2E))
            terms.append(term)
            total = total + jnp.sum(term.reshape(BLK // 8, 8, BLK), axis=0)
            weighted = weighted + jnp.sum((term * prob_grads[n]).reshape(BLK // 8, 8, BLK), axis=0)
        inverse = 1.0 / jnp.sum(total, axis=0, keepdims=True)
        row_dot = jnp.sum(weighted, axis=0, keepdims=True) * inverse
        out = None
        for t in range(3):
            parts = []
            for n in range(SPAN * t, SPAN * t + SPAN):
                share = terms[n] * inverse
                grad = share * (prob_grads[n] - row_dot)
                parts.append(jnp.concatenate([grad.astype(BF), share.astype(BF)], axis=1))
            part = jnp.concatenate(parts, axis=0)
            keys = win[pl.ds(starts[t], SPAN * BLK), :]
            term = dot(part, keys, ((0,), (0,)))
            out = term if out is None else out + term
            acc[pl.ds(starts[t], SPAN * BLK), :] += dot(part, pair, ((1,), (0,)))
        att[rows, :] = out[BLK:, HD:].astype(BF)
        dq_out[rows, :] = (out[:BLK, :HD] * scale).astype(BF)
    att_own[...] = att[pl.ds(pl.multiple_of(side * HALF, HALF), HALF), :]
    att_other[...] = att[pl.ds(pl.multiple_of((1 - side) * HALF, HALF), HALF), :]
    factor = jnp.where(lax.broadcasted_iota(jnp.int32, (1, 2 * HD), 1) < HD, scale, 1.0).astype(F32)
    targets = (first_out, second_out, a1_out, a2_out, b1_out, b2_out, far_a_out, far_b_out)
    for at, target in zip(places, targets):
        target[...] = (acc[pl.ds(at, HALF), :] * factor).astype(target.dtype)


def spread_send_kernel(place, first_own, second_own, a1, b2, b1, a2, dq, w, send, grads):
    side, odd, head = place[0], place[1], place[3]
    grads[:, :HD] = dq[...]
    first = first_own[...] + a1[...].astype(F32) + b2[...].astype(F32)
    second = second_own[...] + b1[...].astype(F32) + a2[...].astype(F32)
    grads[pl.ds(pl.multiple_of((1 - odd) * HALF, HALF), HALF), HD:] = first.astype(BF)
    grads[pl.ds(pl.multiple_of(odd * HALF, HALF), HALF), HD:] = second.astype(BF)
    spread(grads, w, side, head ^ 1, send)


def spread(grads, w, side, head, target):
    for step in range(2):
        out = dot(grads[...], weight_rows(w, head ^ (2 * step), side, (0, 1, 2)), ((1,), (1,))).astype(BF)
        for group in range(2):
            index = 2 * group + step
            part = jnp.where(side == group, out[:HALF], out[HALF:])
            target[index * HALF : (index + 1) * HALF, :] = part


def spread_keep_kernel(place, grads, w, keep):
    spread(grads, w, place[0], place[3], keep)


def body(features, w_qkv, block_links, d_out, n_ctx, n_head):
    ctx, head = lax.axis_index("ctx"), lax.axis_index("head")
    side = ctx % 2
    group = ctx // 2
    odd = group % 2
    n_group = n_ctx // 2
    place = jnp.stack([side, odd, group * GROUP, head]).astype(jnp.int32)

    def across(value, flip_ctx, flip_head):
        pairs = [
            (c * n_head + h, (c ^ flip_ctx) * n_head + (h ^ flip_head))
            for c in range(n_ctx)
            for h in range(n_head)
        ]
        return lax.ppermute(value, ("ctx", "head"), pairs)

    def group_swap(value, offset):
        pairs = []
        for low in range(offset, n_group - 1, 2):
            for s in range(2):
                pairs.append((2 * low + s, 2 * low + 2 + s))
                pairs.append((2 * low + 2 + s, 2 * low + s))
        return lax.ppermute(value, "ctx", pairs)

    f = features
    sx = across(f, 0, 2)
    sy = across(f, 1, 0)
    sd = across(f, 1, 2)
    w = jnp.transpose(w_qkv, (1, 0, 2))
    def call(kernel, name, outs, ins, moved, mebibytes, flops, scratch=()):
        return pl.pallas_call(
            kernel,
            name=name,
            out_shape=outs,
            in_specs=[SMEM if v.dtype == jnp.int32 else VMEM for v in ins],
            out_specs=jax.tree.map(lambda _: VMEM, outs),
            scratch_shapes=list(scratch),
            **params(flops, moved, mebibytes),
        )(*ins)

    def out(rows, cols, kind=BF):
        return jax.ShapeDtypeStruct((rows, cols), kind)

    product = 2 * ROWS * f.shape[1] * 3 * HD
    total, begun = call(
        project_near_kernel,
        "project_near",
        [out(ROWS, 3 * HD, F32), out(ROWS, f.shape[1])],
        (place, f, sy, w),
        2 << 20,
        8,
        product,
    )
    pack = call(pack_kernel, "pack", out(4 * HALF, f.shape[1]), (sx, sd, begun), 1 << 20, 4, 0)
    other = across(pack, 0, 1)
    total = call(
        project_across_kernel, "project_across", out(ROWS, 3 * HD, F32), (place, sx, sd, total, w), 2 << 20, 8, product
    )
    first, second = call(
        project_kv_kernel, "project_kv", [out(HALF, 2 * HD)] * 2, (place, other, total, w), 2 << 20, 8, product,
        [pltpu.VMEM((ROWS, 2 * HD), BF)],
    )
    a1 = group_swap(first, 0)
    b1 = group_swap(second, 1)
    a2 = group_swap(second, 0)
    b2 = group_swap(first, 1)
    q = call(project_q_kernel, "project_q", out(ROWS, HD), (place, other, total, w), 2 << 20, 8, product)
    far_b = group_swap(a1, 1)
    far_a = group_swap(b1, 0)

    link_rows = jnp.zeros((16, HD), BF).at[: block_links.shape[0], : block_links.shape[1]].set(
        block_links.astype(BF)
    )
    d_payload = jnp.concatenate(
        [lax.dynamic_slice_in_dim(d_out, (1 - side) * HD, HD, axis=1), link_rows], axis=0
    )
    d_other = across(d_payload, 1, 0)
    other_links = d_other[HALF : HALF + block_links.shape[0], : block_links.shape[1]].astype(jnp.int32)
    links = jnp.where(
        side == 0,
        jnp.concatenate([block_links, other_links], axis=0),
        jnp.concatenate([other_links, block_links], axis=0),
    )

    (
        att_own, att_other, dq, first_own, second_own,
        a1_grad, a2_grad, b1_grad, b2_grad, far_a_grad, far_b_grad,
    ) = call(
        attend_kernel,
        "attend",
        [out(HALF, HD)] * 2 + [out(ROWS, HD)] + [out(HALF, 2 * HD, F32)] * 2 + [out(HALF, 2 * HD)] * 6,
        (place, links, q, first, second, a1, a2, b1, b2, far_a, far_b, d_out, d_other[:HALF]),
        4 << 20,
        16,
        6 * 2 * GROUP * 9 * BLK * BLK * 2 * HD,
        [
            pltpu.VMEM((WINDOW * BLK, 2 * HD), BF),
            pltpu.VMEM((WINDOW * BLK, 2 * HD), F32),
            pltpu.VMEM((ROWS, HD), BF),
        ],
    )

    back_a = group_swap(far_a_grad, 0)
    back_b = group_swap(far_b_grad, 1)
    a2_back = group_swap(a2_grad, 0)
    b2_back = group_swap(b2_grad, 1)
    b1_back = group_swap((b1_grad.astype(F32) + back_a.astype(F32)).astype(BF), 1)
    a1_back = group_swap((a1_grad.astype(F32) + back_b.astype(F32)).astype(BF), 0)
    att_back = across(att_other, 1, 0)
    attended = jnp.where(
        side == 0,
        jnp.concatenate([att_own, att_back], axis=1),
        jnp.concatenate([att_back, att_own], axis=1),
    )

    send, grads = call(
        spread_send_kernel,
        "spread_send",
        [out(4 * HALF, 2 * HD), out(ROWS, 3 * HD)],
        (place, first_own, second_own, a1_back, b2_back, b1_back, a2_back, dq, w),
        4 << 20,
        8,
        product,
    )
    keep = call(spread_keep_kernel, "spread_keep", out(4 * HALF, 2 * HD), (place, grads, w), 4 << 20, 8, product)
    arrived = across(send, 0, 1)
    chip = (keep.astype(F32) + arrived.astype(F32)).astype(BF)
    gx = across(chip[HALF : 2 * HALF], 0, 2)
    gy = across(chip[2 * HALF : 3 * HALF], 1, 0)
    gd = across(chip[3 * HALF :], 1, 2)
    grad_features = (
        chip[:HALF].astype(F32) + gx.astype(F32) + gy.astype(F32) + gd.astype(F32)
    ).astype(BF)
    return attended, grad_features


def solution(mesh):
    sizes = dict(mesh.shape)
    return jax.shard_map(
        functools.partial(body, n_ctx=sizes["ctx"], n_head=sizes["head"]),
        mesh=mesh,
        in_specs=(P("ctx", "head"), P(None, None, "head"), P("ctx", None), P("ctx", "head")),
        out_specs=(P("ctx", "head"), P("ctx", "head")),
        check_vma=False,
    )
```

```python
import functools

import jax
import jax.numpy as jnp
from jax import lax
from jax.experimental import pallas as pl
from jax.experimental.pallas import tpu as pltpu
from jax.sharding import PartitionSpec as P

HD = 128
BLK = 128
REACH = 6
SPAN = 3
LOG2E = 1.4426950408889634
DEAD = -1e30
BF = jnp.bfloat16
F32 = jnp.float32

GROUP = 4
ROWS = GROUP * BLK
HALF = ROWS // 2
WINDOW = GROUP + 2 * REACH
NEAR_LEFT = (REACH - GROUP) * BLK
OWN = REACH * BLK
NEAR_RIGHT = OWN + ROWS
FAR_RIGHT = NEAR_RIGHT + ROWS


def params(flops, moved, mebibytes):
    return dict(
        compiler_params=pltpu.CompilerParams(vmem_limit_bytes=mebibytes * 1024 * 1024),
        cost_estimate=pl.CostEstimate(flops=flops, bytes_accessed=moved, transcendentals=0),
    )


VMEM = pl.BlockSpec(memory_space=pltpu.VMEM)
SMEM = pl.BlockSpec(memory_space=pltpu.SMEM)


def dot(a, b, dims):
    return lax.dot_general(a, b, (dims, ((), ())), preferred_element_type=F32)


def begin_kernel(place, sy, f, w, w_mine, fy, total, sems):
    side, head = place[0], place[3]
    copies = [pltpu.make_async_copy(f, fy.at[pl.ds(0, HALF), :], sems.at[3])]
    for g in range(3):
        cols = pl.ds(pl.multiple_of(side * HD, HD), HD)
        copies.append(pltpu.make_async_copy(w.at[g, :, cols], w_mine.at[:, pl.ds(g * HD, HD)], sems.at[g]))
    for copy in copies:
        copy.start()
    fy[HALF:, :] = sy[...]
    for copy in copies:
        copy.wait()
    total[...] = dot(fy[...], weight_rows(w_mine, head, fy.shape[1]), ((1,), (0,)))


def weight_rows(w_mine, source, width):
    return w_mine[pl.ds(pl.multiple_of(source * width, width), width), :]


def pack_kernel(sd, sx, fy, out):
    out[:HALF, :] = fy[:HALF, :]
    out[HALF : 2 * HALF, :] = fy[HALF:, :]
    out[2 * HALF : 3 * HALF, :] = sx[...]
    out[3 * HALF :, :] = sd[...]


def project_across_kernel(place, pack, before, w_mine, total):
    width = pack.shape[1]
    total[...] = before[...] + dot(pack[2 * HALF :, :], weight_rows(w_mine, place[3] ^ 2, width), ((1,), (0,)))


def sibling_product(place, other, w_mine, cols):
    width = other.shape[1]
    total = None
    for index in range(2):
        rows = pl.ds(pl.multiple_of((place[3] ^ (1 + 2 * index)) * width, width), width)
        term = dot(other[2 * index * HALF : 2 * (index + 1) * HALF, :], w_mine[rows, cols], ((1,), (0,)))
        total = term if total is None else total + term
    return total


def store_groups(side, total, target):
    for group in range(2):
        rows = pl.ds(pl.multiple_of((side ^ group) * HALF, HALF), HALF)
        target[rows, :] = total[group * HALF : (group + 1) * HALF]


def project_kv_kernel(place, other, before, w_mine, kv_out):
    total = before[:, HD:] + sibling_product(place, other, w_mine, slice(HD, 3 * HD))
    store_groups(place[0], total.astype(BF), kv_out)


def project_q_kernel(place, other, before, w_mine, q_out):
    total = before[:, :HD] + sibling_product(place, other, w_mine, slice(0, HD))
    store_groups(place[0], total.astype(BF), q_out)


def regions(odd):
    even = 1 - odd
    pick = lambda at_even, at_odd: pl.multiple_of(even * at_even + odd * at_odd, HALF)
    return (
        pick(NEAR_RIGHT, NEAR_LEFT),
        pick(NEAR_LEFT, NEAR_RIGHT),
        pick(FAR_RIGHT, 0),
        pick(0, FAR_RIGHT),
    )


def start_of(links, first, i, t):
    if t == 0:
        return (REACH + i - 1) * BLK
    base = jnp.int32(-(1 << 20))
    for j in range(SPAN):
        entry = links[i, SPAN * t + j]
        base = jnp.maximum(base, jnp.where(entry >= 0, entry - j, -(1 << 20)))
    base = jnp.where(base > -(1 << 19), base - first + REACH, REACH + i)
    base = jnp.clip(base, 0, WINDOW - SPAN)
    return pl.multiple_of(base * BLK, BLK)


def is_far(i, t):
    return t == (1 if i < GROUP // 2 else 2)


def run_rows(i, t):
    return slice((i * 3 + t) * SPAN * BLK, (i * 3 + t + 1) * SPAN * BLK)


def side_factor():
    scale = HD ** -0.5
    return jnp.where(lax.broadcasted_iota(jnp.int32, (1, 2 * HD), 1) < HD, scale, 1.0).astype(F32)


def attend_kernel(
    place, links, q, kv, near_a, near_b, far_a, far_b, d_own, d_other,
    mixed, pairs, win, acc, far_a_out, far_b_out,
):
    side, odd, first = place[0], place[1], place[2]
    scale = HD ** -0.5
    at_a, at_b, at_far_a, at_far_b = regions(odd)
    win[OWN : OWN + ROWS, :] = kv[...]
    win[pl.ds(at_a, ROWS), :] = near_a[...]
    win[pl.ds(at_b, ROWS), :] = near_b[...]
    win[pl.ds(at_far_a, HALF), :] = far_a[...]
    win[pl.ds(at_far_b, HALF), :] = far_b[...]
    acc[...] = jnp.zeros_like(acc)
    zeros = jnp.zeros((BLK, HD), BF)
    own_cols = pl.ds(pl.multiple_of(side * HD, HD), HD)
    for i in range(GROUP):
        rows = slice(i * BLK, (i + 1) * BLK)
        here = slice((i % 2) * BLK, (i % 2 + 1) * BLK)
        d_blk = jnp.where(side == i // 2, d_own[here, own_cols], d_other[here, :])
        pair = jnp.concatenate(
            [
                jnp.concatenate([q[rows, :], zeros], axis=1),
                jnp.concatenate([zeros, d_blk], axis=1),
            ],
            axis=0,
        )
        pairs[2 * i * BLK : 2 * (i + 1) * BLK, :] = pair
        scores, prob_grads, peaks, biases = [], [], [], []
        for t in range(3):
            product = dot(win[pl.ds(start_of(links, first, i, t), SPAN * BLK), :], pair, ((1,), (1,)))
            for j in range(SPAN):
                block = product[j * BLK : (j + 1) * BLK]
                bias = jnp.where(links[i, SPAN * t + j] >= 0, 0.0, DEAD).astype(F32)
                scores.append(block[:, :BLK])
                prob_grads.append(block[:, BLK:])
                biases.append(bias)
                peaks.append(jnp.max(block[:, :BLK].reshape(BLK // 8, 8, BLK), axis=0) + bias)
        largest = peaks[0]
        for peak in peaks[1:]:
            largest = jnp.maximum(largest, peak)
        largest = jnp.max(largest, axis=0, keepdims=True)
        terms = []
        total = jnp.zeros((8, BLK), F32)
        weighted = jnp.zeros((8, BLK), F32)
        for n in range(3 * SPAN):
            term = jnp.exp2((scores[n] - (largest - biases[n])) * (scale * LOG2E))
            terms.append(term)
            total = total + jnp.sum(term.reshape(BLK // 8, 8, BLK), axis=0)
            weighted = weighted + jnp.sum((term * prob_grads[n]).reshape(BLK // 8, 8, BLK), axis=0)
        inverse = 1.0 / jnp.sum(total, axis=0, keepdims=True)
        row_dot = jnp.sum(weighted, axis=0, keepdims=True) * inverse
        for t in range(3):
            parts = []
            for n in range(SPAN * t, SPAN * t + SPAN):
                share = terms[n] * inverse
                grad = share * (prob_grads[n] - row_dot)
                parts.append(jnp.concatenate([grad.astype(BF), share.astype(BF)], axis=1))
            part = jnp.concatenate(parts, axis=0)
            mixed[run_rows(i, t), :] = part
            if is_far(i, t):
                acc[pl.ds(start_of(links, first, i, t), SPAN * BLK), :] += dot(part, pair, ((1,), (0,)))
    factor = side_factor()
    far_a_out[...] = (acc[pl.ds(at_far_a, HALF), :] * factor).astype(BF)
    far_b_out[...] = (acc[pl.ds(at_far_b, HALF), :] * factor).astype(BF)


def near_grads_kernel(place, links, mixed, pairs, far_acc, own_out, a_out, b_out, acc):
    odd, first = place[1], place[2]
    acc[...] = far_acc[...]
    for i in range(GROUP):
        pair = pairs[2 * i * BLK : 2 * (i + 1) * BLK, :]
        for t in range(3):
            if not is_far(i, t):
                at = pl.ds(start_of(links, first, i, t), SPAN * BLK)
                acc[at, :] += dot(mixed[run_rows(i, t), :], pair, ((1,), (0,)))
    factor = side_factor()
    at_a, at_b, _, _ = regions(odd)
    own_out[...] = acc[OWN : OWN + ROWS, :] * factor
    a_out[...] = (acc[pl.ds(at_a, ROWS), :] * factor).astype(BF)
    b_out[...] = (acc[pl.ds(at_b, ROWS), :] * factor).astype(BF)


def outputs_kernel(place, links, mixed, win, att_own, att_other, dq_out, att):
    side, first = place[0], place[2]
    for i in range(GROUP):
        rows = slice(i * BLK, (i + 1) * BLK)
        out = None
        for t in range(3):
            keys = win[pl.ds(start_of(links, first, i, t), SPAN * BLK), :]
            term = dot(mixed[run_rows(i, t), :], keys, ((0,), (0,)))
            out = term if out is None else out + term
        att[rows, :] = out[BLK:, HD:].astype(BF)
        dq_out[rows, :] = (out[:BLK, :HD] * (HD ** -0.5)).astype(BF)
    att_own[...] = att[pl.ds(pl.multiple_of(side * HALF, HALF), HALF), :]
    att_other[...] = att[pl.ds(pl.multiple_of((1 - side) * HALF, HALF), HALF), :]


def spread(grads, w_mine, side, head, target):
    for step in range(2):
        out = dot(grads, weight_rows(w_mine, head ^ (2 * step), 2 * HD), ((1,), (1,))).astype(BF)
        for group in range(2):
            index = 2 * group + step
            part = jnp.where(side == group, out[:HALF], out[HALF:])
            target[index * HALF : (index + 1) * HALF, :] = part


def spread_send_kernel(place, own, from_a, from_b, dq, w_mine, send, grads):
    dkv = (own[...] + from_a[...].astype(F32) + from_b[...].astype(F32)).astype(BF)
    grads[:, :HD] = dq[...]
    grads[:, HD:] = dkv
    spread(grads[...], w_mine, place[0], place[3] ^ 1, send)


def spread_keep_kernel(place, grads, w_mine, keep):
    spread(grads[...], w_mine, place[0], place[3], keep)


def body(features, w_qkv, block_links, d_out, n_ctx, n_head):
    ctx, head = lax.axis_index("ctx"), lax.axis_index("head")
    side = ctx % 2
    group = ctx // 2
    odd = group % 2
    n_group = n_ctx // 2
    place = jnp.stack([side, odd, group * GROUP, head]).astype(jnp.int32)

    def across(value, flip_ctx, flip_head):
        pairs = [
            (c * n_head + h, (c ^ flip_ctx) * n_head + (h ^ flip_head))
            for c in range(n_ctx)
            for h in range(n_head)
        ]
        return lax.ppermute(value, ("ctx", "head"), pairs)

    def group_swap(value, offset):
        pairs = []
        for low in range(offset, n_group - 1, 2):
            for s in range(2):
                pairs.append((2 * low + s, 2 * low + 2 + s))
                pairs.append((2 * low + 2 + s, 2 * low + s))
        return lax.ppermute(value, "ctx", pairs)

    f = features
    sx = across(f, 0, 2)
    sy = across(f, 1, 0)
    sd = across(f, 1, 2)
    w = jnp.transpose(w_qkv, (1, 0, 2))

    def call(kernel, name, outs, ins, mebibytes, flops, scratch=()):
        specs = [SMEM if v.dtype == jnp.int32 else VMEM for v in ins]
        if kernel is begin_kernel:
            specs[2:] = [pl.BlockSpec(memory_space=pltpu.HBM)] * 2
            ins = ins[:2] + tuple(pltpu.with_memory_space_constraint(v, pltpu.HBM) for v in ins[2:])
        return pl.pallas_call(
            kernel,
            name=name,
            out_shape=outs,
            in_specs=specs,
            out_specs=[VMEM] * len(outs),
            scratch_shapes=list(scratch),
            **params(flops, 2 << 20, mebibytes),
        )(*ins)

    def out(rows, cols, kind=BF):
        return jax.ShapeDtypeStruct((rows, cols), kind)

    def held(rows, cols, kind=BF):
        return pltpu.VMEM((rows, cols), kind)

    product = 2 * ROWS * f.shape[1] * 3 * HD
    attention = 2 * GROUP * 9 * BLK * BLK * 2 * HD
    w_mine, fy, total = call(
        begin_kernel,
        "begin",
        [held(w.shape[1], 3 * HD), held(ROWS, f.shape[1]), held(ROWS, 3 * HD, F32)],
        (place, sy, f, w),
        4,
        product,
        [pltpu.SemaphoreType.DMA((4,))],
    )
    (pack,) = call(pack_kernel, "pack", [out(4 * HALF, f.shape[1])], (sd, sx, fy), 4, 0)
    other = across(pack, 0, 1)
    (total,) = call(
        project_across_kernel, "project_across", [held(ROWS, 3 * HD, F32)], (place, pack, total, w_mine), 4, product
    )
    (kv,) = call(project_kv_kernel, "project_kv", [out(ROWS, 2 * HD)], (place, other, total, w_mine), 4, product)

    near_a = group_swap(kv, 0)
    near_b = group_swap(kv, 1)
    (q,) = call(project_q_kernel, "project_q", [held(ROWS, HD)], (place, other, total, w_mine), 4, product)
    far_b = group_swap(lax.dynamic_slice_in_dim(near_a, odd * HALF, HALF, axis=0), 1)
    far_a = group_swap(lax.dynamic_slice_in_dim(near_b, (1 - odd) * HALF, HALF, axis=0), 0)

    link_rows = jnp.zeros((16, HD), BF).at[: block_links.shape[0], : block_links.shape[1]].set(
        block_links.astype(BF)
    )
    d_payload = jnp.concatenate(
        [lax.dynamic_slice_in_dim(d_out, (1 - side) * HD, HD, axis=1), link_rows], axis=0
    )
    d_other = across(d_payload, 1, 0)
    other_links = d_other[HALF : HALF + block_links.shape[0], : block_links.shape[1]].astype(jnp.int32)
    links = jnp.where(
        side == 0,
        jnp.concatenate([block_links, other_links], axis=0),
        jnp.concatenate([other_links, block_links], axis=0),
    )

    mixed, pairs, win, acc, far_a_grad, far_b_grad = call(
        attend_kernel,
        "attend",
        [
            held(GROUP * 9 * BLK, 2 * HD),
            held(GROUP * 2 * BLK, 2 * HD),
            held(WINDOW * BLK, 2 * HD),
            held(WINDOW * BLK, 2 * HD, F32),
            out(HALF, 2 * HD),
            out(HALF, 2 * HD),
        ],
        (place, links, q, kv, near_a, near_b, far_a, far_b, d_out, d_other[:HALF]),
        16,
        2 * attention,
    )
    own, near_a_grad, near_b_grad = call(
        near_grads_kernel,
        "near_grads",
        [held(ROWS, 2 * HD, F32), out(ROWS, 2 * HD), out(ROWS, 2 * HD)],
        (place, links, mixed, pairs, acc),
        8,
        attention,
        [pltpu.VMEM((WINDOW * BLK, 2 * HD), F32)],
    )
    att_own, att_other, dq = call(
        outputs_kernel,
        "outputs",
        [out(HALF, HD), out(HALF, HD), held(ROWS, HD)],
        (place, links, mixed, win),
        8,
        attention,
        [pltpu.VMEM((ROWS, HD), BF)],
    )

    back_a = group_swap(far_a_grad, 0)
    back_b = group_swap(far_b_grad, 1)

    def add_half(whole, part, start):
        old = lax.dynamic_slice_in_dim(whole, start, HALF, axis=0)
        new = (old.astype(F32) + part.astype(F32)).astype(BF)
        return lax.dynamic_update_slice_in_dim(whole, new, start, axis=0)

    from_b = group_swap(add_half(near_b_grad, back_a, (1 - odd) * HALF), 1)
    from_a = group_swap(add_half(near_a_grad, back_b, odd * HALF), 0)
    att_back = across(att_other, 1, 0)
    from_a, from_b, att_back = lax.optimization_barrier((from_a, from_b, att_back))
    attended = jnp.where(
        side == 0,
        jnp.concatenate([att_own, att_back], axis=1),
        jnp.concatenate([att_back, att_own], axis=1),
    )

    send, grads = call(
        spread_send_kernel,
        "spread_send",
        [out(4 * HALF, 2 * HD), held(ROWS, 3 * HD)],
        (place, own, from_a, from_b, dq, w_mine),
        4,
        product,
    )
    (keep,) = call(spread_keep_kernel, "spread_keep", [held(4 * HALF, 2 * HD)], (place, grads, w_mine), 4, product)
    arrived = across(send, 0, 1)
    chip = (keep.astype(F32) + arrived.astype(F32)).astype(BF)
    gd = across(chip[3 * HALF :], 1, 2)
    gy = across(chip[2 * HALF : 3 * HALF], 1, 0)
    gx = across(chip[HALF : 2 * HALF], 0, 2)
    grad_features = (
        chip[:HALF].astype(F32) + gd.astype(F32) + gy.astype(F32) + gx.astype(F32)
    ).astype(BF)
    return attended, grad_features


def solution(mesh):
    sizes = dict(mesh.shape)
    return jax.shard_map(
        functools.partial(body, n_ctx=sizes["ctx"], n_head=sizes["head"]),
        mesh=mesh,
        in_specs=(P("ctx", "head"), P(None, None, "head"), P("ctx", None), P("ctx", "head")),
        out_specs=(P("ctx", "head"), P("ctx", "head")),
        check_vma=False,
    )
```

```python
import functools

import jax
import jax.numpy as jnp
from jax import lax
from jax.experimental import pallas as pl
from jax.experimental.pallas import tpu as pltpu
from jax.sharding import PartitionSpec as P

HD = 128
BLK = 128
REACH = 6
SPAN = 3
LOG2E = 1.4426950408889634
DEAD = -1e30
BF = jnp.bfloat16
F32 = jnp.float32

GROUP = 4
ROWS = GROUP * BLK
HALF = ROWS // 2
WINDOW = GROUP + 2 * REACH
NEAR_LEFT = (REACH - GROUP) * BLK
OWN = REACH * BLK
NEAR_RIGHT = OWN + ROWS
FAR_RIGHT = NEAR_RIGHT + ROWS


def params(flops, moved, mebibytes):
    return dict(
        compiler_params=pltpu.CompilerParams(vmem_limit_bytes=mebibytes * 1024 * 1024),
        cost_estimate=pl.CostEstimate(flops=flops, bytes_accessed=moved, transcendentals=0),
    )


VMEM = pl.BlockSpec(memory_space=pltpu.VMEM)
SMEM = pl.BlockSpec(memory_space=pltpu.SMEM)


def dot(a, b, dims):
    return lax.dot_general(a, b, (dims, ((), ())), preferred_element_type=F32)


def position():
    ctx = lax.axis_index("ctx")
    group = ctx // 2
    return ctx % 2, group % 2, group * GROUP, lax.axis_index("head")


def begin_kernel(f, w, w_mine, fm, total, sems):
    side, _, _, head = position()
    copies = [pltpu.make_async_copy(f, fm, sems.at[3])]
    for g in range(3):
        cols = pl.ds(pl.multiple_of(side * HD, HD), HD)
        copies.append(pltpu.make_async_copy(w.at[g, :, cols], w_mine.at[:, pl.ds(g * HD, HD)], sems.at[g]))
    for copy in copies:
        copy.start()
    for copy in copies:
        copy.wait()
    total[...] = dot(fm[...], weight_rows(w_mine, head, fm.shape[1]), ((1,), (0,)))


def weight_rows(w_mine, source, width):
    return w_mine[pl.ds(pl.multiple_of(source * width, width), width), :]


def pack_kernel(fm, sy, sx, sd, out):
    for index, piece in enumerate((fm, sy, sx, sd)):
        out[index * HALF : (index + 1) * HALF, :] = piece[...]


def project_across_kernel(pack, before, w_mine, total):
    head = position()[3]
    width = pack.shape[1]
    far = dot(pack[2 * HALF :, :], weight_rows(w_mine, head ^ 2, width), ((1,), (0,)))
    total[:HALF, :] = before[...] + far[:HALF]
    total[HALF:, :] = far[HALF:] + dot(pack[HALF : 2 * HALF, :], weight_rows(w_mine, head, width), ((1,), (0,)))


def sibling_product(head, other, w_mine, cols):
    width = other.shape[1]
    total = None
    for index in range(2):
        rows = pl.ds(pl.multiple_of((head ^ (1 + 2 * index)) * width, width), width)
        term = dot(other[2 * index * HALF : 2 * (index + 1) * HALF, :], w_mine[rows, cols], ((1,), (0,)))
        total = term if total is None else total + term
    return total


def store_groups(side, total, target):
    for group in range(2):
        rows = pl.ds(pl.multiple_of((side ^ group) * HALF, HALF), HALF)
        target[rows, :] = total[group * HALF : (group + 1) * HALF]


def project_kv_kernel(other, before, w_mine, first_out, second_out):
    side, odd, _, head = position()
    total = (before[:, HD:] + sibling_product(head, other, w_mine, slice(HD, 3 * HD))).astype(BF)
    near_first = side ^ (1 - odd) == 0
    first_out[...] = jnp.where(near_first, total[:HALF], total[HALF:])
    second_out[...] = jnp.where(near_first, total[HALF:], total[:HALF])


def merge_kernel(whole, part, out, which):
    at = pl.ds(pl.multiple_of((position()[1] ^ which) * HALF, HALF), HALF)
    out[...] = whole[...]
    out[at, :] = (whole[at, :].astype(F32) + part[...].astype(F32)).astype(BF)


def lay_out_kernel(own, other, out):
    side = position()[0]
    for half in range(2):
        cols = slice(half * HD, (half + 1) * HD)
        out[:, cols] = jnp.where(side == half, own[...], other[...])


def join_kernel(own_half, arrived, out):
    out[:HALF, :] = own_half[...]
    out[HALF:, :] = arrived[...]


def project_q_kernel(other, before, w_mine, to_a, to_b, q_out):
    del to_a, to_b
    side, _, _, head = position()
    total = before[:, :HD] + sibling_product(head, other, w_mine, slice(0, HD))
    store_groups(side, total.astype(BF), q_out)


def payload_kernel(d_own, link_rows, pack, payload):
    del pack
    side = position()[0]
    payload[:HALF, :] = jnp.where(side == 0, d_own[:, HD:], d_own[:, :HD])
    payload[HALF:, :] = link_rows[...]


def links_kernel(own, other, q, links):
    del q
    side, _, first, _ = position()
    for i in range(GROUP):
        for k in range(3 * SPAN):
            links[i, k] = jnp.where(side == i // 2, own[i % 2, k], other[i % 2, k])
        for t in (1, 2):
            base = jnp.int32(-(1 << 20))
            for j in range(SPAN):
                entry = links[i, SPAN * t + j]
                base = jnp.maximum(base, jnp.where(entry >= 0, entry - j, -(1 << 20)))
            base = jnp.where(base > -(1 << 19), base - first + REACH, REACH + i)
            links[GROUP, 2 * i + t - 1] = jnp.clip(base, 0, WINDOW - SPAN) * BLK


def regions(odd):
    even = 1 - odd
    left_lo, left_hi = NEAR_LEFT, NEAR_LEFT + HALF
    right_lo, right_hi = NEAR_RIGHT, NEAR_RIGHT + HALF
    pick = lambda at_even, at_odd: pl.multiple_of(even * at_even + odd * at_odd, HALF)
    return (
        pick(OWN + HALF, OWN),
        pick(OWN, OWN + HALF),
        pick(right_lo, left_hi),
        pick(left_hi, right_lo),
        pick(right_hi, left_lo),
        pick(FAR_RIGHT, 0),
        pick(left_lo, right_hi),
        pick(0, FAR_RIGHT),
    )


def near_regions(odd):
    even = 1 - odd
    pick = lambda at_even, at_odd: pl.multiple_of(even * at_even + odd * at_odd, HALF)
    return pick(NEAR_RIGHT, NEAR_LEFT), pick(NEAR_LEFT, NEAR_RIGHT)


def start_of(links, i, t):
    if t == 0:
        return (REACH + i - 1) * BLK
    return pl.multiple_of(links[GROUP, 2 * i + t - 1], BLK)


def is_far(i, t):
    return t == (1 if i < GROUP // 2 else 2)


def run_rows(i, t):
    return slice((i * 3 + t) * SPAN * BLK, (i * 3 + t + 1) * SPAN * BLK)


def side_factor():
    scale = HD ** -0.5
    return jnp.where(lax.broadcasted_iota(jnp.int32, (1, 2 * HD), 1) < HD, scale, 1.0).astype(F32)


def attend_kernel(
    links, q, first_kv, second_kv, a1, b1, a2, b2, d_own, d_other,
    mixed, pairs, win, near_acc, far_a_out, far_b_out, acc,
):
    side, odd, _, _ = position()
    scale = HD ** -0.5
    places = regions(odd)
    halves = (
        first_kv[...], second_kv[...], a1[...], b1[...], a2[:HALF, :], a2[HALF:, :], b2[:HALF, :], b2[HALF:, :],
    )
    for at, half in zip(places, halves):
        win[pl.ds(at, HALF), :] = half
    at_far_a, at_far_b = places[5], places[7]
    acc[...] = jnp.zeros_like(acc)
    zeros = jnp.zeros((BLK, HD), BF)
    own_cols = pl.ds(pl.multiple_of(side * HD, HD), HD)
    for i in range(GROUP):
        rows = slice(i * BLK, (i + 1) * BLK)
        here = slice((i % 2) * BLK, (i % 2 + 1) * BLK)
        d_blk = jnp.where(side == i // 2, d_own[here, own_cols], d_other[here, :])
        pair = jnp.concatenate(
            [
                jnp.concatenate([q[rows, :], zeros], axis=1),
                jnp.concatenate([zeros, d_blk], axis=1),
            ],
            axis=0,
        )
        pairs[2 * i * BLK : 2 * (i + 1) * BLK, :] = pair
        scores, prob_grads, peaks, biases = [], [], [], []
        for t in range(3):
            product = dot(win[pl.ds(start_of(links, i, t), SPAN * BLK), :], pair, ((1,), (1,)))
            for j in range(SPAN):
                block = product[j * BLK : (j + 1) * BLK]
                bias = jnp.where(links[i, SPAN * t + j] >= 0, 0.0, DEAD).astype(F32)
                scores.append(block[:, :BLK])
                prob_grads.append(block[:, BLK:])
                biases.append(bias)
                peaks.append(jnp.max(block[:, :BLK].reshape(BLK // 8, 8, BLK), axis=0) + bias)
        largest = peaks[0]
        for peak in peaks[1:]:
            largest = jnp.maximum(largest, peak)
        largest = jnp.max(largest, axis=0, keepdims=True)
        terms = []
        total = jnp.zeros((8, BLK), F32)
        weighted = jnp.zeros((8, BLK), F32)
        for n in range(3 * SPAN):
            term = jnp.exp2((scores[n] - (largest - biases[n])) * (scale * LOG2E))
            terms.append(term)
            total = total + jnp.sum(term.reshape(BLK // 8, 8, BLK), axis=0)
            weighted = weighted + jnp.sum((term * prob_grads[n]).reshape(BLK // 8, 8, BLK), axis=0)
        inverse = 1.0 / jnp.sum(total, axis=0, keepdims=True)
        row_dot = jnp.sum(weighted, axis=0, keepdims=True) * inverse
        for t in range(3):
            parts = []
            for n in range(SPAN * t, SPAN * t + SPAN):
                share = terms[n] * inverse
                grad = share * (prob_grads[n] - row_dot)
                parts.append(jnp.concatenate([grad.astype(BF), share.astype(BF)], axis=1))
            part = jnp.concatenate(parts, axis=0)
            mixed[run_rows(i, t), :] = part
            if is_far(i, t):
                acc[pl.ds(start_of(links, i, t), SPAN * BLK), :] += dot(part, pair, ((1,), (0,)))
    factor = side_factor()
    far_a_out[...] = (acc[pl.ds(at_far_a, HALF), :] * factor).astype(BF)
    far_b_out[...] = (acc[pl.ds(at_far_b, HALF), :] * factor).astype(BF)
    near_acc[:ROWS, :] = acc[NEAR_LEFT:OWN, :]
    near_acc[ROWS:, :] = acc[NEAR_RIGHT:FAR_RIGHT, :]


def near_grads_kernel(links, mixed, pairs, near_acc, own_out, a_out, b_out, acc):
    odd = position()[1]
    acc[NEAR_LEFT:OWN, :] = near_acc[:ROWS, :]
    acc[OWN:NEAR_RIGHT, :] = jnp.zeros((ROWS, 2 * HD), F32)
    acc[NEAR_RIGHT:FAR_RIGHT, :] = near_acc[ROWS:, :]
    for i in range(GROUP):
        pair = pairs[2 * i * BLK : 2 * (i + 1) * BLK, :]
        for t in range(3):
            if not is_far(i, t):
                at = pl.ds(start_of(links, i, t), SPAN * BLK)
                acc[at, :] += dot(mixed[run_rows(i, t), :], pair, ((1,), (0,)))
    factor = side_factor()
    at_a, at_b = near_regions(odd)
    own_out[...] = acc[OWN : OWN + ROWS, :] * factor
    a_out[...] = (acc[pl.ds(at_a, ROWS), :] * factor).astype(BF)
    b_out[...] = (acc[pl.ds(at_b, ROWS), :] * factor).astype(BF)


def outputs_kernel(links, mixed, win, att_own, att_other, dq_out, att):
    side = position()[0]
    for i in range(GROUP):
        rows = slice(i * BLK, (i + 1) * BLK)
        out = None
        for t in range(3):
            keys = win[pl.ds(start_of(links, i, t), SPAN * BLK), :]
            term = dot(mixed[run_rows(i, t), :], keys, ((0,), (0,)))
            out = term if out is None else out + term
        att[rows, :] = out[BLK:, HD:].astype(BF)
        dq_out[rows, :] = (out[:BLK, :HD] * (HD ** -0.5)).astype(BF)
    att_own[...] = att[pl.ds(pl.multiple_of(side * HALF, HALF), HALF), :]
    att_other[...] = att[pl.ds(pl.multiple_of((1 - side) * HALF, HALF), HALF), :]


def spread(grads, w_mine, side, head, target):
    for step in range(2):
        out = dot(grads, weight_rows(w_mine, head ^ (2 * step), 2 * HD), ((1,), (1,))).astype(BF)
        for group in range(2):
            index = 2 * group + step
            part = jnp.where(side == group, out[:HALF], out[HALF:])
            target[index * HALF : (index + 1) * HALF, :] = part


def spread_send_kernel(own, from_a, from_b, dq, w_mine, send, grads):
    dkv = (own[...] + from_a[...].astype(F32) + from_b[...].astype(F32)).astype(BF)
    grads[:, :HD] = dq[...]
    grads[:, HD:] = dkv
    side, _, _, head = position()
    spread(grads[...], w_mine, side, head ^ 1, send)


def spread_keep_kernel(grads, w_mine, keep):
    side, _, _, head = position()
    spread(grads[...], w_mine, side, head, keep)


def body(features, w_qkv, block_links, d_out, n_ctx, n_head):
    n_group = n_ctx // 2

    def across(value, flip_ctx, flip_head):
        pairs = [
            (c * n_head + h, (c ^ flip_ctx) * n_head + (h ^ flip_head))
            for c in range(n_ctx)
            for h in range(n_head)
        ]
        return lax.ppermute(value, ("ctx", "head"), pairs)

    def group_swap(value, offset):
        pairs = []
        for low in range(offset, n_group - 1, 2):
            for s in range(2):
                pairs.append((2 * low + s, 2 * low + 2 + s))
                pairs.append((2 * low + 2 + s, 2 * low + s))
        return lax.ppermute(value, "ctx", pairs)

    f = features
    sx = across(f, 0, 2)
    sy = across(f, 1, 0)
    sd = across(f, 1, 2)
    w = jnp.transpose(w_qkv, (1, 0, 2))

    def call(kernel, name, outs, ins, mebibytes, flops, scratch=()):
        specs = [SMEM if v.dtype == jnp.int32 else VMEM for v in ins]
        if kernel is begin_kernel:
            specs = [pl.BlockSpec(memory_space=pltpu.HBM)] * 2
            ins = [pltpu.with_memory_space_constraint(v, pltpu.HBM) for v in ins]
        return pl.pallas_call(
            kernel,
            name=name,
            out_shape=outs,
            in_specs=specs,
            out_specs=[SMEM if v.dtype == jnp.int32 else VMEM for v in outs],
            scratch_shapes=list(scratch),
            **params(flops, 2 << 20, mebibytes),
        )(*ins)

    def out(rows, cols, kind=BF):
        return jax.ShapeDtypeStruct((rows, cols), kind)

    def held(rows, cols, kind=BF):
        return pltpu.VMEM((rows, cols), kind)

    product = 2 * ROWS * f.shape[1] * 3 * HD
    attention = 2 * GROUP * 9 * BLK * BLK * 2 * HD
    w_mine, fm, total = call(
        begin_kernel,
        "begin",
        [held(w.shape[1], 3 * HD), held(*f.shape), held(HALF, 3 * HD, F32)],
        (f, w),
        4,
        product,
        [pltpu.SemaphoreType.DMA((4,))],
    )
    (pack,) = call(pack_kernel, "pack", [out(4 * HALF, f.shape[1])], (fm, sy, sx, sd), 4, 0)
    other = across(pack, 0, 1)
    (total,) = call(
        project_across_kernel, "project_across", [held(ROWS, 3 * HD, F32)], (pack, total, w_mine), 4, product
    )
    first, second = call(
        project_kv_kernel, "project_kv", [out(HALF, 2 * HD)] * 2, (other, total, w_mine), 4, product
    )

    a1 = group_swap(first, 0)
    b1 = group_swap(second, 1)
    (to_b,) = call(join_kernel, "join_b", [out(ROWS, 2 * HD)], (first, a1), 4, 0)
    (to_a,) = call(join_kernel, "join_a", [out(ROWS, 2 * HD)], (second, b1), 4, 0)
    b2 = group_swap(to_b, 1)
    a2 = group_swap(to_a, 0)
    rows, slots = block_links.shape
    link_rows = jnp.pad(block_links.astype(BF), ((0, 16 - rows), (0, HD - slots)))
    (payload,) = call(payload_kernel, "payload", [out(HALF + 16, HD)], (d_out, link_rows, pack), 4, 0)
    d_other = across(payload, 1, 0)
    (q,) = call(project_q_kernel, "project_q", [held(ROWS, HD)], (other, total, w_mine, to_a, to_b), 4, product)
    other_links = d_other[HALF : HALF + rows, :slots].astype(jnp.int32)
    (links,) = call(
        links_kernel, "links", [pltpu.SMEM((GROUP + 1, slots), jnp.int32)], (block_links, other_links, q), 4, 0
    )
    links = pltpu.with_memory_space_constraint(links, pltpu.SMEM)
    mixed, pairs, win, near_acc, far_a_grad, far_b_grad = call(
        attend_kernel,
        "attend",
        [
            held(GROUP * 9 * BLK, 2 * HD),
            held(GROUP * 2 * BLK, 2 * HD),
            held(WINDOW * BLK, 2 * HD),
            held(2 * ROWS, 2 * HD, F32),
            out(HALF, 2 * HD),
            out(HALF, 2 * HD),
        ],
        (links, q, first, second, a1, b1, a2, b2, d_out, d_other),
        8,
        2 * attention,
        [pltpu.VMEM((WINDOW * BLK, 2 * HD), F32)],
    )
    own, near_a_grad, near_b_grad = call(
        near_grads_kernel,
        "near_grads",
        [held(ROWS, 2 * HD, F32), out(ROWS, 2 * HD), out(ROWS, 2 * HD)],
        (links, mixed, pairs, near_acc),
        4,
        attention,
        [pltpu.VMEM((WINDOW * BLK, 2 * HD), F32)],
    )
    att_own, att_other, dq = call(
        outputs_kernel,
        "outputs",
        [out(HALF, HD), out(HALF, HD), held(ROWS, HD)],
        (links, mixed, win),
        4,
        attention,
        [pltpu.VMEM((ROWS, HD), BF)],
    )

    back_a = group_swap(far_a_grad, 0)
    back_b = group_swap(far_b_grad, 1)

    def merge(whole, part, which, name):
        kernel = functools.partial(merge_kernel, which=which)
        return call(kernel, name, [out(ROWS, 2 * HD)], (whole, part), 4, 0)[0]

    from_b = group_swap(merge(near_b_grad, back_a, 1, "merge_b"), 1)
    from_a = group_swap(merge(near_a_grad, back_b, 0, "merge_a"), 0)
    att_back = across(att_other, 1, 0)
    from_a, from_b, att_back = lax.optimization_barrier((from_a, from_b, att_back))
    (attended,) = call(lay_out_kernel, "lay_out", [out(HALF, 2 * HD)], (att_own, att_back), 4, 0)
    send, grads = call(
        spread_send_kernel,
        "spread_send",
        [out(4 * HALF, 2 * HD), held(ROWS, 3 * HD)],
        (own, from_a, from_b, dq, w_mine),
        4,
        product,
    )
    (keep,) = call(spread_keep_kernel, "spread_keep", [held(4 * HALF, 2 * HD)], (grads, w_mine), 4, product)
    arrived = across(send, 0, 1)
    chip = (keep.astype(F32) + arrived.astype(F32)).astype(BF)
    gd = across(chip[3 * HALF :], 1, 2)
    gy = across(chip[2 * HALF : 3 * HALF], 1, 0)
    gx = across(chip[HALF : 2 * HALF], 0, 2)
    grad_features = (
        chip[:HALF].astype(F32) + gd.astype(F32) + gy.astype(F32) + gx.astype(F32)
    ).astype(BF)
    return attended, grad_features


def solution(mesh):
    sizes = dict(mesh.shape)
    return jax.shard_map(
        functools.partial(body, n_ctx=sizes["ctx"], n_head=sizes["head"]),
        mesh=mesh,
        in_specs=(P("ctx", "head"), P(None, None, "head"), P("ctx", None), P("ctx", "head")),
        out_specs=(P("ctx", "head"), P("ctx", "head")),
        check_vma=False,
    )
```

```python
import functools

import jax
import jax.numpy as jnp
from jax import lax
from jax.experimental import pallas as pl
from jax.experimental.pallas import tpu as pltpu
from jax.sharding import PartitionSpec as P

HD = 128
BLK = 128
REACH = 6
SPAN = 3
LOG2E = 1.4426950408889634
DEAD = -1e30
BF = jnp.bfloat16
F32 = jnp.float32

GROUP = 4
ROWS = GROUP * BLK
HALF = ROWS // 2
WINDOW = GROUP + 2 * REACH
NEAR_LEFT = (REACH - GROUP) * BLK
OWN = REACH * BLK
NEAR_RIGHT = OWN + ROWS
FAR_RIGHT = NEAR_RIGHT + ROWS


def params(flops, moved, mebibytes):
    return dict(
        compiler_params=pltpu.CompilerParams(vmem_limit_bytes=mebibytes * 1024 * 1024),
        cost_estimate=pl.CostEstimate(flops=flops, bytes_accessed=moved, transcendentals=0),
    )


VMEM = pl.BlockSpec(memory_space=pltpu.VMEM)
SMEM = pl.BlockSpec(memory_space=pltpu.SMEM)


def dot(a, b, dims):
    return lax.dot_general(a, b, (dims, ((), ())), preferred_element_type=F32)


def position():
    ctx = lax.axis_index("ctx")
    group = ctx // 2
    return ctx % 2, group % 2, group * GROUP, lax.axis_index("head")


def begin_kernel(f, w, w_mine, fm, total, sems):
    side, _, _, head = position()
    copies = [pltpu.make_async_copy(f, fm, sems.at[3])]
    for g in range(3):
        cols = pl.ds(pl.multiple_of(side * HD, HD), HD)
        copies.append(pltpu.make_async_copy(w.at[g, :, cols], w_mine.at[:, pl.ds(g * HD, HD)], sems.at[g]))
    for copy in copies:
        copy.start()
    for copy in copies:
        copy.wait()
    total[...] = dot(fm[...], weight_rows(w_mine, head, fm.shape[1]), ((1,), (0,)))


def weight_rows(w_mine, source, width):
    return w_mine[pl.ds(pl.multiple_of(source * width, width), width), :]


def pack_kernel(fm, sy, sx, sd, out):
    for index, piece in enumerate((fm, sy, sx, sd)):
        out[index * HALF : (index + 1) * HALF, :] = piece[...]


def project_across_kernel(pack, before, w_mine, total):
    head = position()[3]
    width = pack.shape[1]
    far = dot(pack[2 * HALF :, :], weight_rows(w_mine, head ^ 2, width), ((1,), (0,)))
    total[:HALF, :] = before[...] + far[:HALF]
    total[HALF:, :] = far[HALF:] + dot(pack[HALF : 2 * HALF, :], weight_rows(w_mine, head, width), ((1,), (0,)))


def sibling_product(head, other, w_mine, cols):
    width = other.shape[1]
    total = None
    for index in range(2):
        rows = pl.ds(pl.multiple_of((head ^ (1 + 2 * index)) * width, width), width)
        term = dot(other[2 * index * HALF : 2 * (index + 1) * HALF, :], w_mine[rows, cols], ((1,), (0,)))
        total = term if total is None else total + term
    return total


def store_groups(side, total, target):
    for group in range(2):
        rows = pl.ds(pl.multiple_of((side ^ group) * HALF, HALF), HALF)
        target[rows, :] = total[group * HALF : (group + 1) * HALF]


def project_kv_kernel(other, before, w_mine, first_out, second_out):
    side, odd, _, head = position()
    total = (before[:, HD:] + sibling_product(head, other, w_mine, slice(HD, 3 * HD))).astype(BF)
    near_first = side ^ (1 - odd) == 0
    first_out[...] = jnp.where(near_first, total[:HALF], total[HALF:])
    second_out[...] = jnp.where(near_first, total[HALF:], total[:HALF])


def merge_kernel(whole, part, out, which):
    at = pl.ds(pl.multiple_of((position()[1] ^ which) * HALF, HALF), HALF)
    out[...] = whole[...]
    out[at, :] = (whole[at, :].astype(F32) + part[...].astype(F32)).astype(BF)


def lay_out_kernel(own, other, out):
    side = position()[0]
    for half in range(2):
        cols = slice(half * HD, (half + 1) * HD)
        out[:, cols] = jnp.where(side == half, own[...], other[...])


def join_kernel(own_half, arrived, out):
    out[:HALF, :] = own_half[...]
    out[HALF:, :] = arrived[...]


def project_q_kernel(other, before, w_mine, to_a, to_b, q_out):
    del to_a, to_b
    side, _, _, head = position()
    total = before[:, :HD] + sibling_product(head, other, w_mine, slice(0, HD))
    store_groups(side, total.astype(BF), q_out)


def payload_kernel(d_own, link_rows, pack, payload):
    del pack
    side = position()[0]
    payload[:HALF, :] = jnp.where(side == 0, d_own[:, HD:], d_own[:, :HD])
    payload[HALF:, :] = link_rows[...]


def links_kernel(own, other, q, links):
    del q
    side, _, first, _ = position()
    for i in range(GROUP):
        for k in range(3 * SPAN):
            links[i, k] = jnp.where(side == i // 2, own[i % 2, k], other[i % 2, k])
        for t in (1, 2):
            base = jnp.int32(-(1 << 20))
            for j in range(SPAN):
                entry = links[i, SPAN * t + j]
                base = jnp.maximum(base, jnp.where(entry >= 0, entry - j, -(1 << 20)))
            base = jnp.where(base > -(1 << 19), base - first + REACH, REACH + i)
            links[GROUP, 2 * i + t - 1] = jnp.clip(base, 0, WINDOW - SPAN) * BLK


def regions(odd):
    even = 1 - odd
    left_lo, left_hi = NEAR_LEFT, NEAR_LEFT + HALF
    right_lo, right_hi = NEAR_RIGHT, NEAR_RIGHT + HALF
    pick = lambda at_even, at_odd: pl.multiple_of(even * at_even + odd * at_odd, HALF)
    return (
        pick(OWN + HALF, OWN),
        pick(OWN, OWN + HALF),
        pick(right_lo, left_hi),
        pick(left_hi, right_lo),
        pick(right_hi, left_lo),
        pick(FAR_RIGHT, 0),
        pick(left_lo, right_hi),
        pick(0, FAR_RIGHT),
    )


def near_regions(odd):
    even = 1 - odd
    pick = lambda at_even, at_odd: pl.multiple_of(even * at_even + odd * at_odd, HALF)
    return pick(NEAR_RIGHT, NEAR_LEFT), pick(NEAR_LEFT, NEAR_RIGHT)


def start_of(links, i, t):
    if t == 0:
        return (REACH + i - 1) * BLK
    return pl.multiple_of(links[GROUP, 2 * i + t - 1], BLK)


def is_far(i, t):
    return t == (1 if i < GROUP // 2 else 2)


def run_rows(i, t):
    return slice((i * 3 + t) * SPAN * BLK, (i * 3 + t + 1) * SPAN * BLK)


def side_factor():
    scale = HD ** -0.5
    return jnp.where(lax.broadcasted_iota(jnp.int32, (1, 2 * HD), 1) < HD, scale, 1.0).astype(F32)


def attend_kernel(
    links, q, first_kv, second_kv, a1, b1, a2, b2, d_own, d_other,
    mixed, pairs, win, near_acc, far_a_out, far_b_out, acc,
):
    side, odd, _, _ = position()
    scale = HD ** -0.5
    places = regions(odd)
    halves = (
        first_kv[...], second_kv[...], a1[...], b1[...], a2[:HALF, :], a2[HALF:, :], b2[:HALF, :], b2[HALF:, :],
    )
    for at, half in zip(places, halves):
        win[pl.ds(at, HALF), :] = half
    at_far_a, at_far_b = places[5], places[7]
    acc[...] = jnp.zeros_like(acc)
    zeros = jnp.zeros((BLK, HD), BF)
    own_cols = pl.ds(pl.multiple_of(side * HD, HD), HD)
    for i in range(GROUP):
        rows = slice(i * BLK, (i + 1) * BLK)
        here = slice((i % 2) * BLK, (i % 2 + 1) * BLK)
        d_blk = jnp.where(side == i // 2, d_own[here, own_cols], d_other[here, :])
        pair = jnp.concatenate(
            [
                jnp.concatenate([q[rows, :], zeros], axis=1),
                jnp.concatenate([zeros, d_blk], axis=1),
            ],
            axis=0,
        )
        pairs[2 * i * BLK : 2 * (i + 1) * BLK, :] = pair
        scores, prob_grads, peaks, biases = [], [], [], []
        for t in range(3):
            product = dot(win[pl.ds(start_of(links, i, t), SPAN * BLK), :], pair, ((1,), (1,)))
            for j in range(SPAN):
                block = product[j * BLK : (j + 1) * BLK]
                bias = jnp.where(links[i, SPAN * t + j] >= 0, 0.0, DEAD).astype(F32)
                scores.append(block[:, :BLK])
                prob_grads.append(block[:, BLK:])
                biases.append(bias)
                peaks.append(jnp.max(block[:, :BLK].reshape(BLK // 8, 8, BLK), axis=0) + bias)
        largest = peaks[0]
        for peak in peaks[1:]:
            largest = jnp.maximum(largest, peak)
        largest = jnp.max(largest, axis=0, keepdims=True)
        terms = []
        total = jnp.zeros((8, BLK), F32)
        weighted = jnp.zeros((8, BLK), F32)
        for n in range(3 * SPAN):
            term = jnp.exp2((scores[n] - (largest - biases[n])) * (scale * LOG2E))
            terms.append(term)
            total = total + jnp.sum(term.reshape(BLK // 8, 8, BLK), axis=0)
            weighted = weighted + jnp.sum((term * prob_grads[n]).reshape(BLK // 8, 8, BLK), axis=0)
        inverse = 1.0 / jnp.sum(total, axis=0, keepdims=True)
        row_dot = jnp.sum(weighted, axis=0, keepdims=True) * inverse
        for t in range(3):
            parts = []
            for n in range(SPAN * t, SPAN * t + SPAN):
                share = terms[n] * inverse
                grad = share * (prob_grads[n] - row_dot)
                parts.append(jnp.concatenate([grad.astype(BF), share.astype(BF)], axis=1))
            part = jnp.concatenate(parts, axis=0)
            mixed[run_rows(i, t), :] = part
            if is_far(i, t):
                acc[pl.ds(start_of(links, i, t), SPAN * BLK), :] += dot(part, pair, ((1,), (0,)))
    factor = side_factor()
    far_a_out[...] = (acc[pl.ds(at_far_a, HALF), :] * factor).astype(BF)
    far_b_out[...] = (acc[pl.ds(at_far_b, HALF), :] * factor).astype(BF)
    near_acc[:ROWS, :] = acc[NEAR_LEFT:OWN, :]
    near_acc[ROWS:, :] = acc[NEAR_RIGHT:FAR_RIGHT, :]


def near_grads_kernel(links, mixed, pairs, near_acc, own_out, a_out, b_out, acc):
    odd = position()[1]
    acc[NEAR_LEFT:OWN, :] = near_acc[:ROWS, :]
    acc[OWN:NEAR_RIGHT, :] = jnp.zeros((ROWS, 2 * HD), F32)
    acc[NEAR_RIGHT:FAR_RIGHT, :] = near_acc[ROWS:, :]
    for i in range(GROUP):
        pair = pairs[2 * i * BLK : 2 * (i + 1) * BLK, :]
        for t in range(3):
            if not is_far(i, t):
                at = pl.ds(start_of(links, i, t), SPAN * BLK)
                acc[at, :] += dot(mixed[run_rows(i, t), :], pair, ((1,), (0,)))
    factor = side_factor()
    at_a, at_b = near_regions(odd)
    own_out[...] = acc[OWN : OWN + ROWS, :] * factor
    a_out[...] = (acc[pl.ds(at_a, ROWS), :] * factor).astype(BF)
    b_out[...] = (acc[pl.ds(at_b, ROWS), :] * factor).astype(BF)


def outputs_kernel(links, mixed, win, att_own, att_other, dq_out, att):
    side = position()[0]
    for i in range(GROUP):
        rows = slice(i * BLK, (i + 1) * BLK)
        out = None
        for t in range(3):
            keys = win[pl.ds(start_of(links, i, t), SPAN * BLK), :]
            term = dot(mixed[run_rows(i, t), :], keys, ((0,), (0,)))
            out = term if out is None else out + term
        att[rows, :] = out[BLK:, HD:].astype(BF)
        dq_out[rows, :] = (out[:BLK, :HD] * (HD ** -0.5)).astype(BF)
    att_own[...] = att[pl.ds(pl.multiple_of(side * HALF, HALF), HALF), :]
    att_other[...] = att[pl.ds(pl.multiple_of((1 - side) * HALF, HALF), HALF), :]


def spread(grads, w_mine, side, head, target):
    for step in range(2):
        out = dot(grads, weight_rows(w_mine, head ^ (2 * step), 2 * HD), ((1,), (1,))).astype(BF)
        for group in range(2):
            index = 2 * group + step
            part = jnp.where(side == group, out[:HALF], out[HALF:])
            target[index * HALF : (index + 1) * HALF, :] = part


def spread_send_kernel(own, from_a, from_b, dq, w_mine, send, grads):
    dkv = (own[...] + from_a[...].astype(F32) + from_b[...].astype(F32)).astype(BF)
    grads[:, :HD] = dq[...]
    grads[:, HD:] = dkv
    side, _, _, head = position()
    spread(grads[...], w_mine, side, head ^ 1, send)


def spread_keep_kernel(grads, w_mine, keep):
    side, _, _, head = position()
    spread(grads[...], w_mine, side, head, keep)


def body(features, w_qkv, block_links, d_out, n_ctx, n_head):
    n_group = n_ctx // 2

    def across(value, flip_ctx, flip_head):
        pairs = [
            (c * n_head + h, (c ^ flip_ctx) * n_head + (h ^ flip_head))
            for c in range(n_ctx)
            for h in range(n_head)
        ]
        return lax.ppermute(value, ("ctx", "head"), pairs)

    def group_swap(value, offset):
        partner = list(range(n_group))
        for low in range(offset, n_group - 1, 2):
            partner[low], partner[low + 1] = low + 1, low
        pairs = []
        for ctx in range(n_ctx):
            group, side = divmod(ctx, 2)
            for h in range(n_head):
                alone = 1 if partner[group] == group else 0
                pairs.append((ctx * n_head + h, (2 * partner[group] + side) * n_head + (h ^ alone)))
        return lax.ppermute(value, ("ctx", "head"), pairs)

    f = features
    sx = across(f, 0, 2)
    sy = across(f, 1, 0)
    sd = across(f, 1, 2)
    w = jnp.transpose(w_qkv, (1, 0, 2))

    def call(kernel, name, outs, ins, mebibytes, flops, scratch=()):
        specs = [SMEM if v.dtype == jnp.int32 else VMEM for v in ins]
        if kernel is begin_kernel:
            specs = [pl.BlockSpec(memory_space=pltpu.HBM)] * 2
            ins = [pltpu.with_memory_space_constraint(v, pltpu.HBM) for v in ins]
        return pl.pallas_call(
            kernel,
            name=name,
            out_shape=outs,
            in_specs=specs,
            out_specs=[SMEM if v.dtype == jnp.int32 else VMEM for v in outs],
            scratch_shapes=list(scratch),
            **params(flops, 2 << 20, mebibytes),
        )(*ins)

    def out(rows, cols, kind=BF):
        return jax.ShapeDtypeStruct((rows, cols), kind)

    def held(rows, cols, kind=BF):
        return pltpu.VMEM((rows, cols), kind)

    product = 2 * ROWS * f.shape[1] * 3 * HD
    attention = 2 * GROUP * 9 * BLK * BLK * 2 * HD
    w_mine, fm, total = call(
        begin_kernel,
        "begin",
        [held(w.shape[1], 3 * HD), held(*f.shape), held(HALF, 3 * HD, F32)],
        (f, w),
        4,
        product,
        [pltpu.SemaphoreType.DMA((4,))],
    )
    (pack,) = call(pack_kernel, "pack", [out(4 * HALF, f.shape[1])], (fm, sy, sx, sd), 4, 0)
    other = across(pack, 0, 1)
    (total,) = call(
        project_across_kernel, "project_across", [held(ROWS, 3 * HD, F32)], (pack, total, w_mine), 4, product
    )
    first, second = call(
        project_kv_kernel, "project_kv", [out(HALF, 2 * HD)] * 2, (other, total, w_mine), 4, product
    )

    a1 = group_swap(first, 0)
    b1 = group_swap(second, 1)
    (to_b,) = call(join_kernel, "join_b", [out(ROWS, 2 * HD)], (first, a1), 4, 0)
    (to_a,) = call(join_kernel, "join_a", [out(ROWS, 2 * HD)], (second, b1), 4, 0)
    b2 = group_swap(to_b, 1)
    a2 = group_swap(to_a, 0)
    rows, slots = block_links.shape
    link_rows = jnp.pad(block_links.astype(BF), ((0, 16 - rows), (0, HD - slots)))
    (payload,) = call(payload_kernel, "payload", [out(HALF + 16, HD)], (d_out, link_rows, pack), 4, 0)
    d_other = across(payload, 1, 0)
    (q,) = call(project_q_kernel, "project_q", [held(ROWS, HD)], (other, total, w_mine, to_a, to_b), 4, product)
    other_links = d_other[HALF : HALF + rows, :slots].astype(jnp.int32)
    (links,) = call(
        links_kernel, "links", [pltpu.SMEM((GROUP + 1, slots), jnp.int32)], (block_links, other_links, q), 4, 0
    )
    links = pltpu.with_memory_space_constraint(links, pltpu.SMEM)
    mixed, pairs, win, near_acc, far_a_grad, far_b_grad = call(
        attend_kernel,
        "attend",
        [
            held(GROUP * 9 * BLK, 2 * HD),
            held(GROUP * 2 * BLK, 2 * HD),
            held(WINDOW * BLK, 2 * HD),
            held(2 * ROWS, 2 * HD, F32),
            out(HALF, 2 * HD),
            out(HALF, 2 * HD),
        ],
        (links, q, first, second, a1, b1, a2, b2, d_out, d_other),
        8,
        2 * attention,
        [pltpu.VMEM((WINDOW * BLK, 2 * HD), F32)],
    )
    own, near_a_grad, near_b_grad = call(
        near_grads_kernel,
        "near_grads",
        [held(ROWS, 2 * HD, F32), out(ROWS, 2 * HD), out(ROWS, 2 * HD)],
        (links, mixed, pairs, near_acc),
        4,
        attention,
        [pltpu.VMEM((WINDOW * BLK, 2 * HD), F32)],
    )
    att_own, att_other, dq = call(
        outputs_kernel,
        "outputs",
        [out(HALF, HD), out(HALF, HD), held(ROWS, HD)],
        (links, mixed, win),
        4,
        attention,
        [pltpu.VMEM((ROWS, HD), BF)],
    )

    back_a = group_swap(far_a_grad, 0)
    back_b = group_swap(far_b_grad, 1)

    def merge(whole, part, which, name):
        kernel = functools.partial(merge_kernel, which=which)
        return call(kernel, name, [out(ROWS, 2 * HD)], (whole, part), 4, 0)[0]

    from_b = group_swap(merge(near_b_grad, back_a, 1, "merge_b"), 1)
    from_a = group_swap(merge(near_a_grad, back_b, 0, "merge_a"), 0)
    att_back = across(att_other, 1, 0)
    from_a, from_b, att_back = lax.optimization_barrier((from_a, from_b, att_back))
    (attended,) = call(lay_out_kernel, "lay_out", [out(HALF, 2 * HD)], (att_own, att_back), 4, 0)
    send, grads = call(
        spread_send_kernel,
        "spread_send",
        [out(4 * HALF, 2 * HD), held(ROWS, 3 * HD)],
        (own, from_a, from_b, dq, w_mine),
        4,
        product,
    )
    (keep,) = call(spread_keep_kernel, "spread_keep", [held(4 * HALF, 2 * HD)], (grads, w_mine), 4, product)
    arrived = across(send, 0, 1)
    chip = (keep.astype(F32) + arrived.astype(F32)).astype(BF)
    gd = across(chip[3 * HALF :], 1, 2)
    gy = across(chip[2 * HALF : 3 * HALF], 1, 0)
    gx = across(chip[HALF : 2 * HALF], 0, 2)
    grad_features = (
        chip[:HALF].astype(F32) + gd.astype(F32) + gy.astype(F32) + gx.astype(F32)
    ).astype(BF)
    return attended, grad_features


def solution(mesh):
    sizes = dict(mesh.shape)
    return jax.shard_map(
        functools.partial(body, n_ctx=sizes["ctx"], n_head=sizes["head"]),
        mesh=mesh,
        in_specs=(P("ctx", "head"), P(None, None, "head"), P("ctx", None), P("ctx", "head")),
        out_specs=(P("ctx", "head"), P("ctx", "head")),
        check_vma=False,
    )
```

```python
import functools

import jax
import jax.numpy as jnp
from jax import lax
from jax.experimental import pallas as pl
from jax.experimental.pallas import tpu as pltpu
from jax.sharding import PartitionSpec as P

HD = 128
BLK = 128
REACH = 6
SPAN = 3
LOG2E = 1.4426950408889634
DEAD = -1e30
BF = jnp.bfloat16
F32 = jnp.float32

GROUP = 4
ROWS = GROUP * BLK
HALF = ROWS // 2
WINDOW = GROUP + 2 * REACH
NEAR_LEFT = (REACH - GROUP) * BLK
OWN = REACH * BLK
NEAR_RIGHT = OWN + ROWS
FAR_RIGHT = NEAR_RIGHT + ROWS


def params(flops, moved, mebibytes):
    return dict(
        compiler_params=pltpu.CompilerParams(vmem_limit_bytes=mebibytes * 1024 * 1024),
        cost_estimate=pl.CostEstimate(flops=flops, bytes_accessed=moved, transcendentals=0),
    )


VMEM = pl.BlockSpec(memory_space=pltpu.VMEM)
SMEM = pl.BlockSpec(memory_space=pltpu.SMEM)


def dot(a, b, dims):
    return lax.dot_general(a, b, (dims, ((), ())), preferred_element_type=F32)


def position():
    ctx, head = lax.axis_index("ctx"), lax.axis_index("head")
    return ctx % 2, head % 2, ctx // 2 * GROUP, head


def begin_kernel(f, w, w_mine, fm, total, sems):
    side, _, _, head = position()
    copies = [pltpu.make_async_copy(f, fm, sems.at[3])]
    for g in range(3):
        cols = pl.ds(pl.multiple_of(side * HD, HD), HD)
        copies.append(pltpu.make_async_copy(w.at[g, :, cols], w_mine.at[:, pl.ds(g * HD, HD)], sems.at[g]))
    for copy in copies:
        copy.start()
    for copy in copies:
        copy.wait()
    total[...] = dot(fm[...], weight_rows(w_mine, head, fm.shape[1]), ((1,), (0,)))


def weight_rows(w_mine, source, width):
    return w_mine[pl.ds(pl.multiple_of(source * width, width), width), :]


def pack_kernel(fm, sy, sx, sd, out):
    for index, piece in enumerate((fm, sy, sx, sd)):
        out[index * HALF : (index + 1) * HALF, :] = piece[...]


def project_across_kernel(pack, before, w_mine, total):
    head = position()[3]
    width = pack.shape[1]
    far = dot(pack[2 * HALF :, :], weight_rows(w_mine, head ^ 2, width), ((1,), (0,)))
    total[:HALF, :] = before[...] + far[:HALF]
    total[HALF:, :] = far[HALF:] + dot(pack[HALF : 2 * HALF, :], weight_rows(w_mine, head, width), ((1,), (0,)))


def sibling_product(head, other, w_mine, cols):
    width = other.shape[1]
    total = None
    for index in range(2):
        rows = pl.ds(pl.multiple_of((head ^ (1 + 2 * index)) * width, width), width)
        term = dot(other[2 * index * HALF : 2 * (index + 1) * HALF, :], w_mine[rows, cols], ((1,), (0,)))
        total = term if total is None else total + term
    return total


def store_groups(side, total, target):
    for group in range(2):
        rows = pl.ds(pl.multiple_of((side ^ group) * HALF, HALF), HALF)
        target[rows, :] = total[group * HALF : (group + 1) * HALF]


def project_kv_kernel(other, before, w_mine, first_out, second_out):
    side, flip, _, head = position()
    total = (before[:, HD:] + sibling_product(head, other, w_mine, slice(HD, 3 * HD))).astype(BF)
    near_first = side ^ (1 - flip) == 0
    first_out[...] = jnp.where(near_first, total[:HALF], total[HALF:])
    second_out[...] = jnp.where(near_first, total[HALF:], total[:HALF])


def merge_kernel(whole, part, dq, out):
    del dq
    out[:HALF, :] = (whole[:HALF, :].astype(F32) + part[...].astype(F32)).astype(BF)
    out[HALF:, :] = whole[HALF:, :]


def lay_out_kernel(own, other, out):
    side = position()[0]
    for half in range(2):
        cols = slice(half * HD, (half + 1) * HD)
        out[:, cols] = jnp.where(side == half, own[...], other[...])


def project_q_kernel(other, before, w_mine, u1, d1, q_out):
    del u1, d1
    side, _, _, head = position()
    total = before[:, :HD] + sibling_product(head, other, w_mine, slice(0, HD))
    store_groups(side, total.astype(BF), q_out)


def payload_kernel(d_own, link_rows, pack, payload):
    del pack
    side = position()[0]
    payload[:HALF, :] = jnp.where(side == 0, d_own[:, HD:], d_own[:, :HD])
    payload[HALF:, :] = link_rows[...]


def links_kernel(own, other, q, links):
    del q
    side, _, first, _ = position()
    for i in range(GROUP):
        for k in range(3 * SPAN):
            links[i, k] = jnp.where(side == i // 2, own[i % 2, k], other[i % 2, k])
        for t in (1, 2):
            base = jnp.int32(-(1 << 20))
            for j in range(SPAN):
                entry = links[i, SPAN * t + j]
                base = jnp.maximum(base, jnp.where(entry >= 0, entry - j, -(1 << 20)))
            base = jnp.where(base > -(1 << 19), base - first + REACH, REACH + i)
            links[GROUP, 2 * i + t - 1] = jnp.clip(base, 0, WINDOW - SPAN) * BLK


def regions(flip):
    left_lo, left_hi = NEAR_LEFT, NEAR_LEFT + HALF
    right_lo, right_hi = NEAR_RIGHT, NEAR_RIGHT + HALF
    pick = lambda plain, flipped: pl.multiple_of((1 - flip) * plain + flip * flipped, HALF)
    return (
        pick(OWN + HALF, OWN),
        pick(OWN, OWN + HALF),
        pick(left_hi, right_lo),
        pick(right_lo, left_hi),
        pick(left_lo, right_hi),
        pick(0, FAR_RIGHT),
        pick(right_hi, left_lo),
        pick(FAR_RIGHT, 0),
    )


def start_of(links, i, t):
    if t == 0:
        return (REACH + i - 1) * BLK
    return pl.multiple_of(links[GROUP, 2 * i + t - 1], BLK)


def is_far(i, t):
    return t == (1 if i < GROUP // 2 else 2)


def run_rows(i, t):
    return slice((i * 3 + t) * SPAN * BLK, (i * 3 + t + 1) * SPAN * BLK)


def side_factor():
    scale = HD ** -0.5
    return jnp.where(lax.broadcasted_iota(jnp.int32, (1, 2 * HD), 1) < HD, scale, 1.0).astype(F32)


def attend_kernel(
    links, q, first_kv, second_kv, u1, d1, u2, u3, d2, d3, d_own, d_other,
    mixed, pairs, win, near_acc, far_u_out, far_d_out, acc,
):
    side, flip, _, _ = position()
    scale = HD ** -0.5
    places = regions(flip)
    halves = (first_kv, second_kv, u1, d1, u2, u3, d2, d3)
    for at, half in zip(places, halves):
        win[pl.ds(at, HALF), :] = half[...]
    at_far_u, at_far_d = places[7], places[5]
    acc[...] = jnp.zeros_like(acc)
    zeros = jnp.zeros((BLK, HD), BF)
    own_cols = pl.ds(pl.multiple_of(side * HD, HD), HD)
    for i in range(GROUP):
        rows = slice(i * BLK, (i + 1) * BLK)
        here = slice((i % 2) * BLK, (i % 2 + 1) * BLK)
        d_blk = jnp.where(side == i // 2, d_own[here, own_cols], d_other[here, :])
        pair = jnp.concatenate(
            [
                jnp.concatenate([q[rows, :], zeros], axis=1),
                jnp.concatenate([zeros, d_blk], axis=1),
            ],
            axis=0,
        )
        pairs[2 * i * BLK : 2 * (i + 1) * BLK, :] = pair
        scores, prob_grads, peaks, biases = [], [], [], []
        for t in range(3):
            product = dot(win[pl.ds(start_of(links, i, t), SPAN * BLK), :], pair, ((1,), (1,)))
            for j in range(SPAN):
                block = product[j * BLK : (j + 1) * BLK]
                bias = jnp.where(links[i, SPAN * t + j] >= 0, 0.0, DEAD).astype(F32)
                scores.append(block[:, :BLK])
                prob_grads.append(block[:, BLK:])
                biases.append(bias)
                peaks.append(jnp.max(block[:, :BLK].reshape(BLK // 8, 8, BLK), axis=0) + bias)
        largest = peaks[0]
        for peak in peaks[1:]:
            largest = jnp.maximum(largest, peak)
        largest = jnp.max(largest, axis=0, keepdims=True)
        terms = []
        total = jnp.zeros((8, BLK), F32)
        weighted = jnp.zeros((8, BLK), F32)
        for n in range(3 * SPAN):
            term = jnp.exp2((scores[n] - (largest - biases[n])) * (scale * LOG2E))
            terms.append(term)
            total = total + jnp.sum(term.reshape(BLK // 8, 8, BLK), axis=0)
            weighted = weighted + jnp.sum((term * prob_grads[n]).reshape(BLK // 8, 8, BLK), axis=0)
        inverse = 1.0 / jnp.sum(total, axis=0, keepdims=True)
        row_dot = jnp.sum(weighted, axis=0, keepdims=True) * inverse
        for t in range(3):
            parts = []
            for n in range(SPAN * t, SPAN * t + SPAN):
                share = terms[n] * inverse
                grad = share * (prob_grads[n] - row_dot)
                parts.append(jnp.concatenate([grad.astype(BF), share.astype(BF)], axis=1))
            part = jnp.concatenate(parts, axis=0)
            mixed[run_rows(i, t), :] = part
            if is_far(i, t):
                acc[pl.ds(start_of(links, i, t), SPAN * BLK), :] += dot(part, pair, ((1,), (0,)))
    factor = side_factor()
    far_u_out[...] = (acc[pl.ds(at_far_u, HALF), :] * factor).astype(BF)
    far_d_out[...] = (acc[pl.ds(at_far_d, HALF), :] * factor).astype(BF)
    near_acc[:ROWS, :] = acc[NEAR_LEFT:OWN, :]
    near_acc[ROWS:, :] = acc[NEAR_RIGHT:FAR_RIGHT, :]


def near_grads_kernel(links, mixed, pairs, near_acc, first_own, second_own, u_out, d_out, acc):
    acc[NEAR_LEFT:OWN, :] = near_acc[:ROWS, :]
    acc[OWN:NEAR_RIGHT, :] = jnp.zeros((ROWS, 2 * HD), F32)
    acc[NEAR_RIGHT:FAR_RIGHT, :] = near_acc[ROWS:, :]
    for i in range(GROUP):
        pair = pairs[2 * i * BLK : 2 * (i + 1) * BLK, :]
        for t in range(3):
            if not is_far(i, t):
                at = pl.ds(start_of(links, i, t), SPAN * BLK)
                acc[at, :] += dot(mixed[run_rows(i, t), :], pair, ((1,), (0,)))
    factor = side_factor()
    first, second, u1, d1, u2, _, d2, _ = regions(position()[1])
    first_own[...] = acc[pl.ds(first, HALF), :] * factor
    second_own[...] = acc[pl.ds(second, HALF), :] * factor
    for target, at_first, at_second in ((u_out, d1, d2), (d_out, u1, u2)):
        target[:HALF, :] = (acc[pl.ds(at_first, HALF), :] * factor).astype(BF)
        target[HALF:, :] = (acc[pl.ds(at_second, HALF), :] * factor).astype(BF)


def outputs_kernel(links, mixed, win, att_own, att_other, dq_out, att):
    side = position()[0]
    for i in range(GROUP):
        rows = slice(i * BLK, (i + 1) * BLK)
        out = None
        for t in range(3):
            keys = win[pl.ds(start_of(links, i, t), SPAN * BLK), :]
            term = dot(mixed[run_rows(i, t), :], keys, ((0,), (0,)))
            out = term if out is None else out + term
        att[rows, :] = out[BLK:, HD:].astype(BF)
        dq_out[rows, :] = (out[:BLK, :HD] * (HD ** -0.5)).astype(BF)
    att_own[...] = att[pl.ds(pl.multiple_of(side * HALF, HALF), HALF), :]
    att_other[...] = att[pl.ds(pl.multiple_of((1 - side) * HALF, HALF), HALF), :]


def spread(grads, w_mine, side, head, target):
    for step in range(2):
        out = dot(grads, weight_rows(w_mine, head ^ (2 * step), 2 * HD), ((1,), (1,))).astype(BF)
        for group in range(2):
            index = 2 * group + step
            part = jnp.where(side == group, out[:HALF], out[HALF:])
            target[index * HALF : (index + 1) * HALF, :] = part


def spread_send_kernel(first_own, second_own, from_u, from_d, dq, w_mine, send, grads):
    side, flip, _, head = position()
    first = first_own[...] + from_u[HALF:, :].astype(F32) + from_d[:HALF, :].astype(F32)
    second = second_own[...] + from_u[:HALF, :].astype(F32) + from_d[HALF:, :].astype(F32)
    grads[:, :HD] = dq[...]
    grads[:HALF, HD:] = jnp.where(flip == 1, first, second).astype(BF)
    grads[HALF:, HD:] = jnp.where(flip == 1, second, first).astype(BF)
    spread(grads[...], w_mine, side, head ^ 1, send)


def spread_keep_kernel(grads, w_mine, keep):
    side, _, _, head = position()
    spread(grads[...], w_mine, side, head, keep)


def body(features, w_qkv, block_links, d_out, n_ctx, n_head):
    n_group = n_ctx // 2

    def across(value, flip_ctx, flip_head):
        pairs = [
            (c * n_head + h, (c ^ flip_ctx) * n_head + (h ^ flip_head))
            for c in range(n_ctx)
            for h in range(n_head)
        ]
        return lax.ppermute(value, ("ctx", "head"), pairs)

    def chain(value, back):
        pairs = []
        for ctx in range(n_ctx):
            group, side = divmod(ctx, 2)
            for h in range(n_head):
                to = group + (1 if h % 2 == back else -1)
                inside = 0 <= to < n_group
                target = (2 * to + side) * n_head + h if inside else ctx * n_head + (h ^ 1)
                pairs.append((ctx * n_head + h, target))
        return lax.ppermute(value, ("ctx", "head"), pairs)

    f = features
    sx = across(f, 0, 2)
    sy = across(f, 1, 0)
    sd = across(f, 1, 2)
    w = jnp.transpose(w_qkv, (1, 0, 2))

    def call(kernel, name, outs, ins, mebibytes, flops, scratch=()):
        specs = [SMEM if v.dtype == jnp.int32 else VMEM for v in ins]
        if kernel is begin_kernel:
            specs = [pl.BlockSpec(memory_space=pltpu.HBM)] * 2
            ins = [pltpu.with_memory_space_constraint(v, pltpu.HBM) for v in ins]
        return pl.pallas_call(
            kernel,
            name=name,
            out_shape=outs,
            in_specs=specs,
            out_specs=[SMEM if v.dtype == jnp.int32 else VMEM for v in outs],
            scratch_shapes=list(scratch),
            **params(flops, 2 << 20, mebibytes),
        )(*ins)

    def out(rows, cols, kind=BF):
        return jax.ShapeDtypeStruct((rows, cols), kind)

    def held(rows, cols, kind=BF):
        return pltpu.VMEM((rows, cols), kind)

    product = 2 * ROWS * f.shape[1] * 3 * HD
    attention = 2 * GROUP * 9 * BLK * BLK * 2 * HD
    w_mine, fm, total = call(
        begin_kernel,
        "begin",
        [held(w.shape[1], 3 * HD), held(*f.shape), held(HALF, 3 * HD, F32)],
        (f, w),
        4,
        product,
        [pltpu.SemaphoreType.DMA((4,))],
    )
    (pack,) = call(pack_kernel, "pack", [out(4 * HALF, f.shape[1])], (fm, sy, sx, sd), 4, 0)
    other = across(pack, 0, 1)
    (total,) = call(
        project_across_kernel, "project_across", [held(ROWS, 3 * HD, F32)], (pack, total, w_mine), 4, product
    )
    first, second = call(
        project_kv_kernel, "project_kv", [out(HALF, 2 * HD)] * 2, (other, total, w_mine), 4, product
    )

    u1 = chain(first, 0)
    d1 = chain(second, 1)
    u2 = chain(second, 0)
    d2 = chain(first, 1)
    u3 = chain(u1, 0)
    d3 = chain(d1, 1)
    rows, slots = block_links.shape
    link_rows = jnp.pad(block_links.astype(BF), ((0, 16 - rows), (0, HD - slots)))
    (payload,) = call(payload_kernel, "payload", [out(HALF + 16, HD)], (d_out, link_rows, pack), 4, 0)
    d_other = across(payload, 1, 0)
    (q,) = call(project_q_kernel, "project_q", [held(ROWS, HD)], (other, total, w_mine, u1, d1), 4, product)
    other_links = d_other[HALF : HALF + rows, :slots].astype(jnp.int32)
    (links,) = call(
        links_kernel, "links", [pltpu.SMEM((GROUP + 1, slots), jnp.int32)], (block_links, other_links, q), 4, 0
    )
    links = pltpu.with_memory_space_constraint(links, pltpu.SMEM)
    mixed, pairs, win, near_acc, far_u_grad, far_d_grad = call(
        attend_kernel,
        "attend",
        [
            held(GROUP * 9 * BLK, 2 * HD),
            held(GROUP * 2 * BLK, 2 * HD),
            held(WINDOW * BLK, 2 * HD),
            held(2 * ROWS, 2 * HD, F32),
            out(HALF, 2 * HD),
            out(HALF, 2 * HD),
        ],
        (links, q, first, second, u1, d1, u2, u3, d2, d3, d_out, d_other),
        8,
        2 * attention,
        [pltpu.VMEM((WINDOW * BLK, 2 * HD), F32)],
    )
    first_own, second_own, u_grad, d_grad = call(
        near_grads_kernel,
        "near_grads",
        [held(HALF, 2 * HD, F32)] * 2 + [out(ROWS, 2 * HD)] * 2,
        (links, mixed, pairs, near_acc),
        4,
        attention,
        [pltpu.VMEM((WINDOW * BLK, 2 * HD), F32)],
    )
    att_own, att_other, dq = call(
        outputs_kernel,
        "outputs",
        [out(HALF, HD), out(HALF, HD), held(ROWS, HD)],
        (links, mixed, win),
        4,
        attention,
        [pltpu.VMEM((ROWS, HD), BF)],
    )

    back_u = chain(far_u_grad, 0)
    back_d = chain(far_d_grad, 1)

    def merge(whole, part, name):
        return call(merge_kernel, name, [out(ROWS, 2 * HD)], (whole, part, dq), 4, 0)[0]

    from_u = chain(merge(u_grad, back_u, "merge_u"), 0)
    from_d = chain(merge(d_grad, back_d, "merge_d"), 1)
    att_back = across(att_other, 1, 0)
    from_u, from_d, att_back = lax.optimization_barrier((from_u, from_d, att_back))
    (attended,) = call(lay_out_kernel, "lay_out", [out(HALF, 2 * HD)], (att_own, att_back), 4, 0)
    send, grads = call(
        spread_send_kernel,
        "spread_send",
        [out(4 * HALF, 2 * HD), held(ROWS, 3 * HD)],
        (first_own, second_own, from_u, from_d, dq, w_mine),
        4,
        product,
    )
    (keep,) = call(spread_keep_kernel, "spread_keep", [held(4 * HALF, 2 * HD)], (grads, w_mine), 4, product)
    arrived = across(send, 0, 1)
    chip = (keep.astype(F32) + arrived.astype(F32)).astype(BF)
    gd = across(chip[3 * HALF :], 1, 2)
    gy = across(chip[2 * HALF : 3 * HALF], 1, 0)
    gx = across(chip[HALF : 2 * HALF], 0, 2)
    grad_features = (
        chip[:HALF].astype(F32) + gd.astype(F32) + gy.astype(F32) + gx.astype(F32)
    ).astype(BF)
    return attended, grad_features


def solution(mesh):
    sizes = dict(mesh.shape)
    return jax.shard_map(
        functools.partial(body, n_ctx=sizes["ctx"], n_head=sizes["head"]),
        mesh=mesh,
        in_specs=(P("ctx", "head"), P(None, None, "head"), P("ctx", None), P("ctx", "head")),
        out_specs=(P("ctx", "head"), P("ctx", "head")),
        check_vma=False,
    )
```

```python
import functools

import jax
import jax.numpy as jnp
from jax import lax
from jax.experimental import pallas as pl
from jax.experimental.pallas import tpu as pltpu
from jax.sharding import PartitionSpec as P

HD = 128
BLK = 128
REACH = 6
SPAN = 3
LOG2E = 1.4426950408889634
DEAD = -1e30
BF = jnp.bfloat16
F32 = jnp.float32

GROUP = 4
ROWS = GROUP * BLK
HALF = ROWS // 2
WINDOW = GROUP + 2 * REACH
NEAR_LEFT = (REACH - GROUP) * BLK
OWN = REACH * BLK
NEAR_RIGHT = OWN + ROWS
FAR_RIGHT = NEAR_RIGHT + ROWS


def params(flops, moved, mebibytes):
    return dict(
        compiler_params=pltpu.CompilerParams(vmem_limit_bytes=mebibytes * 1024 * 1024),
        cost_estimate=pl.CostEstimate(flops=flops, bytes_accessed=moved, transcendentals=0),
    )


VMEM = pl.BlockSpec(memory_space=pltpu.VMEM)
SMEM = pl.BlockSpec(memory_space=pltpu.SMEM)


def dot(a, b, dims):
    return lax.dot_general(a, b, (dims, ((), ())), preferred_element_type=F32)


def position():
    ctx, head = lax.axis_index("ctx"), lax.axis_index("head")
    return ctx % 2, head % 2, ctx // 2 * GROUP, head


def begin_kernel(f, w, w_mine, fm, total, sems):
    side, _, _, head = position()
    copies = [pltpu.make_async_copy(f, fm, sems.at[3])]
    for g in range(3):
        cols = pl.ds(pl.multiple_of(side * HD, HD), HD)
        copies.append(pltpu.make_async_copy(w.at[g, :, cols], w_mine.at[:, pl.ds(g * HD, HD)], sems.at[g]))
    for copy in copies:
        copy.start()
    for copy in copies:
        copy.wait()
    total[...] = dot(fm[...], weight_rows(w_mine, head, fm.shape[1]), ((1,), (0,)))


def weight_rows(w_mine, source, width):
    return w_mine[pl.ds(pl.multiple_of(source * width, width), width), :]


def pack_kernel(fm, sy, sx, sd, out):
    for index, piece in enumerate((fm, sy, sx, sd)):
        out[index * HALF : (index + 1) * HALF, :] = piece[...]


def project_across_kernel(pack, before, w_mine, total):
    head = position()[3]
    width = pack.shape[1]
    far = dot(pack[2 * HALF :, :], weight_rows(w_mine, head ^ 2, width), ((1,), (0,)))
    total[:HALF, :] = before[...] + far[:HALF]
    total[HALF:, :] = far[HALF:] + dot(pack[HALF : 2 * HALF, :], weight_rows(w_mine, head, width), ((1,), (0,)))


def sibling_product(head, other, w_mine, cols):
    width = other.shape[1]
    total = None
    for index in range(2):
        rows = pl.ds(pl.multiple_of((head ^ (1 + 2 * index)) * width, width), width)
        term = dot(other[2 * index * HALF : 2 * (index + 1) * HALF, :], w_mine[rows, cols], ((1,), (0,)))
        total = term if total is None else total + term
    return total


def store_groups(side, total, target):
    for group in range(2):
        rows = pl.ds(pl.multiple_of((side ^ group) * HALF, HALF), HALF)
        target[rows, :] = total[group * HALF : (group + 1) * HALF]


def project_kv_kernel(other, before, w_mine, first_out, second_out):
    side, flip, _, head = position()
    total = (before[:, HD:] + sibling_product(head, other, w_mine, slice(HD, 3 * HD))).astype(BF)
    near_first = side ^ (1 - flip) == 0
    first_out[...] = jnp.where(near_first, total[:HALF], total[HALF:])
    second_out[...] = jnp.where(near_first, total[HALF:], total[:HALF])


def merge_kernel(whole, part, dq, out):
    del dq
    out[:HALF, :] = (whole[:HALF, :].astype(F32) + part[...].astype(F32)).astype(BF)
    out[HALF:, :] = whole[HALF:, :]


def lay_out_kernel(own, other, out):
    side = position()[0]
    for half in range(2):
        cols = slice(half * HD, (half + 1) * HD)
        out[:, cols] = jnp.where(side == half, own[...], other[...])


def project_q_kernel(other, before, w_mine, u1, d1, q_out):
    del u1, d1
    side, _, _, head = position()
    total = before[:, :HD] + sibling_product(head, other, w_mine, slice(0, HD))
    store_groups(side, total.astype(BF), q_out)


def payload_kernel(d_own, link_rows, pack, payload):
    del pack
    side = position()[0]
    payload[:HALF, :] = jnp.where(side == 0, d_own[:, HD:], d_own[:, :HD])
    payload[HALF:, :] = link_rows[...]


def links_kernel(own, other, q, links):
    del q
    side, _, first, _ = position()
    for i in range(GROUP):
        for k in range(3 * SPAN):
            links[i, k] = jnp.where(side == i // 2, own[i % 2, k], other[i % 2, k])
        for t in (1, 2):
            base = jnp.int32(-(1 << 20))
            for j in range(SPAN):
                entry = links[i, SPAN * t + j]
                base = jnp.maximum(base, jnp.where(entry >= 0, entry - j, -(1 << 20)))
            base = jnp.where(base > -(1 << 19), base - first + REACH, REACH + i)
            links[GROUP, 2 * i + t - 1] = jnp.clip(base, 0, WINDOW - SPAN) * BLK


def regions(flip):
    left_lo, left_hi = NEAR_LEFT, NEAR_LEFT + HALF
    right_lo, right_hi = NEAR_RIGHT, NEAR_RIGHT + HALF
    pick = lambda plain, flipped: pl.multiple_of((1 - flip) * plain + flip * flipped, HALF)
    return (
        pick(OWN + HALF, OWN),
        pick(OWN, OWN + HALF),
        pick(left_hi, right_lo),
        pick(right_lo, left_hi),
        pick(left_lo, right_hi),
        pick(0, FAR_RIGHT),
        pick(right_hi, left_lo),
        pick(FAR_RIGHT, 0),
    )


def start_of(links, i, t):
    if t == 0:
        return (REACH + i - 1) * BLK
    return pl.multiple_of(links[GROUP, 2 * i + t - 1], BLK)


def far_run(i):
    return 1 if i < GROUP // 2 else 2


def near_runs(i):
    return tuple(t for t in range(3) if t != far_run(i))


def near_rows(i, index, j):
    first = ((2 * i + index) * SPAN + j) * BLK
    return slice(first, first + BLK)


def far_rows(i):
    return slice(i * SPAN * BLK, (i + 1) * SPAN * BLK)


def run_scores(links, rows, pair, i, t):
    product = dot(rows, pair, ((1,), (1,)))
    blocks = []
    for j in range(SPAN):
        block = product[j * BLK : (j + 1) * BLK]
        bias = jnp.where(links[i, SPAN * t + j] >= 0, 0.0, DEAD).astype(F32)
        blocks.append((block[:, :BLK], block[:, BLK:], bias))
    return blocks


def fold(block):
    return block.reshape(BLK // 8, 8, BLK)


def largest_of(blocks):
    best = None
    for score, _, bias in blocks:
        peak = jnp.max(fold(score), axis=0) + bias
        best = peak if best is None else jnp.maximum(best, peak)
    return jnp.max(best, axis=0, keepdims=True)


def exponentials(blocks, largest):
    terms = []
    total = jnp.zeros((8, BLK), F32)
    weighted = jnp.zeros((8, BLK), F32)
    for score, prob_grad, bias in blocks:
        term = jnp.exp2((score - (largest - bias)) * (HD ** -0.5 * LOG2E))
        terms.append(term)
        total = total + jnp.sum(fold(term), axis=0)
        weighted = weighted + jnp.sum(fold(term * prob_grad), axis=0)
    return terms, jnp.sum(total, axis=0, keepdims=True), jnp.sum(weighted, axis=0, keepdims=True)


def mix(share, prob_grad, row_dot):
    grad = share * (prob_grad - row_dot)
    return jnp.concatenate([grad.astype(BF), share.astype(BF)], axis=1)


def side_factor():
    scale = HD ** -0.5
    return jnp.where(lax.broadcasted_iota(jnp.int32, (1, 2 * HD), 1) < HD, scale, 1.0).astype(F32)


def near_scores_kernel(
    links, q, first_kv, second_kv, u1, d1, u2, d2, d_own, d_other,
    pairs, terms_out, prob_grads_out, stats, win,
):
    side, flip, _, _ = position()
    places = regions(flip)
    for at, half in zip(places[:5] + places[6:7], (first_kv, second_kv, u1, d1, u2, d2)):
        win[pl.ds(at, HALF), :] = half[...]
    zeros = jnp.zeros((BLK, HD), BF)
    own_cols = pl.ds(pl.multiple_of(side * HD, HD), HD)
    for i in range(GROUP):
        rows = slice(i * BLK, (i + 1) * BLK)
        here = slice((i % 2) * BLK, (i % 2 + 1) * BLK)
        d_blk = jnp.where(side == i // 2, d_own[here, own_cols], d_other[here, :])
        pair = jnp.concatenate(
            [
                jnp.concatenate([q[rows, :], zeros], axis=1),
                jnp.concatenate([zeros, d_blk], axis=1),
            ],
            axis=0,
        )
        pairs[2 * i * BLK : 2 * (i + 1) * BLK, :] = pair
        blocks = []
        for t in near_runs(i):
            blocks += run_scores(links, win[pl.ds(start_of(links, i, t), SPAN * BLK), :], pair, i, t)
        largest = largest_of(blocks)
        terms, total, weighted = exponentials(blocks, largest)
        for n, term in enumerate(terms):
            terms_out[near_rows(i, 0, n), :] = term
            prob_grads_out[near_rows(i, 0, n), :] = blocks[n][1]
        for n, row in enumerate((largest, total, weighted)):
            stats[8 * (3 * i + n) : 8 * (3 * i + n + 1), :] = jnp.broadcast_to(row, (8, BLK))


def far_grads_kernel(
    links, pairs, stats, u1, d1, u2, u3, d2, d3,
    mixed, near_acc, far_u_out, far_d_out, scales, win, acc,
):
    places = regions(position()[1])
    for at, half in zip(places[2:], (u1, d1, u2, u3, d2, d3)):
        win[pl.ds(at, HALF), :] = half[...]
    acc[:OWN, :] = jnp.zeros((OWN, 2 * HD), F32)
    acc[NEAR_RIGHT:, :] = jnp.zeros((OWN, 2 * HD), F32)
    for i in range(GROUP):
        pair = pairs[2 * i * BLK : 2 * (i + 1) * BLK, :]
        at = pl.ds(start_of(links, i, far_run(i)), SPAN * BLK)
        blocks = run_scores(links, win[at, :], pair, i, far_run(i))
        near_largest, near_total, near_weighted = (stats[8 * (3 * i + n) : 8 * (3 * i + n) + 1, :] for n in range(3))
        largest = jnp.maximum(near_largest, largest_of(blocks))
        terms, total, weighted = exponentials(blocks, largest)
        near_scale = jnp.exp2((near_largest - largest) * (HD ** -0.5 * LOG2E))
        inverse = 1.0 / (total + near_scale * near_total)
        row_dot = (weighted + near_scale * near_weighted) * inverse
        for n, row in enumerate((near_scale * inverse, row_dot)):
            scales[8 * (2 * i + n) : 8 * (2 * i + n + 1), :] = jnp.broadcast_to(row, (8, BLK))
        part = jnp.concatenate(
            [mix(term * inverse, block[1], row_dot) for term, block in zip(terms, blocks)], axis=0
        )
        mixed[far_rows(i), :] = part
        acc[at, :] += dot(part, pair, ((1,), (0,)))
    factor = side_factor()
    far_u_out[...] = (acc[pl.ds(places[7], HALF), :] * factor).astype(BF)
    far_d_out[...] = (acc[pl.ds(places[5], HALF), :] * factor).astype(BF)
    near_acc[:ROWS, :] = acc[NEAR_LEFT:OWN, :]
    near_acc[ROWS:, :] = acc[NEAR_RIGHT:FAR_RIGHT, :]


def near_grads_kernel(
    links, pairs, terms, prob_grads, scales, near_acc, mixed, first_own, second_own, u_out, d_out, acc
):
    acc[NEAR_LEFT:OWN, :] = near_acc[:ROWS, :]
    acc[OWN:NEAR_RIGHT, :] = jnp.zeros((ROWS, 2 * HD), F32)
    acc[NEAR_RIGHT:FAR_RIGHT, :] = near_acc[ROWS:, :]
    for i in range(GROUP):
        pair = pairs[2 * i * BLK : 2 * (i + 1) * BLK, :]
        scale, row_dot = (scales[8 * (2 * i + n) : 8 * (2 * i + n) + 1, :] for n in range(2))
        for index, t in enumerate(near_runs(i)):
            parts = []
            for j in range(SPAN):
                rows = near_rows(i, index, j)
                parts.append(mix(terms[rows, :] * scale, prob_grads[rows, :], row_dot))
                mixed[rows, :] = parts[-1]
            at = pl.ds(start_of(links, i, t), SPAN * BLK)
            acc[at, :] += dot(jnp.concatenate(parts, axis=0), pair, ((1,), (0,)))
    factor = side_factor()
    first, second, u1, d1, u2, _, d2, _ = regions(position()[1])
    first_own[...] = acc[pl.ds(first, HALF), :] * factor
    second_own[...] = acc[pl.ds(second, HALF), :] * factor
    for target, at_first, at_second in ((u_out, d1, d2), (d_out, u1, u2)):
        target[:HALF, :] = (acc[pl.ds(at_first, HALF), :] * factor).astype(BF)
        target[HALF:, :] = (acc[pl.ds(at_second, HALF), :] * factor).astype(BF)


def outputs_kernel(
    links, near_mixed, far_mixed, first_kv, second_kv, u1, d1, u2, u3, d2, d3,
    att_own, att_other, dq_out, win, att,
):
    side, flip, _, _ = position()
    for at, half in zip(regions(flip), (first_kv, second_kv, u1, d1, u2, u3, d2, d3)):
        win[pl.ds(at, HALF), :] = half[...]
    for i in range(GROUP):
        rows = slice(i * BLK, (i + 1) * BLK)
        out = dot(
            far_mixed[far_rows(i), :], win[pl.ds(start_of(links, i, far_run(i)), SPAN * BLK), :], ((0,), (0,))
        )
        for index, t in enumerate(near_runs(i)):
            part = near_mixed[near_rows(i, index, 0).start : near_rows(i, index, SPAN - 1).stop, :]
            out = out + dot(part, win[pl.ds(start_of(links, i, t), SPAN * BLK), :], ((0,), (0,)))
        att[rows, :] = out[BLK:, HD:].astype(BF)
        dq_out[rows, :] = (out[:BLK, :HD] * (HD ** -0.5)).astype(BF)
    att_own[...] = att[pl.ds(pl.multiple_of(side * HALF, HALF), HALF), :]
    att_other[...] = att[pl.ds(pl.multiple_of((1 - side) * HALF, HALF), HALF), :]


def spread(grads, w_mine, side, head, target):
    for step in range(2):
        out = dot(grads, weight_rows(w_mine, head ^ (2 * step), 2 * HD), ((1,), (1,))).astype(BF)
        for group in range(2):
            index = 2 * group + step
            part = jnp.where(side == group, out[:HALF], out[HALF:])
            target[index * HALF : (index + 1) * HALF, :] = part


def spread_send_kernel(first_own, second_own, from_u, from_d, dq, w_mine, send, grads):
    side, flip, _, head = position()
    first = first_own[...] + from_u[HALF:, :].astype(F32) + from_d[:HALF, :].astype(F32)
    second = second_own[...] + from_u[:HALF, :].astype(F32) + from_d[HALF:, :].astype(F32)
    grads[:, :HD] = dq[...]
    grads[:HALF, HD:] = jnp.where(flip == 1, first, second).astype(BF)
    grads[HALF:, HD:] = jnp.where(flip == 1, second, first).astype(BF)
    spread(grads[...], w_mine, side, head ^ 1, send)


def spread_keep_kernel(grads, w_mine, keep):
    side, _, _, head = position()
    spread(grads[...], w_mine, side, head, keep)


def body(features, w_qkv, block_links, d_out, n_ctx, n_head):
    n_group = n_ctx // 2

    def across(value, flip_ctx, flip_head):
        pairs = [
            (c * n_head + h, (c ^ flip_ctx) * n_head + (h ^ flip_head))
            for c in range(n_ctx)
            for h in range(n_head)
        ]
        return lax.ppermute(value, ("ctx", "head"), pairs)

    def chain(value, back):
        pairs = []
        for ctx in range(n_ctx):
            group, side = divmod(ctx, 2)
            for h in range(n_head):
                to = group + (1 if h % 2 == back else -1)
                inside = 0 <= to < n_group
                target = (2 * to + side) * n_head + h if inside else ctx * n_head + (h ^ 1)
                pairs.append((ctx * n_head + h, target))
        return lax.ppermute(value, ("ctx", "head"), pairs)

    f = features
    sx = across(f, 0, 2)
    sy = across(f, 1, 0)
    sd = across(f, 1, 2)
    w = jnp.transpose(w_qkv, (1, 0, 2))

    def call(kernel, name, outs, ins, mebibytes, flops, scratch=()):
        specs = [SMEM if v.dtype == jnp.int32 else VMEM for v in ins]
        if kernel is begin_kernel:
            specs = [pl.BlockSpec(memory_space=pltpu.HBM)] * 2
            ins = [pltpu.with_memory_space_constraint(v, pltpu.HBM) for v in ins]
        return pl.pallas_call(
            kernel,
            name=name,
            out_shape=outs,
            in_specs=specs,
            out_specs=[SMEM if v.dtype == jnp.int32 else VMEM for v in outs],
            scratch_shapes=list(scratch),
            **params(flops, 2 << 20, mebibytes),
        )(*ins)

    def out(rows, cols, kind=BF):
        return jax.ShapeDtypeStruct((rows, cols), kind)

    def held(rows, cols, kind=BF):
        return pltpu.VMEM((rows, cols), kind)

    product = 2 * ROWS * f.shape[1] * 3 * HD
    attention = 2 * GROUP * 9 * BLK * BLK * 2 * HD
    w_mine, fm, total = call(
        begin_kernel,
        "begin",
        [held(w.shape[1], 3 * HD), held(*f.shape), held(HALF, 3 * HD, F32)],
        (f, w),
        4,
        product,
        [pltpu.SemaphoreType.DMA((4,))],
    )
    (pack,) = call(pack_kernel, "pack", [out(4 * HALF, f.shape[1])], (fm, sy, sx, sd), 4, 0)
    other = across(pack, 0, 1)
    (total,) = call(
        project_across_kernel, "project_across", [held(ROWS, 3 * HD, F32)], (pack, total, w_mine), 4, product
    )
    first, second = call(
        project_kv_kernel, "project_kv", [out(HALF, 2 * HD)] * 2, (other, total, w_mine), 4, product
    )

    u1 = chain(first, 0)
    d1 = chain(second, 1)
    u2 = chain(second, 0)
    d2 = chain(first, 1)
    u3 = chain(u1, 0)
    d3 = chain(d1, 1)
    rows, slots = block_links.shape
    link_rows = jnp.pad(block_links.astype(BF), ((0, 16 - rows), (0, HD - slots)))
    (payload,) = call(payload_kernel, "payload", [out(HALF + 16, HD)], (d_out, link_rows, pack), 4, 0)
    d_other = across(payload, 1, 0)
    (q,) = call(project_q_kernel, "project_q", [held(ROWS, HD)], (other, total, w_mine, u1, d1), 4, product)
    other_links = d_other[HALF : HALF + rows, :slots].astype(jnp.int32)
    (links,) = call(
        links_kernel, "links", [pltpu.SMEM((GROUP + 1, slots), jnp.int32)], (block_links, other_links, q), 4, 0
    )
    links = pltpu.with_memory_space_constraint(links, pltpu.SMEM)
    window = pltpu.VMEM((WINDOW * BLK, 2 * HD), BF)
    sums = pltpu.VMEM((WINDOW * BLK, 2 * HD), F32)
    run = SPAN * BLK
    pairs, terms, prob_grads, stats = call(
        near_scores_kernel,
        "near_scores",
        [
            held(GROUP * 2 * BLK, 2 * HD),
            held(GROUP * 2 * run, BLK, F32),
            held(GROUP * 2 * run, BLK, F32),
            held(GROUP * 3 * 8, BLK, F32),
        ],
        (links, q, first, second, u1, d1, u2, d2, d_out, d_other),
        6,
        attention,
        [window],
    )
    far_mixed, near_acc, far_u_grad, far_d_grad, scales = call(
        far_grads_kernel,
        "far_grads",
        [
            held(GROUP * run, 2 * HD),
            held(2 * ROWS, 2 * HD, F32),
            out(HALF, 2 * HD),
            out(HALF, 2 * HD),
            held(GROUP * 2 * 8, BLK, F32),
        ],
        (links, pairs, stats, u1, d1, u2, u3, d2, d3),
        6,
        attention,
        [window, sums],
    )
    near_mixed, first_own, second_own, u_grad, d_grad = call(
        near_grads_kernel,
        "near_grads",
        [held(GROUP * 2 * run, 2 * HD)] + [held(HALF, 2 * HD, F32)] * 2 + [out(ROWS, 2 * HD)] * 2,
        (links, pairs, terms, prob_grads, scales, near_acc),
        4,
        attention,
        [sums],
    )
    att_own, att_other, dq = call(
        outputs_kernel,
        "outputs",
        [out(HALF, HD), out(HALF, HD), held(ROWS, HD)],
        (links, near_mixed, far_mixed, first, second, u1, d1, u2, u3, d2, d3),
        4,
        attention,
        [window, pltpu.VMEM((ROWS, HD), BF)],
    )

    back_u = chain(far_u_grad, 0)
    back_d = chain(far_d_grad, 1)

    def merge(whole, part, name):
        return call(merge_kernel, name, [out(ROWS, 2 * HD)], (whole, part, dq), 4, 0)[0]

    from_u = chain(merge(u_grad, back_u, "merge_u"), 0)
    from_d = chain(merge(d_grad, back_d, "merge_d"), 1)
    att_back = across(att_other, 1, 0)
    from_u, from_d, att_back = lax.optimization_barrier((from_u, from_d, att_back))
    (attended,) = call(lay_out_kernel, "lay_out", [out(HALF, 2 * HD)], (att_own, att_back), 4, 0)
    send, grads = call(
        spread_send_kernel,
        "spread_send",
        [out(4 * HALF, 2 * HD), held(ROWS, 3 * HD)],
        (first_own, second_own, from_u, from_d, dq, w_mine),
        4,
        product,
    )
    (keep,) = call(spread_keep_kernel, "spread_keep", [held(4 * HALF, 2 * HD)], (grads, w_mine), 4, product)
    arrived = across(send, 0, 1)
    chip = (keep.astype(F32) + arrived.astype(F32)).astype(BF)
    gd = across(chip[3 * HALF :], 1, 2)
    gy = across(chip[2 * HALF : 3 * HALF], 1, 0)
    gx = across(chip[HALF : 2 * HALF], 0, 2)
    grad_features = (
        chip[:HALF].astype(F32) + gd.astype(F32) + gy.astype(F32) + gx.astype(F32)
    ).astype(BF)
    return attended, grad_features


def solution(mesh):
    sizes = dict(mesh.shape)
    return jax.shard_map(
        functools.partial(body, n_ctx=sizes["ctx"], n_head=sizes["head"]),
        mesh=mesh,
        in_specs=(P("ctx", "head"), P(None, None, "head"), P("ctx", None), P("ctx", "head")),
        out_specs=(P("ctx", "head"), P("ctx", "head")),
        check_vma=False,
    )
```

```python
import functools

import jax
import jax.numpy as jnp
from jax import lax
from jax.experimental import pallas as pl
from jax.experimental.pallas import tpu as pltpu
from jax.sharding import PartitionSpec as P

HD = 128
BLK = 128
REACH = 6
SPAN = 3
LOG2E = 1.4426950408889634
DEAD = -1e30
BF = jnp.bfloat16
F32 = jnp.float32

GROUP = 4
ROWS = GROUP * BLK
HALF = ROWS // 2
WINDOW = GROUP + 2 * REACH
NEAR_LEFT = (REACH - GROUP) * BLK
OWN = REACH * BLK
NEAR_RIGHT = OWN + ROWS
FAR_RIGHT = NEAR_RIGHT + ROWS


def params(flops, moved, mebibytes):
    return dict(
        compiler_params=pltpu.CompilerParams(vmem_limit_bytes=mebibytes * 1024 * 1024),
        cost_estimate=pl.CostEstimate(flops=flops, bytes_accessed=moved, transcendentals=0),
    )


VMEM = pl.BlockSpec(memory_space=pltpu.VMEM)
SMEM = pl.BlockSpec(memory_space=pltpu.SMEM)


def dot(a, b, dims):
    return lax.dot_general(a, b, (dims, ((), ())), preferred_element_type=F32)


def position():
    ctx, head = lax.axis_index("ctx"), lax.axis_index("head")
    return ctx % 2, head % 2, ctx // 2 * GROUP, head


def begin_kernel(f, w, w_mine, fm, total, sems):
    side, _, _, head = position()
    copies = [pltpu.make_async_copy(f, fm, sems.at[3])]
    for g in range(3):
        cols = pl.ds(pl.multiple_of(side * HD, HD), HD)
        copies.append(pltpu.make_async_copy(w.at[g, :, cols], w_mine.at[:, pl.ds(g * HD, HD)], sems.at[g]))
    for copy in copies:
        copy.start()
    for copy in copies:
        copy.wait()
    total[...] = dot(fm[...], weight_rows(w_mine, head, fm.shape[1]), ((1,), (0,)))


def weight_rows(w_mine, source, width):
    return w_mine[pl.ds(pl.multiple_of(source * width, width), width), :]


def pack_kernel(fm, sd, sx, sy, out):
    for index, piece in enumerate((fm, sy, sx, sd)):
        out[index * HALF : (index + 1) * HALF, :] = piece[...]


def project_across_kernel(pack, before, w_mine, total):
    head = position()[3]
    width = pack.shape[1]
    far = dot(pack[2 * HALF :, :], weight_rows(w_mine, head ^ 2, width), ((1,), (0,)))
    total[:HALF, :] = before[...] + far[:HALF]
    total[HALF:, :] = far[HALF:] + dot(pack[HALF : 2 * HALF, :], weight_rows(w_mine, head, width), ((1,), (0,)))


def sibling_product(head, other, w_mine, cols):
    width = other.shape[1]
    total = None
    for index in range(2):
        rows = pl.ds(pl.multiple_of((head ^ (1 + 2 * index)) * width, width), width)
        term = dot(other[2 * index * HALF : 2 * (index + 1) * HALF, :], w_mine[rows, cols], ((1,), (0,)))
        total = term if total is None else total + term
    return total


def store_groups(side, total, target):
    for group in range(2):
        rows = pl.ds(pl.multiple_of((side ^ group) * HALF, HALF), HALF)
        target[rows, :] = total[group * HALF : (group + 1) * HALF]


def project_kv_kernel(other, before, w_mine, first_out, second_out):
    side, flip, _, head = position()
    total = (before[:, HD:] + sibling_product(head, other, w_mine, slice(HD, 3 * HD))).astype(BF)
    near_first = side ^ (1 - flip) == 0
    first_out[...] = jnp.where(near_first, total[:HALF], total[HALF:])
    second_out[...] = jnp.where(near_first, total[HALF:], total[:HALF])


def merge_kernel(whole, part, dq, out):
    del dq
    out[:HALF, :] = (whole[:HALF, :].astype(F32) + part[...].astype(F32)).astype(BF)
    out[HALF:, :] = whole[HALF:, :]


def lay_out_kernel(own, other, out):
    side = position()[0]
    for half in range(2):
        cols = slice(half * HD, (half + 1) * HD)
        out[:, cols] = jnp.where(side == half, own[...], other[...])


def project_q_kernel(other, before, w_mine, u1, d1, q_out):
    del u1, d1
    side, _, _, head = position()
    total = before[:, :HD] + sibling_product(head, other, w_mine, slice(0, HD))
    store_groups(side, total.astype(BF), q_out)


def payload_kernel(d_own, link_rows, pack, payload):
    del pack
    side = position()[0]
    payload[:HALF, :] = jnp.where(side == 0, d_own[:, HD:], d_own[:, :HD])
    payload[HALF:, :] = link_rows[...]


def links_kernel(own, other, q, links):
    del q
    side, _, first, _ = position()
    for i in range(GROUP):
        for k in range(3 * SPAN):
            links[i, k] = jnp.where(side == i // 2, own[i % 2, k], other[i % 2, k])
        for t in (1, 2):
            base = jnp.int32(-(1 << 20))
            for j in range(SPAN):
                entry = links[i, SPAN * t + j]
                base = jnp.maximum(base, jnp.where(entry >= 0, entry - j, -(1 << 20)))
            base = jnp.where(base > -(1 << 19), base - first + REACH, i + 1 if t == 1 else i + REACH + SPAN)
            links[GROUP, 2 * i + t - 1] = jnp.clip(base, 0, WINDOW - SPAN) * BLK


def regions(flip):
    left_lo, left_hi = NEAR_LEFT, NEAR_LEFT + HALF
    right_lo, right_hi = NEAR_RIGHT, NEAR_RIGHT + HALF
    pick = lambda plain, flipped: pl.multiple_of((1 - flip) * plain + flip * flipped, HALF)
    return (
        pick(OWN + HALF, OWN),
        pick(OWN, OWN + HALF),
        pick(left_hi, right_lo),
        pick(right_lo, left_hi),
        pick(left_lo, right_hi),
        pick(0, FAR_RIGHT),
        pick(right_hi, left_lo),
        pick(FAR_RIGHT, 0),
    )


def start_of(links, i, t):
    if t == 0:
        return (REACH + i - 1) * BLK
    return pl.multiple_of(links[GROUP, 2 * i + t - 1], BLK)


def far_run(i):
    return 1 if i < GROUP // 2 else 2


def near_runs(i):
    return tuple(t for t in range(3) if t != far_run(i))


def near_rows(i, index, j):
    first = ((2 * i + index) * SPAN + j) * BLK
    return slice(first, first + BLK)


def far_rows(i):
    return slice(i * SPAN * BLK, (i + 1) * SPAN * BLK)


def run_scores(links, rows, pair, i, t):
    product = dot(rows, pair, ((1,), (1,)))
    blocks = []
    for j in range(SPAN):
        block = product[j * BLK : (j + 1) * BLK]
        bias = jnp.where(links[i, SPAN * t + j] >= 0, 0.0, DEAD).astype(F32)
        blocks.append((block[:, :BLK], block[:, BLK:], bias))
    return blocks


def fold(block):
    return block.reshape(BLK // 8, 8, BLK)


def largest_of(blocks):
    best = None
    for score, _, bias in blocks:
        peak = jnp.max(fold(score), axis=0) + bias
        best = peak if best is None else jnp.maximum(best, peak)
    return jnp.max(best, axis=0, keepdims=True)


def exponentials(blocks, largest):
    terms = []
    total = jnp.zeros((8, BLK), F32)
    weighted = jnp.zeros((8, BLK), F32)
    for score, prob_grad, bias in blocks:
        term = jnp.exp2((score - (largest - bias)) * (HD ** -0.5 * LOG2E))
        terms.append(term)
        total = total + jnp.sum(fold(term), axis=0)
        weighted = weighted + jnp.sum(fold(term * prob_grad), axis=0)
    return terms, jnp.sum(total, axis=0, keepdims=True), jnp.sum(weighted, axis=0, keepdims=True)


def mix(share, prob_grad, row_dot):
    grad = share * (prob_grad - row_dot)
    return jnp.concatenate([grad.astype(BF), share.astype(BF)], axis=1)


def side_factor():
    scale = HD ** -0.5
    return jnp.where(lax.broadcasted_iota(jnp.int32, (1, 2 * HD), 1) < HD, scale, 1.0).astype(F32)


def near_scores_kernel(
    links, q, first_kv, second_kv, u1, d1, u2, d2, d_own, d_other,
    pairs, terms_out, prob_grads_out, stats, win,
):
    side, flip, _, _ = position()
    places = regions(flip)
    for at, half in zip(places[:5] + places[6:7], (first_kv, second_kv, u1, d1, u2, d2)):
        win[pl.ds(at, HALF), :] = half[...]
    zeros = jnp.zeros((BLK, HD), BF)
    own_cols = pl.ds(pl.multiple_of(side * HD, HD), HD)
    for i in range(GROUP):
        rows = slice(i * BLK, (i + 1) * BLK)
        here = slice((i % 2) * BLK, (i % 2 + 1) * BLK)
        d_blk = jnp.where(side == i // 2, d_own[here, own_cols], d_other[here, :])
        pair = jnp.concatenate(
            [
                jnp.concatenate([q[rows, :], zeros], axis=1),
                jnp.concatenate([zeros, d_blk], axis=1),
            ],
            axis=0,
        )
        pairs[2 * i * BLK : 2 * (i + 1) * BLK, :] = pair
        blocks = []
        for t in near_runs(i):
            blocks += run_scores(links, win[pl.ds(start_of(links, i, t), SPAN * BLK), :], pair, i, t)
        largest = largest_of(blocks)
        terms, total, weighted = exponentials(blocks, largest)
        for n, term in enumerate(terms):
            terms_out[near_rows(i, 0, n), :] = term
            prob_grads_out[near_rows(i, 0, n), :] = blocks[n][1]
        for n, row in enumerate((largest, total, weighted)):
            stats[8 * (3 * i + n) : 8 * (3 * i + n + 1), :] = jnp.broadcast_to(row, (8, BLK))


def far_grads_kernel(
    links, pairs, stats, u1, d1, u2, u3, d2, d3,
    mixed, edges, far_u_out, far_d_out, scales, win,
):
    places = regions(position()[1])
    for at, half in zip(places[2:], (u1, d1, u2, u3, d2, d3)):
        win[pl.ds(at, HALF), :] = half[...]
    edges[...] = jnp.zeros_like(edges)
    scale = HD ** -0.5 * LOG2E
    span = range(GROUP)
    starts = [start_of(links, i, far_run(i)) for i in span]
    pair = [pairs[2 * i * BLK : 2 * (i + 1) * BLK, :] for i in span]
    near = [[stats[8 * (3 * i + n) : 8 * (3 * i + n) + 1, :] for n in range(3)] for i in span]
    blocks = [
        run_scores(links, win[pl.ds(starts[i], SPAN * BLK), :], pair[i], i, far_run(i)) for i in span
    ]
    largest = [jnp.maximum(near[i][0], largest_of(blocks[i])) for i in span]
    found = [exponentials(blocks[i], largest[i]) for i in span]
    parts = []
    for i in span:
        terms, total, weighted = found[i]
        near_scale = jnp.exp2((near[i][0] - largest[i]) * scale)
        inverse = 1.0 / (total + near_scale * near[i][1])
        row_dot = (weighted + near_scale * near[i][2]) * inverse
        for n, row in enumerate((near_scale * inverse, row_dot)):
            scales[8 * (2 * i + n) : 8 * (2 * i + n + 1), :] = jnp.broadcast_to(row, (8, BLK))
        parts.append(
            jnp.concatenate([mix(term * inverse, block[1], row_dot) for term, block in zip(terms, blocks[i])], axis=0)
        )
    for i in span:
        mixed[far_rows(i), :] = parts[i]
        at = starts[i] if i < GROUP // 2 else starts[i] - ROWS
        edges[pl.ds(pl.multiple_of(at, BLK), SPAN * BLK), :] += dot(parts[i], pair[i], ((1,), (0,)))
    factor = side_factor()
    flip = position()[1]
    for target, left in ((far_u_out, flip), (far_d_out, 1 - flip)):
        at = pl.multiple_of((1 - left) * (2 * OWN - HALF), HALF)
        target[...] = (edges[pl.ds(at, HALF), :] * factor).astype(BF)


def near_grads_kernel(
    links, pairs, terms, prob_grads, scales, edges, mixed, first_own, second_own, u_out, d_out, acc
):
    acc[NEAR_LEFT:OWN, :] = edges[NEAR_LEFT:OWN, :]
    acc[OWN:NEAR_RIGHT, :] = jnp.zeros((ROWS, 2 * HD), F32)
    acc[NEAR_RIGHT:FAR_RIGHT, :] = edges[OWN : OWN + ROWS, :]
    for i in range(GROUP):
        pair = pairs[2 * i * BLK : 2 * (i + 1) * BLK, :]
        scale, row_dot = (scales[8 * (2 * i + n) : 8 * (2 * i + n) + 1, :] for n in range(2))
        for index, t in enumerate(near_runs(i)):
            parts = []
            for j in range(SPAN):
                rows = near_rows(i, index, j)
                parts.append(mix(terms[rows, :] * scale, prob_grads[rows, :], row_dot))
                mixed[rows, :] = parts[-1]
            at = pl.ds(start_of(links, i, t), SPAN * BLK)
            acc[at, :] += dot(jnp.concatenate(parts, axis=0), pair, ((1,), (0,)))
    factor = side_factor()
    first, second, u1, d1, u2, _, d2, _ = regions(position()[1])
    first_own[...] = acc[pl.ds(first, HALF), :] * factor
    second_own[...] = acc[pl.ds(second, HALF), :] * factor
    for target, at_first, at_second in ((u_out, d1, d2), (d_out, u1, u2)):
        target[:HALF, :] = (acc[pl.ds(at_first, HALF), :] * factor).astype(BF)
        target[HALF:, :] = (acc[pl.ds(at_second, HALF), :] * factor).astype(BF)


def outputs_kernel(
    links, near_mixed, far_mixed, first_kv, second_kv, u1, d1, u2, u3, d2, d3,
    att_own, att_other, dq_out, win, att,
):
    side, flip, _, _ = position()
    for at, half in zip(regions(flip), (first_kv, second_kv, u1, d1, u2, u3, d2, d3)):
        win[pl.ds(at, HALF), :] = half[...]
    for i in range(GROUP):
        rows = slice(i * BLK, (i + 1) * BLK)
        out = dot(
            far_mixed[far_rows(i), :], win[pl.ds(start_of(links, i, far_run(i)), SPAN * BLK), :], ((0,), (0,))
        )
        for index, t in enumerate(near_runs(i)):
            part = near_mixed[near_rows(i, index, 0).start : near_rows(i, index, SPAN - 1).stop, :]
            out = out + dot(part, win[pl.ds(start_of(links, i, t), SPAN * BLK), :], ((0,), (0,)))
        att[rows, :] = out[BLK:, HD:].astype(BF)
        dq_out[rows, :] = (out[:BLK, :HD] * (HD ** -0.5)).astype(BF)
    att_own[...] = att[pl.ds(pl.multiple_of(side * HALF, HALF), HALF), :]
    att_other[...] = att[pl.ds(pl.multiple_of((1 - side) * HALF, HALF), HALF), :]


def spread(grads, w_mine, side, head, target):
    for step in range(2):
        out = dot(grads, weight_rows(w_mine, head ^ (2 * step), 2 * HD), ((1,), (1,))).astype(BF)
        for group in range(2):
            index = 2 * group + step
            part = jnp.where(side == group, out[:HALF], out[HALF:])
            target[index * HALF : (index + 1) * HALF, :] = part


def spread_send_kernel(first_own, second_own, from_u, from_d, dq, w_mine, send, grads):
    side, flip, _, head = position()
    first = first_own[...] + from_u[HALF:, :].astype(F32) + from_d[:HALF, :].astype(F32)
    second = second_own[...] + from_u[:HALF, :].astype(F32) + from_d[HALF:, :].astype(F32)
    grads[:, :HD] = dq[...]
    grads[:HALF, HD:] = jnp.where(flip == 1, first, second).astype(BF)
    grads[HALF:, HD:] = jnp.where(flip == 1, second, first).astype(BF)
    spread(grads[...], w_mine, side, head ^ 1, send)


def spread_keep_kernel(grads, w_mine, keep):
    side, _, _, head = position()
    spread(grads[...], w_mine, side, head, keep)


def body(features, w_qkv, block_links, d_out, n_ctx, n_head):
    n_group = n_ctx // 2

    def across(value, flip_ctx, flip_head):
        pairs = [
            (c * n_head + h, (c ^ flip_ctx) * n_head + (h ^ flip_head))
            for c in range(n_ctx)
            for h in range(n_head)
        ]
        return lax.ppermute(value, ("ctx", "head"), pairs)

    def chain(value, back):
        pairs = []
        for ctx in range(n_ctx):
            group, side = divmod(ctx, 2)
            for h in range(n_head):
                to = group + (1 if h % 2 == back else -1)
                inside = 0 <= to < n_group
                target = (2 * to + side) * n_head + h if inside else ctx * n_head + (h ^ 1)
                pairs.append((ctx * n_head + h, target))
        return lax.ppermute(value, ("ctx", "head"), pairs)

    f = features
    sx = across(f, 0, 2)
    sy = across(f, 1, 0)
    sd = across(f, 1, 2)
    w = jnp.transpose(w_qkv, (1, 0, 2))

    def call(kernel, name, outs, ins, mebibytes, flops, scratch=()):
        specs = [SMEM if v.dtype == jnp.int32 else VMEM for v in ins]
        if kernel is begin_kernel:
            specs = [pl.BlockSpec(memory_space=pltpu.HBM)] * 2
            ins = [pltpu.with_memory_space_constraint(v, pltpu.HBM) for v in ins]
        return pl.pallas_call(
            kernel,
            name=name,
            out_shape=outs,
            in_specs=specs,
            out_specs=[SMEM if v.dtype == jnp.int32 else VMEM for v in outs],
            scratch_shapes=list(scratch),
            **params(flops, 2 << 20, mebibytes),
        )(*ins)

    def out(rows, cols, kind=BF):
        return jax.ShapeDtypeStruct((rows, cols), kind)

    def held(rows, cols, kind=BF):
        return pltpu.VMEM((rows, cols), kind)

    product = 2 * ROWS * f.shape[1] * 3 * HD
    attention = 2 * GROUP * 9 * BLK * BLK * 2 * HD
    w_mine, fm, total = call(
        begin_kernel,
        "begin",
        [held(w.shape[1], 3 * HD), held(*f.shape), held(HALF, 3 * HD, F32)],
        (f, w),
        4,
        product,
        [pltpu.SemaphoreType.DMA((4,))],
    )
    (pack,) = call(pack_kernel, "pack", [out(4 * HALF, f.shape[1])], (fm, sd, sx, sy), 4, 0)
    other = across(pack, 0, 1)
    (total,) = call(
        project_across_kernel, "project_across", [held(ROWS, 3 * HD, F32)], (pack, total, w_mine), 4, product
    )
    first, second = call(
        project_kv_kernel, "project_kv", [out(HALF, 2 * HD)] * 2, (other, total, w_mine), 4, product
    )

    u1 = chain(first, 0)
    d1 = chain(second, 1)
    u2 = chain(second, 0)
    d2 = chain(first, 1)
    u3 = chain(u1, 0)
    d3 = chain(d1, 1)
    rows, slots = block_links.shape
    link_rows = jnp.pad(block_links.astype(BF), ((0, 16 - rows), (0, HD - slots)))
    (payload,) = call(payload_kernel, "payload", [out(HALF + 16, HD)], (d_out, link_rows, pack), 4, 0)
    d_other = across(payload, 1, 0)
    (q,) = call(project_q_kernel, "project_q", [held(ROWS, HD)], (other, total, w_mine, u1, d1), 4, product)
    other_links = d_other[HALF : HALF + rows, :slots].astype(jnp.int32)
    (links,) = call(
        links_kernel, "links", [pltpu.SMEM((GROUP + 1, slots), jnp.int32)], (block_links, other_links, q), 4, 0
    )
    links = pltpu.with_memory_space_constraint(links, pltpu.SMEM)
    window = pltpu.VMEM((WINDOW * BLK, 2 * HD), BF)
    sums = pltpu.VMEM((WINDOW * BLK, 2 * HD), F32)
    run = SPAN * BLK
    pairs, terms, prob_grads, stats = call(
        near_scores_kernel,
        "near_scores",
        [
            held(GROUP * 2 * BLK, 2 * HD),
            held(GROUP * 2 * run, BLK, F32),
            held(GROUP * 2 * run, BLK, F32),
            held(GROUP * 3 * 8, BLK, F32),
        ],
        (links, q, first, second, u1, d1, u2, d2, d_out, d_other),
        6,
        attention,
        [window],
    )
    far_mixed, edges, far_u_grad, far_d_grad, scales = call(
        far_grads_kernel,
        "far_grads",
        [
            held(GROUP * run, 2 * HD),
            held(2 * OWN, 2 * HD, F32),
            out(HALF, 2 * HD),
            out(HALF, 2 * HD),
            held(GROUP * 2 * 8, BLK, F32),
        ],
        (links, pairs, stats, u1, d1, u2, u3, d2, d3),
        6,
        attention,
        [window],
    )
    near_mixed, first_own, second_own, u_grad, d_grad = call(
        near_grads_kernel,
        "near_grads",
        [held(GROUP * 2 * run, 2 * HD)] + [held(HALF, 2 * HD, F32)] * 2 + [out(ROWS, 2 * HD)] * 2,
        (links, pairs, terms, prob_grads, scales, edges),
        4,
        attention,
        [sums],
    )
    att_own, att_other, dq = call(
        outputs_kernel,
        "outputs",
        [out(HALF, HD), out(HALF, HD), held(ROWS, HD)],
        (links, near_mixed, far_mixed, first, second, u1, d1, u2, u3, d2, d3),
        4,
        attention,
        [window, pltpu.VMEM((ROWS, HD), BF)],
    )

    back_u = chain(far_u_grad, 0)
    back_d = chain(far_d_grad, 1)

    def merge(whole, part, name):
        return call(merge_kernel, name, [out(ROWS, 2 * HD)], (whole, part, dq), 4, 0)[0]

    from_u = chain(merge(u_grad, back_u, "merge_u"), 0)
    from_d = chain(merge(d_grad, back_d, "merge_d"), 1)
    att_back = across(att_other, 1, 0)
    from_u, from_d, att_back = lax.optimization_barrier((from_u, from_d, att_back))
    (attended,) = call(lay_out_kernel, "lay_out", [out(HALF, 2 * HD)], (att_own, att_back), 4, 0)
    send, grads = call(
        spread_send_kernel,
        "spread_send",
        [out(4 * HALF, 2 * HD), held(ROWS, 3 * HD)],
        (first_own, second_own, from_u, from_d, dq, w_mine),
        4,
        product,
    )
    (keep,) = call(spread_keep_kernel, "spread_keep", [held(4 * HALF, 2 * HD)], (grads, w_mine), 4, product)
    arrived = across(send, 0, 1)
    chip = (keep.astype(F32) + arrived.astype(F32)).astype(BF)
    gd = across(chip[3 * HALF :], 1, 2)
    gy = across(chip[2 * HALF : 3 * HALF], 1, 0)
    gx = across(chip[HALF : 2 * HALF], 0, 2)
    grad_features = (
        chip[:HALF].astype(F32) + gd.astype(F32) + gy.astype(F32) + gx.astype(F32)
    ).astype(BF)
    return attended, grad_features


def solution(mesh):
    sizes = dict(mesh.shape)
    return jax.shard_map(
        functools.partial(body, n_ctx=sizes["ctx"], n_head=sizes["head"]),
        mesh=mesh,
        in_specs=(P("ctx", "head"), P(None, None, "head"), P("ctx", None), P("ctx", "head")),
        out_specs=(P("ctx", "head"), P("ctx", "head")),
        check_vma=False,
    )
```

```python
import functools

import jax
import jax.numpy as jnp
from jax import lax
from jax.experimental import pallas as pl
from jax.experimental.pallas import tpu as pltpu
from jax.sharding import PartitionSpec as P

HD = 128
BLK = 128
REACH = 6
SPAN = 3
LOG2E = 1.4426950408889634
DEAD = -1e30
BF = jnp.bfloat16
F32 = jnp.float32

GROUP = 4
ROWS = GROUP * BLK
HALF = ROWS // 2
WINDOW = GROUP + 2 * REACH
NEAR_LEFT = (REACH - GROUP) * BLK
OWN = REACH * BLK
NEAR_RIGHT = OWN + ROWS
FAR_RIGHT = NEAR_RIGHT + ROWS


def params(flops, moved, mebibytes):
    return dict(
        compiler_params=pltpu.CompilerParams(vmem_limit_bytes=mebibytes * 1024 * 1024),
        cost_estimate=pl.CostEstimate(flops=flops, bytes_accessed=moved, transcendentals=0),
    )


VMEM = pl.BlockSpec(memory_space=pltpu.VMEM)
SMEM = pl.BlockSpec(memory_space=pltpu.SMEM)


def dot(a, b, dims):
    return lax.dot_general(a, b, (dims, ((), ())), preferred_element_type=F32)


def position():
    ctx, head = lax.axis_index("ctx"), lax.axis_index("head")
    return ctx % 2, head % 2, ctx // 2 * GROUP, head


def begin_kernel(f, w, w_mine, fm, total, sems):
    side, _, _, head = position()
    copies = [pltpu.make_async_copy(f, fm, sems.at[3])]
    for g in range(3):
        cols = pl.ds(pl.multiple_of(side * HD, HD), HD)
        copies.append(pltpu.make_async_copy(w.at[g, :, cols], w_mine.at[:, pl.ds(g * HD, HD)], sems.at[g]))
    for copy in copies:
        copy.start()
    for copy in copies:
        copy.wait()
    total[...] = dot(fm[...], weight_rows(w_mine, head, fm.shape[1]), ((1,), (0,)))


def weight_rows(w_mine, source, width):
    return w_mine[pl.ds(pl.multiple_of(source * width, width), width), :]


def pack_kernel(one, two, out):
    out[:HALF, :] = one[...]
    out[HALF:, :] = two[...]


def project_rest_kernel(before, early, late, other_early, w_mine, total):
    head = position()[3]
    width = early.shape[1]
    mine, across_x, sibling, across_both = (weight_rows(w_mine, head ^ k, width) for k in (0, 2, 1, 3))
    own = before[...] + dot(late[HALF:, :], across_x, ((1,), (0,)))
    total[:HALF, :] = own + dot(other_early[:HALF, :], sibling, ((1,), (0,)))
    partner = dot(late[:HALF, :], mine, ((1,), (0,))) + dot(early[HALF:, :], across_x, ((1,), (0,)))
    total[HALF:, :] = partner + dot(other_early[HALF:, :], across_both, ((1,), (0,)))


def last_product(head, other_late, w_mine, cols, group):
    width = other_late.shape[1]
    rows = pl.ds(pl.multiple_of((head ^ (3 if group == 0 else 1)) * width, width), width)
    piece = other_late[HALF:, :] if group == 0 else other_late[:HALF, :]
    return dot(piece, w_mine[rows, cols], ((1,), (0,)))


def project_kv_kernel(other_late, before, w_mine, first_out, second_out):
    side, flip, _, head = position()
    own, partner = (
        (before[g * HALF : (g + 1) * HALF, HD:] + last_product(head, other_late, w_mine, slice(HD, 3 * HD), g)).astype(BF)
        for g in range(2)
    )
    near_first = side ^ (1 - flip) == 0
    first_out[...] = jnp.where(near_first, own, partner)
    second_out[...] = jnp.where(near_first, partner, own)


def merge_kernel(whole, part, dq, out):
    del dq
    out[:HALF, :] = (whole[:HALF, :].astype(F32) + part[...].astype(F32)).astype(BF)
    out[HALF:, :] = whole[HALF:, :]


def lay_out_kernel(own, other, out):
    side = position()[0]
    for half in range(2):
        cols = slice(half * HD, (half + 1) * HD)
        out[:, cols] = jnp.where(side == half, own[...], other[...])


def project_q_kernel(other_late, before, w_mine, u1, d1, q_out):
    del u1, d1
    side, _, _, head = position()
    for g in range(2):
        part = before[g * HALF : (g + 1) * HALF, :HD] + last_product(head, other_late, w_mine, slice(0, HD), g)
        q_out[pl.ds(pl.multiple_of((side ^ g) * HALF, HALF), HALF), :] = part.astype(BF)


def payload_kernel(d_own, link_rows, late, payload):
    del late
    side = position()[0]
    payload[:HALF, :] = jnp.where(side == 0, d_own[:, HD:], d_own[:, :HD])
    payload[HALF:, :] = link_rows[...]


def links_kernel(own, other, q, links):
    del q
    side, _, first, _ = position()
    for i in range(GROUP):
        for k in range(3 * SPAN):
            links[i, k] = jnp.where(side == i // 2, own[i % 2, k], other[i % 2, k])
        for t in (1, 2):
            base = jnp.int32(-(1 << 20))
            for j in range(SPAN):
                entry = links[i, SPAN * t + j]
                base = jnp.maximum(base, jnp.where(entry >= 0, entry - j, -(1 << 20)))
            base = jnp.where(base > -(1 << 19), base - first + REACH, i + 1 if t == 1 else i + REACH + SPAN)
            lowest = i if t == 1 else i + REACH + SPAN - 1
            links[GROUP, 2 * i + t - 1] = jnp.clip(base, lowest, lowest + 2) * BLK


def regions(flip):
    left_lo, left_hi = NEAR_LEFT, NEAR_LEFT + HALF
    right_lo, right_hi = NEAR_RIGHT, NEAR_RIGHT + HALF
    pick = lambda plain, flipped: pl.multiple_of((1 - flip) * plain + flip * flipped, HALF)
    return (
        pick(OWN + HALF, OWN),
        pick(OWN, OWN + HALF),
        pick(left_hi, right_lo),
        pick(right_lo, left_hi),
        pick(left_lo, right_hi),
        pick(0, FAR_RIGHT),
        pick(right_hi, left_lo),
        pick(FAR_RIGHT, 0),
    )


def start_of(links, i, t):
    if t == 0:
        return (REACH + i - 1) * BLK
    return pl.multiple_of(links[GROUP, 2 * i + t - 1], BLK)


def far_run(i):
    return 1 if i < GROUP // 2 else 2


def near_runs(i):
    return tuple(t for t in range(3) if t != far_run(i))


def near_rows(i, index, j):
    first = ((2 * i + index) * SPAN + j) * BLK
    return slice(first, first + BLK)


def far_rows(i):
    return slice(i * SPAN * BLK, (i + 1) * SPAN * BLK)


def run_scores(links, rows, pair, i, t):
    product = dot(rows, pair, ((1,), (1,)))
    blocks = []
    for j in range(SPAN):
        block = product[j * BLK : (j + 1) * BLK]
        bias = jnp.where(links[i, SPAN * t + j] >= 0, 0.0, DEAD).astype(F32)
        blocks.append((block[:, :BLK], block[:, BLK:], bias))
    return blocks


def fold(block):
    return block.reshape(BLK // 8, 8, BLK)


def largest_of(blocks):
    best = None
    for score, _, bias in blocks:
        peak = jnp.max(fold(score), axis=0) + bias
        best = peak if best is None else jnp.maximum(best, peak)
    return jnp.max(best, axis=0, keepdims=True)


def exponentials(blocks, largest):
    terms = []
    total = jnp.zeros((8, BLK), F32)
    weighted = jnp.zeros((8, BLK), F32)
    for score, prob_grad, bias in blocks:
        term = jnp.exp2((score - (largest - bias)) * (HD ** -0.5 * LOG2E))
        terms.append(term)
        total = total + jnp.sum(fold(term), axis=0)
        weighted = weighted + jnp.sum(fold(term * prob_grad), axis=0)
    return terms, jnp.sum(total, axis=0, keepdims=True), jnp.sum(weighted, axis=0, keepdims=True)


def mix(share, prob_grad, row_dot):
    grad = share * (prob_grad - row_dot)
    return jnp.concatenate([grad.astype(BF), share.astype(BF)], axis=1)


def side_factor():
    scale = HD ** -0.5
    return jnp.where(lax.broadcasted_iota(jnp.int32, (1, 2 * HD), 1) < HD, scale, 1.0).astype(F32)


def near_scores_kernel(
    links, q, first_kv, second_kv, u1, d1, u2, d2, d_own, d_other,
    pairs, terms_out, prob_grads_out, stats, win,
):
    side, flip, _, _ = position()
    places = regions(flip)
    for at, half in zip(places[:5] + places[6:7], (first_kv, second_kv, u1, d1, u2, d2)):
        win[pl.ds(at, HALF), :] = half[...]
    zeros = jnp.zeros((BLK, HD), BF)
    own_cols = pl.ds(pl.multiple_of(side * HD, HD), HD)
    for i in range(GROUP):
        rows = slice(i * BLK, (i + 1) * BLK)
        here = slice((i % 2) * BLK, (i % 2 + 1) * BLK)
        d_blk = jnp.where(side == i // 2, d_own[here, own_cols], d_other[here, :])
        pair = jnp.concatenate(
            [
                jnp.concatenate([q[rows, :], zeros], axis=1),
                jnp.concatenate([zeros, d_blk], axis=1),
            ],
            axis=0,
        )
        pairs[2 * i * BLK : 2 * (i + 1) * BLK, :] = pair
        blocks = []
        for t in near_runs(i):
            blocks += run_scores(links, win[pl.ds(start_of(links, i, t), SPAN * BLK), :], pair, i, t)
        largest = largest_of(blocks)
        terms, total, weighted = exponentials(blocks, largest)
        for n, term in enumerate(terms):
            terms_out[near_rows(i, 0, n), :] = term
            prob_grads_out[near_rows(i, 0, n), :] = blocks[n][1]
        for n, row in enumerate((largest, total, weighted)):
            stats[8 * (3 * i + n) : 8 * (3 * i + n + 1), :] = jnp.broadcast_to(row, (8, BLK))


def far_grads_kernel(
    links, pairs, stats, u1, d1, u2, u3, d2, d3,
    mixed, edges, far_u_out, far_d_out, scales, win,
):
    places = regions(position()[1])
    for at, half in zip(places[2:], (u1, d1, u2, u3, d2, d3)):
        win[pl.ds(at, HALF), :] = half[...]
    edges[...] = jnp.zeros_like(edges)
    scale = HD ** -0.5 * LOG2E
    span = range(GROUP)
    starts = [start_of(links, i, far_run(i)) for i in span]
    pair = [pairs[2 * i * BLK : 2 * (i + 1) * BLK, :] for i in span]
    near = [[stats[8 * (3 * i + n) : 8 * (3 * i + n) + 1, :] for n in range(3)] for i in span]
    blocks = [
        run_scores(links, win[pl.ds(starts[i], SPAN * BLK), :], pair[i], i, far_run(i)) for i in span
    ]
    largest = [jnp.maximum(near[i][0], largest_of(blocks[i])) for i in span]
    found = [exponentials(blocks[i], largest[i]) for i in span]
    parts = []
    for i in span:
        terms, total, weighted = found[i]
        near_scale = jnp.exp2((near[i][0] - largest[i]) * scale)
        inverse = 1.0 / (total + near_scale * near[i][1])
        row_dot = (weighted + near_scale * near[i][2]) * inverse
        for n, row in enumerate((near_scale * inverse, row_dot)):
            scales[8 * (2 * i + n) : 8 * (2 * i + n + 1), :] = jnp.broadcast_to(row, (8, BLK))
        parts.append(
            jnp.concatenate([mix(term * inverse, block[1], row_dot) for term, block in zip(terms, blocks[i])], axis=0)
        )
    for i in span:
        mixed[far_rows(i), :] = parts[i]
        at = starts[i] if i < GROUP // 2 else starts[i] - ROWS
        edges[pl.ds(pl.multiple_of(at, BLK), SPAN * BLK), :] += dot(parts[i], pair[i], ((1,), (0,)))
    factor = side_factor()
    flip = position()[1]
    for target, left in ((far_u_out, flip), (far_d_out, 1 - flip)):
        at = pl.multiple_of((1 - left) * (2 * OWN - HALF), HALF)
        target[...] = (edges[pl.ds(at, HALF), :] * factor).astype(BF)


def near_grads_kernel(
    links, pairs, terms, prob_grads, scales, edges, mixed, first_own, second_own, u_out, d_out, acc
):
    acc[NEAR_LEFT:OWN, :] = edges[NEAR_LEFT:OWN, :]
    acc[OWN:NEAR_RIGHT, :] = jnp.zeros((ROWS, 2 * HD), F32)
    acc[NEAR_RIGHT:FAR_RIGHT, :] = edges[OWN : OWN + ROWS, :]
    for i in range(GROUP):
        pair = pairs[2 * i * BLK : 2 * (i + 1) * BLK, :]
        scale, row_dot = (scales[8 * (2 * i + n) : 8 * (2 * i + n) + 1, :] for n in range(2))
        for index, t in enumerate(near_runs(i)):
            parts = []
            for j in range(SPAN):
                rows = near_rows(i, index, j)
                parts.append(mix(terms[rows, :] * scale, prob_grads[rows, :], row_dot))
                mixed[rows, :] = parts[-1]
            at = pl.ds(start_of(links, i, t), SPAN * BLK)
            acc[at, :] += dot(jnp.concatenate(parts, axis=0), pair, ((1,), (0,)))
    factor = side_factor()
    first, second, u1, d1, u2, _, d2, _ = regions(position()[1])
    first_own[...] = acc[pl.ds(first, HALF), :] * factor
    second_own[...] = acc[pl.ds(second, HALF), :] * factor
    for target, at_first, at_second in ((u_out, d1, d2), (d_out, u1, u2)):
        target[:HALF, :] = (acc[pl.ds(at_first, HALF), :] * factor).astype(BF)
        target[HALF:, :] = (acc[pl.ds(at_second, HALF), :] * factor).astype(BF)


def outputs_kernel(
    links, near_mixed, far_mixed, first_kv, second_kv, u1, d1, u2, u3, d2, d3,
    att_own, att_other, dq_out, win, att,
):
    side, flip, _, _ = position()
    for at, half in zip(regions(flip), (first_kv, second_kv, u1, d1, u2, u3, d2, d3)):
        win[pl.ds(at, HALF), :] = half[...]
    for i in range(GROUP):
        rows = slice(i * BLK, (i + 1) * BLK)
        out = dot(
            far_mixed[far_rows(i), :], win[pl.ds(start_of(links, i, far_run(i)), SPAN * BLK), :], ((0,), (0,))
        )
        for index, t in enumerate(near_runs(i)):
            part = near_mixed[near_rows(i, index, 0).start : near_rows(i, index, SPAN - 1).stop, :]
            out = out + dot(part, win[pl.ds(start_of(links, i, t), SPAN * BLK), :], ((0,), (0,)))
        att[rows, :] = out[BLK:, HD:].astype(BF)
        dq_out[rows, :] = (out[:BLK, :HD] * (HD ** -0.5)).astype(BF)
    att_own[...] = att[pl.ds(pl.multiple_of(side * HALF, HALF), HALF), :]
    att_other[...] = att[pl.ds(pl.multiple_of((1 - side) * HALF, HALF), HALF), :]


def spread(grads, w_mine, side, head, target):
    for step in range(2):
        out = dot(grads, weight_rows(w_mine, head ^ (2 * step), 2 * HD), ((1,), (1,))).astype(BF)
        for group in range(2):
            index = 2 * group + step
            part = jnp.where(side == group, out[:HALF], out[HALF:])
            target[index * HALF : (index + 1) * HALF, :] = part


def spread_send_kernel(first_own, second_own, from_u, from_d, dq, w_mine, send, grads):
    side, flip, _, head = position()
    first = first_own[...] + from_u[HALF:, :].astype(F32) + from_d[:HALF, :].astype(F32)
    second = second_own[...] + from_u[:HALF, :].astype(F32) + from_d[HALF:, :].astype(F32)
    grads[:, :HD] = dq[...]
    grads[:HALF, HD:] = jnp.where(flip == 1, first, second).astype(BF)
    grads[HALF:, HD:] = jnp.where(flip == 1, second, first).astype(BF)
    spread(grads[...], w_mine, side, head ^ 1, send)


def spread_keep_kernel(grads, w_mine, keep):
    side, _, _, head = position()
    spread(grads[...], w_mine, side, head, keep)


def body(features, w_qkv, block_links, d_out, n_ctx, n_head):
    n_group = n_ctx // 2

    def across(value, flip_ctx, flip_head):
        pairs = [
            (c * n_head + h, (c ^ flip_ctx) * n_head + (h ^ flip_head))
            for c in range(n_ctx)
            for h in range(n_head)
        ]
        return lax.ppermute(value, ("ctx", "head"), pairs)

    def chain(value, back):
        pairs = []
        for ctx in range(n_ctx):
            group, side = divmod(ctx, 2)
            for h in range(n_head):
                to = group + (1 if h % 2 == back else -1)
                inside = 0 <= to < n_group
                target = (2 * to + side) * n_head + h if inside else ctx * n_head + (h ^ 1)
                pairs.append((ctx * n_head + h, target))
        return lax.ppermute(value, ("ctx", "head"), pairs)

    f = features
    sx = across(f, 0, 2)
    sy = across(f, 1, 0)
    sd = across(f, 1, 2)
    w = jnp.transpose(w_qkv, (1, 0, 2))

    def call(kernel, name, outs, ins, mebibytes, flops, scratch=()):
        specs = [SMEM if v.dtype == jnp.int32 else VMEM for v in ins]
        if kernel is begin_kernel:
            specs = [pl.BlockSpec(memory_space=pltpu.HBM)] * 2
            ins = [pltpu.with_memory_space_constraint(v, pltpu.HBM) for v in ins]
        return pl.pallas_call(
            kernel,
            name=name,
            out_shape=outs,
            in_specs=specs,
            out_specs=[SMEM if v.dtype == jnp.int32 else VMEM for v in outs],
            scratch_shapes=list(scratch),
            **params(flops, 2 << 20, mebibytes),
        )(*ins)

    def out(rows, cols, kind=BF):
        return jax.ShapeDtypeStruct((rows, cols), kind)

    def held(rows, cols, kind=BF):
        return pltpu.VMEM((rows, cols), kind)

    product = 2 * ROWS * f.shape[1] * 3 * HD
    attention = 2 * GROUP * 9 * BLK * BLK * 2 * HD
    w_mine, fm, total = call(
        begin_kernel,
        "begin",
        [held(w.shape[1], 3 * HD), held(*f.shape), held(HALF, 3 * HD, F32)],
        (f, w),
        4,
        product,
        [pltpu.SemaphoreType.DMA((4,))],
    )
    (early,) = call(pack_kernel, "pack_early", [out(ROWS, f.shape[1])], (fm, sd), 4, 0)
    other_early = across(early, 0, 1)
    (late,) = call(pack_kernel, "pack_late", [out(ROWS, f.shape[1])], (sy, sx), 4, 0)
    other_late = across(late, 0, 1)
    (total,) = call(
        project_rest_kernel,
        "project_rest",
        [held(ROWS, 3 * HD, F32)],
        (total, early, late, other_early, w_mine),
        4,
        product,
    )
    first, second = call(
        project_kv_kernel, "project_kv", [out(HALF, 2 * HD)] * 2, (other_late, total, w_mine), 4, product
    )

    u1 = chain(first, 0)
    d1 = chain(second, 1)
    u2 = chain(second, 0)
    d2 = chain(first, 1)
    u3 = chain(u1, 0)
    d3 = chain(d1, 1)
    rows, slots = block_links.shape
    link_rows = jnp.pad(block_links.astype(BF), ((0, 16 - rows), (0, HD - slots)))
    (payload,) = call(payload_kernel, "payload", [out(HALF + 16, HD)], (d_out, link_rows, late), 4, 0)
    d_other = across(payload, 1, 0)
    (q,) = call(project_q_kernel, "project_q", [held(ROWS, HD)], (other_late, total, w_mine, u1, d1), 4, product)
    other_links = d_other[HALF : HALF + rows, :slots].astype(jnp.int32)
    (links,) = call(
        links_kernel, "links", [pltpu.SMEM((GROUP + 1, slots), jnp.int32)], (block_links, other_links, q), 4, 0
    )
    links = pltpu.with_memory_space_constraint(links, pltpu.SMEM)
    window = pltpu.VMEM((WINDOW * BLK, 2 * HD), BF)
    sums = pltpu.VMEM((WINDOW * BLK, 2 * HD), F32)
    run = SPAN * BLK
    pairs, terms, prob_grads, stats = call(
        near_scores_kernel,
        "near_scores",
        [
            held(GROUP * 2 * BLK, 2 * HD),
            held(GROUP * 2 * run, BLK, F32),
            held(GROUP * 2 * run, BLK, F32),
            held(GROUP * 3 * 8, BLK, F32),
        ],
        (links, q, first, second, u1, d1, u2, d2, d_out, d_other),
        6,
        attention,
        [window],
    )
    far_mixed, edges, far_u_grad, far_d_grad, scales = call(
        far_grads_kernel,
        "far_grads",
        [
            held(GROUP * run, 2 * HD),
            held(2 * OWN, 2 * HD, F32),
            out(HALF, 2 * HD),
            out(HALF, 2 * HD),
            held(GROUP * 2 * 8, BLK, F32),
        ],
        (links, pairs, stats, u1, d1, u2, u3, d2, d3),
        6,
        attention,
        [window],
    )
    near_mixed, first_own, second_own, u_grad, d_grad = call(
        near_grads_kernel,
        "near_grads",
        [held(GROUP * 2 * run, 2 * HD)] + [held(HALF, 2 * HD, F32)] * 2 + [out(ROWS, 2 * HD)] * 2,
        (links, pairs, terms, prob_grads, scales, edges),
        4,
        attention,
        [sums],
    )
    att_own, att_other, dq = call(
        outputs_kernel,
        "outputs",
        [out(HALF, HD), out(HALF, HD), held(ROWS, HD)],
        (links, near_mixed, far_mixed, first, second, u1, d1, u2, u3, d2, d3),
        4,
        attention,
        [window, pltpu.VMEM((ROWS, HD), BF)],
    )

    back_u = chain(far_u_grad, 0)
    back_d = chain(far_d_grad, 1)

    def merge(whole, part, name):
        return call(merge_kernel, name, [out(ROWS, 2 * HD)], (whole, part, dq), 4, 0)[0]

    from_u = chain(merge(u_grad, back_u, "merge_u"), 0)
    from_d = chain(merge(d_grad, back_d, "merge_d"), 1)
    att_back = across(att_other, 1, 0)
    from_u, from_d, att_back = lax.optimization_barrier((from_u, from_d, att_back))
    (attended,) = call(lay_out_kernel, "lay_out", [out(HALF, 2 * HD)], (att_own, att_back), 4, 0)
    send, grads = call(
        spread_send_kernel,
        "spread_send",
        [out(4 * HALF, 2 * HD), held(ROWS, 3 * HD)],
        (first_own, second_own, from_u, from_d, dq, w_mine),
        4,
        product,
    )
    (keep,) = call(spread_keep_kernel, "spread_keep", [held(4 * HALF, 2 * HD)], (grads, w_mine), 4, product)
    arrived = across(send, 0, 1)
    chip = (keep.astype(F32) + arrived.astype(F32)).astype(BF)
    gd = across(chip[3 * HALF :], 1, 2)
    gy = across(chip[2 * HALF : 3 * HALF], 1, 0)
    gx = across(chip[HALF : 2 * HALF], 0, 2)
    grad_features = (
        chip[:HALF].astype(F32) + gd.astype(F32) + gy.astype(F32) + gx.astype(F32)
    ).astype(BF)
    return attended, grad_features


def solution(mesh):
    sizes = dict(mesh.shape)
    return jax.shard_map(
        functools.partial(body, n_ctx=sizes["ctx"], n_head=sizes["head"]),
        mesh=mesh,
        in_specs=(P("ctx", "head"), P(None, None, "head"), P("ctx", None), P("ctx", "head")),
        out_specs=(P("ctx", "head"), P("ctx", "head")),
        check_vma=False,
    )
```

```python
import functools

import jax
import jax.numpy as jnp
from jax import lax
from jax.experimental import pallas as pl
from jax.experimental.pallas import tpu as pltpu
from jax.sharding import PartitionSpec as P

HD = 128
BLK = 128
REACH = 6
SPAN = 3
LOG2E = 1.4426950408889634
DEAD = -1e30
BF = jnp.bfloat16
F32 = jnp.float32

GROUP = 4
ROWS = GROUP * BLK
HALF = ROWS // 2
WINDOW = GROUP + 2 * REACH
NEAR_LEFT = (REACH - GROUP) * BLK
OWN = REACH * BLK
NEAR_RIGHT = OWN + ROWS
FAR_RIGHT = NEAR_RIGHT + ROWS


def params(flops, moved, mebibytes):
    return dict(
        compiler_params=pltpu.CompilerParams(vmem_limit_bytes=mebibytes * 1024 * 1024),
        cost_estimate=pl.CostEstimate(flops=flops, bytes_accessed=moved, transcendentals=0),
    )


VMEM = pl.BlockSpec(memory_space=pltpu.VMEM)
SMEM = pl.BlockSpec(memory_space=pltpu.SMEM)


def dot(a, b, dims):
    return lax.dot_general(a, b, (dims, ((), ())), preferred_element_type=F32)


def position():
    ctx, head = lax.axis_index("ctx"), lax.axis_index("head")
    return ctx % 2, head % 2, ctx // 2 * GROUP, head


def begin_kernel(f, w, w_mine, fm, total, sems):
    side, _, _, head = position()
    copies = [pltpu.make_async_copy(f, fm, sems.at[3])]
    for g in range(3):
        cols = pl.ds(pl.multiple_of(side * HD, HD), HD)
        copies.append(pltpu.make_async_copy(w.at[g, :, cols], w_mine.at[:, pl.ds(g * HD, HD)], sems.at[g]))
    for copy in copies:
        copy.start()
    for copy in copies:
        copy.wait()
    total[...] = dot(fm[...], weight_rows(w_mine, head, fm.shape[1]), ((1,), (0,)))


def weight_rows(w_mine, source, width):
    return w_mine[pl.ds(pl.multiple_of(source * width, width), width), :]


def pack_kernel(one, two, out):
    out[:HALF, :] = one[...]
    out[HALF:, :] = two[...]


def project_rest_kernel(before, early, late, other_early, w_mine, total):
    head = position()[3]
    width = early.shape[1]
    mine, across_x, sibling, across_both = (weight_rows(w_mine, head ^ k, width) for k in (0, 2, 1, 3))
    own = before[...] + dot(late[HALF:, :], across_x, ((1,), (0,)))
    total[:HALF, :] = own + dot(other_early[:HALF, :], sibling, ((1,), (0,)))
    partner = dot(late[:HALF, :], mine, ((1,), (0,))) + dot(early[HALF:, :], across_x, ((1,), (0,)))
    total[HALF:, :] = partner + dot(other_early[HALF:, :], across_both, ((1,), (0,)))


def last_product(head, other_late, w_mine, cols, group):
    width = other_late.shape[1]
    rows = pl.ds(pl.multiple_of((head ^ (3 if group == 0 else 1)) * width, width), width)
    piece = other_late[HALF:, :] if group == 0 else other_late[:HALF, :]
    return dot(piece, w_mine[rows, cols], ((1,), (0,)))


def project_kv_kernel(other_late, before, w_mine, first_out, second_out):
    side, flip, _, head = position()
    own, partner = (
        (before[g * HALF : (g + 1) * HALF, HD:] + last_product(head, other_late, w_mine, slice(HD, 3 * HD), g)).astype(BF)
        for g in range(2)
    )
    near_first = side ^ (1 - flip) == 0
    first_out[...] = jnp.where(near_first, own, partner)
    second_out[...] = jnp.where(near_first, partner, own)


def merge_kernel(one, two, dq, out):
    del dq
    out[...] = (one[...].astype(F32) + two[...].astype(F32)).astype(BF)


def gather_kernel(first_own, second_own, d, u, first_out, second_out):
    first_out[...] = first_own[...] + u[...].astype(F32)
    second_out[...] = second_own[...] + d[...].astype(F32)


def chip_sum_kernel(keep, arrived, att_other, mine, to_x, to_y, to_d):
    for index, target in enumerate((mine, to_x, to_y, to_d)):
        rows = slice(index * HALF, (index + 1) * HALF)
        target[:HALF, :] = (keep[rows, :].astype(F32) + arrived[rows, :].astype(F32)).astype(BF)
    for half in range(2):
        to_y[HALF:, half * HD : (half + 1) * HD] = att_other[half * BLK : (half + 1) * BLK, :]


def finish_kernel(mine, gd, gx, from_y, att_own, attended, grad_features):
    total = mine[...].astype(F32) + gd[...].astype(F32) + gx[...].astype(F32) + from_y[:HALF, :].astype(F32)
    grad_features[...] = total.astype(BF)
    side = position()[0]
    att_other = jnp.concatenate([from_y[HALF:, :HD], from_y[HALF:, HD:]], axis=0)
    for half in range(2):
        cols = slice(half * HD, (half + 1) * HD)
        attended[:, cols] = jnp.where(side == half, att_own[...], att_other)


def project_q_kernel(other_late, before, w_mine, u1, d1, q_out):
    del u1, d1
    side, _, _, head = position()
    for g in range(2):
        part = before[g * HALF : (g + 1) * HALF, :HD] + last_product(head, other_late, w_mine, slice(0, HD), g)
        q_out[pl.ds(pl.multiple_of((side ^ g) * HALF, HALF), HALF), :] = part.astype(BF)


def payload_kernel(d_own, link_rows, late, payload):
    del late
    side = position()[0]
    payload[:HALF, :] = jnp.where(side == 0, d_own[:, HD:], d_own[:, :HD])
    payload[HALF:, :] = link_rows[...]


def links_kernel(own, other, q, links):
    del q
    side, _, first, _ = position()
    for i in range(GROUP):
        for k in range(3 * SPAN):
            links[i, k] = jnp.where(side == i // 2, own[i % 2, k], other[i % 2, k])
        for t in (1, 2):
            base = jnp.int32(-(1 << 20))
            for j in range(SPAN):
                entry = links[i, SPAN * t + j]
                base = jnp.maximum(base, jnp.where(entry >= 0, entry - j, -(1 << 20)))
            base = jnp.where(base > -(1 << 19), base - first + REACH, i + 1 if t == 1 else i + REACH + SPAN)
            lowest = i if t == 1 else i + REACH + SPAN - 1
            links[GROUP, 2 * i + t - 1] = jnp.clip(base, lowest, lowest + 2) * BLK


def regions(flip):
    left_lo, left_hi = NEAR_LEFT, NEAR_LEFT + HALF
    right_lo, right_hi = NEAR_RIGHT, NEAR_RIGHT + HALF
    pick = lambda plain, flipped: pl.multiple_of((1 - flip) * plain + flip * flipped, HALF)
    return (
        pick(OWN + HALF, OWN),
        pick(OWN, OWN + HALF),
        pick(left_hi, right_lo),
        pick(right_lo, left_hi),
        pick(left_lo, right_hi),
        pick(0, FAR_RIGHT),
        pick(right_hi, left_lo),
        pick(FAR_RIGHT, 0),
    )


def start_of(links, i, t):
    if t == 0:
        return (REACH + i - 1) * BLK
    return pl.multiple_of(links[GROUP, 2 * i + t - 1], BLK)


def far_run(i):
    return 1 if i < GROUP // 2 else 2


def near_runs(i):
    return tuple(t for t in range(3) if t != far_run(i))


def near_rows(i, index, j):
    first = ((2 * i + index) * SPAN + j) * BLK
    return slice(first, first + BLK)


def far_rows(i):
    return slice(i * SPAN * BLK, (i + 1) * SPAN * BLK)


def run_scores(links, rows, pair, i, t):
    product = dot(rows, pair, ((1,), (1,)))
    blocks = []
    for j in range(SPAN):
        block = product[j * BLK : (j + 1) * BLK]
        bias = jnp.where(links[i, SPAN * t + j] >= 0, 0.0, DEAD).astype(F32)
        blocks.append((block[:, :BLK], block[:, BLK:], bias))
    return blocks


def fold(block):
    return block.reshape(BLK // 8, 8, BLK)


def largest_of(blocks):
    best = None
    for score, _, bias in blocks:
        peak = jnp.max(fold(score), axis=0) + bias
        best = peak if best is None else jnp.maximum(best, peak)
    return jnp.max(best, axis=0, keepdims=True)


def exponentials(blocks, largest):
    terms = []
    total = jnp.zeros((8, BLK), F32)
    weighted = jnp.zeros((8, BLK), F32)
    for score, prob_grad, bias in blocks:
        term = jnp.exp2((score - (largest - bias)) * (HD ** -0.5 * LOG2E))
        terms.append(term)
        total = total + jnp.sum(fold(term), axis=0)
        weighted = weighted + jnp.sum(fold(term * prob_grad), axis=0)
    return terms, jnp.sum(total, axis=0, keepdims=True), jnp.sum(weighted, axis=0, keepdims=True)


def mix(share, prob_grad, row_dot):
    grad = share * (prob_grad - row_dot)
    return jnp.concatenate([grad.astype(BF), share.astype(BF)], axis=1)


def side_factor():
    scale = HD ** -0.5
    return jnp.where(lax.broadcasted_iota(jnp.int32, (1, 2 * HD), 1) < HD, scale, 1.0).astype(F32)


def near_scores_kernel(
    links, q, first_kv, second_kv, u1, d1, u2, d2, d_own, d_other,
    pairs, terms_out, prob_grads_out, stats, win,
):
    side, flip, _, _ = position()
    places = regions(flip)
    for at, half in zip(places[:5] + places[6:7], (first_kv, second_kv, u1, d1, u2, d2)):
        win[pl.ds(at, HALF), :] = half[...]
    zeros = jnp.zeros((BLK, HD), BF)
    own_cols = pl.ds(pl.multiple_of(side * HD, HD), HD)
    for i in range(GROUP):
        rows = slice(i * BLK, (i + 1) * BLK)
        here = slice((i % 2) * BLK, (i % 2 + 1) * BLK)
        d_blk = jnp.where(side == i // 2, d_own[here, own_cols], d_other[here, :])
        pair = jnp.concatenate(
            [
                jnp.concatenate([q[rows, :], zeros], axis=1),
                jnp.concatenate([zeros, d_blk], axis=1),
            ],
            axis=0,
        )
        pairs[2 * i * BLK : 2 * (i + 1) * BLK, :] = pair
        blocks = []
        for t in near_runs(i):
            blocks += run_scores(links, win[pl.ds(start_of(links, i, t), SPAN * BLK), :], pair, i, t)
        largest = largest_of(blocks)
        terms, total, weighted = exponentials(blocks, largest)
        for n, term in enumerate(terms):
            terms_out[near_rows(i, 0, n), :] = term
            prob_grads_out[near_rows(i, 0, n), :] = blocks[n][1]
        for n, row in enumerate((largest, total, weighted)):
            stats[8 * (3 * i + n) : 8 * (3 * i + n + 1), :] = jnp.broadcast_to(row, (8, BLK))


def far_grads_kernel(
    links, pairs, stats, u1, d1, u2, u3, d2, d3,
    mixed, edges, far_u_out, far_d_out, scales, win,
):
    places = regions(position()[1])
    for at, half in zip(places[2:], (u1, d1, u2, u3, d2, d3)):
        win[pl.ds(at, HALF), :] = half[...]
    edges[...] = jnp.zeros_like(edges)
    scale = HD ** -0.5 * LOG2E
    span = range(GROUP)
    starts = [start_of(links, i, far_run(i)) for i in span]
    pair = [pairs[2 * i * BLK : 2 * (i + 1) * BLK, :] for i in span]
    near = [[stats[8 * (3 * i + n) : 8 * (3 * i + n) + 1, :] for n in range(3)] for i in span]
    blocks = [
        run_scores(links, win[pl.ds(starts[i], SPAN * BLK), :], pair[i], i, far_run(i)) for i in span
    ]
    largest = [jnp.maximum(near[i][0], largest_of(blocks[i])) for i in span]
    found = [exponentials(blocks[i], largest[i]) for i in span]
    parts = []
    for i in span:
        terms, total, weighted = found[i]
        near_scale = jnp.exp2((near[i][0] - largest[i]) * scale)
        inverse = 1.0 / (total + near_scale * near[i][1])
        row_dot = (weighted + near_scale * near[i][2]) * inverse
        for n, row in enumerate((near_scale * inverse, row_dot)):
            scales[8 * (2 * i + n) : 8 * (2 * i + n + 1), :] = jnp.broadcast_to(row, (8, BLK))
        parts.append(
            jnp.concatenate([mix(term * inverse, block[1], row_dot) for term, block in zip(terms, blocks[i])], axis=0)
        )
    for i in span:
        mixed[far_rows(i), :] = parts[i]
        at = starts[i] if i < GROUP // 2 else starts[i] - ROWS
        edges[pl.ds(pl.multiple_of(at, BLK), SPAN * BLK), :] += dot(parts[i], pair[i], ((1,), (0,)))
    factor = side_factor()
    flip = position()[1]
    for target, left in ((far_u_out, flip), (far_d_out, 1 - flip)):
        at = pl.multiple_of((1 - left) * (2 * OWN - HALF), HALF)
        target[...] = (edges[pl.ds(at, HALF), :] * factor).astype(BF)


def near_grads_kernel(
    links, pairs, terms, prob_grads, scales, edges, mixed, first_own, second_own,
    u2_out, d2_out, u3_out, d3_out, acc,
):
    acc[NEAR_LEFT:OWN, :] = edges[NEAR_LEFT:OWN, :]
    acc[OWN:NEAR_RIGHT, :] = jnp.zeros((ROWS, 2 * HD), F32)
    acc[NEAR_RIGHT:FAR_RIGHT, :] = edges[OWN : OWN + ROWS, :]
    for i in range(GROUP):
        pair = pairs[2 * i * BLK : 2 * (i + 1) * BLK, :]
        scale, row_dot = (scales[8 * (2 * i + n) : 8 * (2 * i + n) + 1, :] for n in range(2))
        for index, t in enumerate(near_runs(i)):
            parts = []
            for j in range(SPAN):
                rows = near_rows(i, index, j)
                parts.append(mix(terms[rows, :] * scale, prob_grads[rows, :], row_dot))
                mixed[rows, :] = parts[-1]
            at = pl.ds(start_of(links, i, t), SPAN * BLK)
            acc[at, :] += dot(jnp.concatenate(parts, axis=0), pair, ((1,), (0,)))
    factor = side_factor()
    first, second, u1, d1, u2, _, d2, _ = regions(position()[1])
    first_own[...] = acc[pl.ds(first, HALF), :] * factor
    second_own[...] = acc[pl.ds(second, HALF), :] * factor
    for target, at in ((u2_out, d2), (d2_out, u2), (u3_out, d1), (d3_out, u1)):
        target[...] = (acc[pl.ds(at, HALF), :] * factor).astype(BF)


def outputs_kernel(
    links, near_mixed, far_mixed, first_kv, second_kv, u1, d1, u2, u3, d2, d3,
    att_own, att_other, dq_out, win, att,
):
    side, flip, _, _ = position()
    for at, half in zip(regions(flip), (first_kv, second_kv, u1, d1, u2, u3, d2, d3)):
        win[pl.ds(at, HALF), :] = half[...]
    for i in range(GROUP):
        rows = slice(i * BLK, (i + 1) * BLK)
        out = dot(
            far_mixed[far_rows(i), :], win[pl.ds(start_of(links, i, far_run(i)), SPAN * BLK), :], ((0,), (0,))
        )
        for index, t in enumerate(near_runs(i)):
            part = near_mixed[near_rows(i, index, 0).start : near_rows(i, index, SPAN - 1).stop, :]
            out = out + dot(part, win[pl.ds(start_of(links, i, t), SPAN * BLK), :], ((0,), (0,)))
        att[rows, :] = out[BLK:, HD:].astype(BF)
        dq_out[rows, :] = (out[:BLK, :HD] * (HD ** -0.5)).astype(BF)
    att_own[...] = att[pl.ds(pl.multiple_of(side * HALF, HALF), HALF), :]
    att_other[...] = att[pl.ds(pl.multiple_of((1 - side) * HALF, HALF), HALF), :]


def spread(grads, w_mine, side, head, target):
    for step in range(2):
        out = dot(grads, weight_rows(w_mine, head ^ (2 * step), 2 * HD), ((1,), (1,))).astype(BF)
        for group in range(2):
            index = 2 * group + step
            part = jnp.where(side == group, out[:HALF], out[HALF:])
            target[index * HALF : (index + 1) * HALF, :] = part


def spread_send_kernel(first_own, second_own, from_d, from_u, dq, w_mine, send, grads):
    side, flip, _, head = position()
    first = first_own[...] + from_d[...].astype(F32)
    second = second_own[...] + from_u[...].astype(F32)
    grads[:, :HD] = dq[...]
    grads[:HALF, HD:] = jnp.where(flip == 1, first, second).astype(BF)
    grads[HALF:, HD:] = jnp.where(flip == 1, second, first).astype(BF)
    spread(grads[...], w_mine, side, head ^ 1, send)


def spread_keep_kernel(grads, w_mine, keep):
    side, _, _, head = position()
    spread(grads[...], w_mine, side, head, keep)


def body(features, w_qkv, block_links, d_out, n_ctx, n_head):
    n_group = n_ctx // 2

    def across(value, flip_ctx, flip_head):
        pairs = [
            (c * n_head + h, (c ^ flip_ctx) * n_head + (h ^ flip_head))
            for c in range(n_ctx)
            for h in range(n_head)
        ]
        return lax.ppermute(value, ("ctx", "head"), pairs)

    def chain(value, back):
        pairs = []
        for ctx in range(n_ctx):
            group, side = divmod(ctx, 2)
            for h in range(n_head):
                to = group + (1 if h % 2 == back else -1)
                inside = 0 <= to < n_group
                target = (2 * to + side) * n_head + h if inside else ctx * n_head + (h ^ 1)
                pairs.append((ctx * n_head + h, target))
        return lax.ppermute(value, ("ctx", "head"), pairs)

    f = features
    sx = across(f, 0, 2)
    sy = across(f, 1, 0)
    sd = across(f, 1, 2)
    w = jnp.transpose(w_qkv, (1, 0, 2))

    def call(kernel, name, outs, ins, mebibytes, flops, scratch=()):
        specs = [SMEM if v.dtype == jnp.int32 else VMEM for v in ins]
        if kernel is begin_kernel:
            specs = [pl.BlockSpec(memory_space=pltpu.HBM)] * 2
            ins = [pltpu.with_memory_space_constraint(v, pltpu.HBM) for v in ins]
        return pl.pallas_call(
            kernel,
            name=name,
            out_shape=outs,
            in_specs=specs,
            out_specs=[SMEM if v.dtype == jnp.int32 else VMEM for v in outs],
            scratch_shapes=list(scratch),
            **params(flops, 2 << 20, mebibytes),
        )(*ins)

    def out(rows, cols, kind=BF):
        return jax.ShapeDtypeStruct((rows, cols), kind)

    def held(rows, cols, kind=BF):
        return pltpu.VMEM((rows, cols), kind)

    product = 2 * ROWS * f.shape[1] * 3 * HD
    attention = 2 * GROUP * 9 * BLK * BLK * 2 * HD
    w_mine, fm, total = call(
        begin_kernel,
        "begin",
        [held(w.shape[1], 3 * HD), held(*f.shape), held(HALF, 3 * HD, F32)],
        (f, w),
        4,
        product,
        [pltpu.SemaphoreType.DMA((4,))],
    )
    (early,) = call(pack_kernel, "pack_early", [out(ROWS, f.shape[1])], (fm, sd), 4, 0)
    other_early = across(early, 0, 1)
    (late,) = call(pack_kernel, "pack_late", [out(ROWS, f.shape[1])], (sy, sx), 4, 0)
    other_late = across(late, 0, 1)
    (total,) = call(
        project_rest_kernel,
        "project_rest",
        [held(ROWS, 3 * HD, F32)],
        (total, early, late, other_early, w_mine),
        4,
        product,
    )
    first, second = call(
        project_kv_kernel, "project_kv", [out(HALF, 2 * HD)] * 2, (other_late, total, w_mine), 4, product
    )

    u1 = chain(first, 0)
    d1 = chain(second, 1)
    u2 = chain(second, 0)
    d2 = chain(first, 1)
    u3 = chain(u1, 0)
    d3 = chain(d1, 1)
    rows, slots = block_links.shape
    link_rows = jnp.pad(block_links.astype(BF), ((0, 16 - rows), (0, HD - slots)))
    (payload,) = call(payload_kernel, "payload", [out(HALF + 16, HD)], (d_out, link_rows, late), 4, 0)
    d_other = across(payload, 1, 0)
    (q,) = call(project_q_kernel, "project_q", [held(ROWS, HD)], (other_late, total, w_mine, u1, d1), 4, product)
    other_links = d_other[HALF : HALF + rows, :slots].astype(jnp.int32)
    (links,) = call(
        links_kernel, "links", [pltpu.SMEM((GROUP + 1, slots), jnp.int32)], (block_links, other_links, q), 4, 0
    )
    links = pltpu.with_memory_space_constraint(links, pltpu.SMEM)
    window = pltpu.VMEM((WINDOW * BLK, 2 * HD), BF)
    sums = pltpu.VMEM((WINDOW * BLK, 2 * HD), F32)
    run = SPAN * BLK
    pairs, terms, prob_grads, stats = call(
        near_scores_kernel,
        "near_scores",
        [
            held(GROUP * 2 * BLK, 2 * HD),
            held(GROUP * 2 * run, BLK, F32),
            held(GROUP * 2 * run, BLK, F32),
            held(GROUP * 3 * 8, BLK, F32),
        ],
        (links, q, first, second, u1, d1, u2, d2, d_out, d_other),
        6,
        attention,
        [window],
    )
    far_mixed, edges, far_u_grad, far_d_grad, scales = call(
        far_grads_kernel,
        "far_grads",
        [
            held(GROUP * run, 2 * HD),
            held(2 * OWN, 2 * HD, F32),
            out(HALF, 2 * HD),
            out(HALF, 2 * HD),
            held(GROUP * 2 * 8, BLK, F32),
        ],
        (links, pairs, stats, u1, d1, u2, u3, d2, d3),
        6,
        attention,
        [window],
    )
    near_mixed, first_own, second_own, u2_grad, d2_grad, u3_grad, d3_grad = call(
        near_grads_kernel,
        "near_grads",
        [held(GROUP * 2 * run, 2 * HD)] + [held(HALF, 2 * HD, F32)] * 2 + [out(HALF, 2 * HD)] * 4,
        (links, pairs, terms, prob_grads, scales, edges),
        4,
        attention,
        [sums],
    )
    att_own, att_other, dq = call(
        outputs_kernel,
        "outputs",
        [out(HALF, HD), out(HALF, HD), held(ROWS, HD)],
        (links, near_mixed, far_mixed, first, second, u1, d1, u2, u3, d2, d3),
        4,
        attention,
        [window, pltpu.VMEM((ROWS, HD), BF)],
    )

    back_d = chain(far_d_grad, 1)
    back_u = chain(far_u_grad, 0)
    d2_back = chain(d2_grad, 1)
    u2_back = chain(u2_grad, 0)

    def merge(one, two, name):
        return call(merge_kernel, name, [out(HALF, 2 * HD)], (one, two, dq), 4, 0)[0]

    from_d = chain(merge(d3_grad, back_d, "merge_d"), 1)
    from_u = chain(merge(u3_grad, back_u, "merge_u"), 0)
    first_own, second_own = call(
        gather_kernel, "gather", [held(HALF, 2 * HD, F32)] * 2, (first_own, second_own, d2_back, u2_back), 4, 0
    )
    send, grads = call(
        spread_send_kernel,
        "spread_send",
        [out(4 * HALF, 2 * HD), held(ROWS, 3 * HD)],
        (first_own, second_own, from_d, from_u, dq, w_mine),
        4,
        product,
    )
    (keep,) = call(spread_keep_kernel, "spread_keep", [held(4 * HALF, 2 * HD)], (grads, w_mine), 4, product)
    arrived = across(send, 0, 1)
    mine, to_x, to_y, to_d = call(
        chip_sum_kernel,
        "chip_sum",
        [out(HALF, 2 * HD)] * 2 + [out(HALF + BLK, 2 * HD), out(HALF, 2 * HD)],
        (keep, arrived, att_other),
        4,
        0,
    )
    gd = across(to_d, 1, 2)
    gy = across(to_y, 1, 0)
    gx = across(to_x, 0, 2)
    attended, grad_features = call(
        finish_kernel, "finish", [out(HALF, 2 * HD)] * 2, (mine, gd, gx, gy, att_own), 4, 0
    )
    return attended, grad_features


def solution(mesh):
    sizes = dict(mesh.shape)
    return jax.shard_map(
        functools.partial(body, n_ctx=sizes["ctx"], n_head=sizes["head"]),
        mesh=mesh,
        in_specs=(P("ctx", "head"), P(None, None, "head"), P("ctx", None), P("ctx", "head")),
        out_specs=(P("ctx", "head"), P("ctx", "head")),
        check_vma=False,
    )
```

```python
import functools

import jax
import jax.numpy as jnp
from jax import lax
from jax.experimental import pallas as pl
from jax.experimental.pallas import tpu as pltpu
from jax.sharding import PartitionSpec as P

HD = 128
BLK = 128
REACH = 6
SPAN = 3
LOG2E = 1.4426950408889634
DEAD = -1e30
BF = jnp.bfloat16
F32 = jnp.float32

GROUP = 4
ROWS = GROUP * BLK
HALF = ROWS // 2
WINDOW = GROUP + 2 * REACH
NEAR_LEFT = (REACH - GROUP) * BLK
OWN = REACH * BLK
NEAR_RIGHT = OWN + ROWS
FAR_RIGHT = NEAR_RIGHT + ROWS


def params(flops, moved, mebibytes):
    return dict(
        compiler_params=pltpu.CompilerParams(vmem_limit_bytes=mebibytes * 1024 * 1024),
        cost_estimate=pl.CostEstimate(flops=flops, bytes_accessed=moved, transcendentals=0),
    )


VMEM = pl.BlockSpec(memory_space=pltpu.VMEM)
SMEM = pl.BlockSpec(memory_space=pltpu.SMEM)


def dot(a, b, dims):
    return lax.dot_general(a, b, (dims, ((), ())), preferred_element_type=F32)


def position():
    ctx, head = lax.axis_index("ctx"), lax.axis_index("head")
    return ctx % 2, head % 2, ctx // 2 * GROUP, head


def begin_kernel(f, w, w_mine, fm, total, sems):
    side, _, _, head = position()
    copies = [pltpu.make_async_copy(f, fm, sems.at[3])]
    for g in range(3):
        cols = pl.ds(pl.multiple_of(side * HD, HD), HD)
        copies.append(pltpu.make_async_copy(w.at[g, :, cols], w_mine.at[:, pl.ds(g * HD, HD)], sems.at[g]))
    for copy in copies:
        copy.start()
    for copy in copies:
        copy.wait()
    total[...] = dot(fm[...], weight_rows(w_mine, head, fm.shape[1]), ((1,), (0,)))


def weight_rows(w_mine, source, width):
    return w_mine[pl.ds(pl.multiple_of(source * width, width), width), :]


def pack_kernel(one, two, out):
    out[:HALF, :] = one[...]
    out[HALF:, :] = two[...]


def project_rest_kernel(before, early, late, other_early, w_mine, total):
    head = position()[3]
    width = early.shape[1]
    mine, across_x, sibling, across_both = (weight_rows(w_mine, head ^ k, width) for k in (0, 2, 1, 3))
    own = before[...] + dot(late[HALF:, :], across_x, ((1,), (0,)))
    total[:HALF, :] = own + dot(other_early[:HALF, :], sibling, ((1,), (0,)))
    partner = dot(late[:HALF, :], mine, ((1,), (0,))) + dot(early[HALF:, :], across_x, ((1,), (0,)))
    total[HALF:, :] = partner + dot(other_early[HALF:, :], across_both, ((1,), (0,)))


def last_product(head, other_late, w_mine, cols, group):
    width = other_late.shape[1]
    rows = pl.ds(pl.multiple_of((head ^ (3 if group == 0 else 1)) * width, width), width)
    piece = other_late[HALF:, :] if group == 0 else other_late[:HALF, :]
    return dot(piece, w_mine[rows, cols], ((1,), (0,)))


def project_kv_kernel(other_late, before, w_mine, first_out, second_out):
    side, flip, _, head = position()
    own, partner = (
        (before[g * HALF : (g + 1) * HALF, HD:] + last_product(head, other_late, w_mine, slice(HD, 3 * HD), g)).astype(BF)
        for g in range(2)
    )
    near_first = side ^ (1 - flip) == 0
    first_out[...] = jnp.where(near_first, own, partner)
    second_out[...] = jnp.where(near_first, partner, own)


def merge_kernel(one, two, dq, out):
    del dq
    out[...] = (one[...].astype(F32) + two[...].astype(F32)).astype(BF)


def gather_kernel(first_own, second_own, d, u, first_out, second_out):
    first_out[...] = first_own[...] + u[...].astype(F32)
    second_out[...] = second_own[...] + d[...].astype(F32)


def chip_sum_near_kernel(keep, arrived, att_other, mine, to_y):
    total = (keep[...].astype(F32) + arrived[...].astype(F32)).astype(BF)
    mine[...] = total[:HALF]
    to_y[:HALF, :] = total[HALF:]
    for half in range(2):
        to_y[HALF:, half * HD : (half + 1) * HD] = att_other[half * BLK : (half + 1) * BLK, :]


def chip_sum_far_kernel(keep, arrived, to_x, to_d):
    total = (keep[...].astype(F32) + arrived[...].astype(F32)).astype(BF)
    to_x[...] = total[:HALF]
    to_d[...] = total[HALF:]


def finish_kernel(mine, gd, gx, from_y, att_own, attended, grad_features):
    total = mine[...].astype(F32) + gd[...].astype(F32) + gx[...].astype(F32) + from_y[:HALF, :].astype(F32)
    grad_features[...] = total.astype(BF)
    side = position()[0]
    att_other = jnp.concatenate([from_y[HALF:, :HD], from_y[HALF:, HD:]], axis=0)
    for half in range(2):
        cols = slice(half * HD, (half + 1) * HD)
        attended[:, cols] = jnp.where(side == half, att_own[...], att_other)


def project_q_kernel(other_late, before, w_mine, u1, d1, q_out):
    del u1, d1
    side, _, _, head = position()
    for g in range(2):
        part = before[g * HALF : (g + 1) * HALF, :HD] + last_product(head, other_late, w_mine, slice(0, HD), g)
        q_out[pl.ds(pl.multiple_of((side ^ g) * HALF, HALF), HALF), :] = part.astype(BF)


def payload_kernel(d_own, link_rows, late, payload):
    del late
    side = position()[0]
    payload[:HALF, :] = jnp.where(side == 0, d_own[:, HD:], d_own[:, :HD])
    payload[HALF:, :] = link_rows[...]


def links_kernel(own, other, q, links):
    del q
    side, _, first, _ = position()
    for i in range(GROUP):
        for k in range(3 * SPAN):
            links[i, k] = jnp.where(side == i // 2, own[i % 2, k], other[i % 2, k])
        for t in (1, 2):
            base = jnp.int32(-(1 << 20))
            for j in range(SPAN):
                entry = links[i, SPAN * t + j]
                base = jnp.maximum(base, jnp.where(entry >= 0, entry - j, -(1 << 20)))
            base = jnp.where(base > -(1 << 19), base - first + REACH, i + 1 if t == 1 else i + REACH + SPAN)
            lowest = i if t == 1 else i + REACH + SPAN - 1
            links[GROUP, 2 * i + t - 1] = jnp.clip(base, lowest, lowest + 2) * BLK


def regions(flip):
    left_lo, left_hi = NEAR_LEFT, NEAR_LEFT + HALF
    right_lo, right_hi = NEAR_RIGHT, NEAR_RIGHT + HALF
    pick = lambda plain, flipped: pl.multiple_of((1 - flip) * plain + flip * flipped, HALF)
    return (
        pick(OWN + HALF, OWN),
        pick(OWN, OWN + HALF),
        pick(left_hi, right_lo),
        pick(right_lo, left_hi),
        pick(left_lo, right_hi),
        pick(0, FAR_RIGHT),
        pick(right_hi, left_lo),
        pick(FAR_RIGHT, 0),
    )


def start_of(links, i, t):
    if t == 0:
        return (REACH + i - 1) * BLK
    return pl.multiple_of(links[GROUP, 2 * i + t - 1], BLK)


def far_run(i):
    return 1 if i < GROUP // 2 else 2


def near_runs(i):
    return tuple(t for t in range(3) if t != far_run(i))


def near_rows(i, index, j):
    first = ((2 * i + index) * SPAN + j) * BLK
    return slice(first, first + BLK)


def far_rows(i):
    return slice(i * SPAN * BLK, (i + 1) * SPAN * BLK)


def run_scores(links, rows, pair, i, t):
    product = dot(rows, pair, ((1,), (1,)))
    blocks = []
    for j in range(SPAN):
        block = product[j * BLK : (j + 1) * BLK]
        bias = jnp.where(links[i, SPAN * t + j] >= 0, 0.0, DEAD).astype(F32)
        blocks.append((block[:, :BLK], block[:, BLK:], bias))
    return blocks


def fold(block):
    return block.reshape(BLK // 8, 8, BLK)


def largest_of(blocks):
    best = None
    for score, _, bias in blocks:
        peak = jnp.max(fold(score), axis=0) + bias
        best = peak if best is None else jnp.maximum(best, peak)
    return jnp.max(best, axis=0, keepdims=True)


def exponentials(blocks, largest):
    terms = []
    total = jnp.zeros((8, BLK), F32)
    weighted = jnp.zeros((8, BLK), F32)
    for score, prob_grad, bias in blocks:
        term = jnp.exp2((score - (largest - bias)) * (HD ** -0.5 * LOG2E))
        terms.append(term)
        total = total + jnp.sum(fold(term), axis=0)
        weighted = weighted + jnp.sum(fold(term * prob_grad), axis=0)
    return terms, jnp.sum(total, axis=0, keepdims=True), jnp.sum(weighted, axis=0, keepdims=True)


def mix(share, prob_grad, row_dot):
    grad = share * (prob_grad - row_dot)
    return jnp.concatenate([grad.astype(BF), share.astype(BF)], axis=1)


def side_factor():
    scale = HD ** -0.5
    return jnp.where(lax.broadcasted_iota(jnp.int32, (1, 2 * HD), 1) < HD, scale, 1.0).astype(F32)


def near_scores_kernel(
    links, q, first_kv, second_kv, u1, d1, u2, d2, d_own, d_other,
    pairs, terms_out, prob_grads_out, stats, win,
):
    side, flip, _, _ = position()
    places = regions(flip)
    for at, half in zip(places[:5] + places[6:7], (first_kv, second_kv, u1, d1, u2, d2)):
        win[pl.ds(at, HALF), :] = half[...]
    zeros = jnp.zeros((BLK, HD), BF)
    own_cols = pl.ds(pl.multiple_of(side * HD, HD), HD)
    for i in range(GROUP):
        rows = slice(i * BLK, (i + 1) * BLK)
        here = slice((i % 2) * BLK, (i % 2 + 1) * BLK)
        d_blk = jnp.where(side == i // 2, d_own[here, own_cols], d_other[here, :])
        pair = jnp.concatenate(
            [
                jnp.concatenate([q[rows, :], zeros], axis=1),
                jnp.concatenate([zeros, d_blk], axis=1),
            ],
            axis=0,
        )
        pairs[2 * i * BLK : 2 * (i + 1) * BLK, :] = pair
        blocks = []
        for t in near_runs(i):
            blocks += run_scores(links, win[pl.ds(start_of(links, i, t), SPAN * BLK), :], pair, i, t)
        largest = largest_of(blocks)
        terms, total, weighted = exponentials(blocks, largest)
        for n, term in enumerate(terms):
            terms_out[near_rows(i, 0, n), :] = term
            prob_grads_out[near_rows(i, 0, n), :] = blocks[n][1]
        for n, row in enumerate((largest, total, weighted)):
            stats[8 * (3 * i + n) : 8 * (3 * i + n + 1), :] = jnp.broadcast_to(row, (8, BLK))


def far_grads_kernel(
    links, pairs, stats, u1, d1, u2, u3, d2, d3,
    mixed, edges, far_u_out, far_d_out, scales, win,
):
    places = regions(position()[1])
    for at, half in zip(places[2:], (u1, d1, u2, u3, d2, d3)):
        win[pl.ds(at, HALF), :] = half[...]
    edges[...] = jnp.zeros_like(edges)
    scale = HD ** -0.5 * LOG2E
    span = range(GROUP)
    starts = [start_of(links, i, far_run(i)) for i in span]
    pair = [pairs[2 * i * BLK : 2 * (i + 1) * BLK, :] for i in span]
    near = [[stats[8 * (3 * i + n) : 8 * (3 * i + n) + 1, :] for n in range(3)] for i in span]
    blocks = [
        run_scores(links, win[pl.ds(starts[i], SPAN * BLK), :], pair[i], i, far_run(i)) for i in span
    ]
    largest = [jnp.maximum(near[i][0], largest_of(blocks[i])) for i in span]
    found = [exponentials(blocks[i], largest[i]) for i in span]
    parts = []
    for i in span:
        terms, total, weighted = found[i]
        near_scale = jnp.exp2((near[i][0] - largest[i]) * scale)
        inverse = 1.0 / (total + near_scale * near[i][1])
        row_dot = (weighted + near_scale * near[i][2]) * inverse
        for n, row in enumerate((near_scale * inverse, row_dot)):
            scales[8 * (2 * i + n) : 8 * (2 * i + n + 1), :] = jnp.broadcast_to(row, (8, BLK))
        parts.append(
            jnp.concatenate([mix(term * inverse, block[1], row_dot) for term, block in zip(terms, blocks[i])], axis=0)
        )
    for i in span:
        mixed[far_rows(i), :] = parts[i]
        at = starts[i] if i < GROUP // 2 else starts[i] - ROWS
        edges[pl.ds(pl.multiple_of(at, BLK), SPAN * BLK), :] += dot(parts[i], pair[i], ((1,), (0,)))
    factor = side_factor()
    flip = position()[1]
    for target, left in ((far_u_out, flip), (far_d_out, 1 - flip)):
        at = pl.multiple_of((1 - left) * (2 * OWN - HALF), HALF)
        target[...] = (edges[pl.ds(at, HALF), :] * factor).astype(BF)


def near_grads_kernel(
    links, pairs, terms, prob_grads, scales, edges, mixed, first_own, second_own,
    u2_out, d2_out, u3_out, d3_out, acc,
):
    acc[NEAR_LEFT:OWN, :] = edges[NEAR_LEFT:OWN, :]
    acc[OWN:NEAR_RIGHT, :] = jnp.zeros((ROWS, 2 * HD), F32)
    acc[NEAR_RIGHT:FAR_RIGHT, :] = edges[OWN : OWN + ROWS, :]
    for i in range(GROUP):
        pair = pairs[2 * i * BLK : 2 * (i + 1) * BLK, :]
        scale, row_dot = (scales[8 * (2 * i + n) : 8 * (2 * i + n) + 1, :] for n in range(2))
        for index, t in enumerate(near_runs(i)):
            parts = []
            for j in range(SPAN):
                rows = near_rows(i, index, j)
                parts.append(mix(terms[rows, :] * scale, prob_grads[rows, :], row_dot))
                mixed[rows, :] = parts[-1]
            at = pl.ds(start_of(links, i, t), SPAN * BLK)
            acc[at, :] += dot(jnp.concatenate(parts, axis=0), pair, ((1,), (0,)))
    factor = side_factor()
    first, second, u1, d1, u2, _, d2, _ = regions(position()[1])
    first_own[...] = acc[pl.ds(first, HALF), :] * factor
    second_own[...] = acc[pl.ds(second, HALF), :] * factor
    for target, at in ((u2_out, d2), (d2_out, u2), (u3_out, d1), (d3_out, u1)):
        target[...] = (acc[pl.ds(at, HALF), :] * factor).astype(BF)


def outputs_kernel(
    links, near_mixed, far_mixed, first_kv, second_kv, u1, d1, u2, u3, d2, d3,
    att_own, att_other, dq_out, win, att,
):
    side, flip, _, _ = position()
    for at, half in zip(regions(flip), (first_kv, second_kv, u1, d1, u2, u3, d2, d3)):
        win[pl.ds(at, HALF), :] = half[...]
    for i in range(GROUP):
        rows = slice(i * BLK, (i + 1) * BLK)
        out = dot(
            far_mixed[far_rows(i), :], win[pl.ds(start_of(links, i, far_run(i)), SPAN * BLK), :], ((0,), (0,))
        )
        for index, t in enumerate(near_runs(i)):
            part = near_mixed[near_rows(i, index, 0).start : near_rows(i, index, SPAN - 1).stop, :]
            out = out + dot(part, win[pl.ds(start_of(links, i, t), SPAN * BLK), :], ((0,), (0,)))
        att[rows, :] = out[BLK:, HD:].astype(BF)
        dq_out[rows, :] = (out[:BLK, :HD] * (HD ** -0.5)).astype(BF)
    att_own[...] = att[pl.ds(pl.multiple_of(side * HALF, HALF), HALF), :]
    att_other[...] = att[pl.ds(pl.multiple_of((1 - side) * HALF, HALF), HALF), :]


def spread(grads, w_mine, side, head, target):
    out = dot(grads, weight_rows(w_mine, head, 2 * HD), ((1,), (1,))).astype(BF)
    target[:HALF, :] = jnp.where(side == 0, out[:HALF], out[HALF:])
    target[HALF:, :] = jnp.where(side == 0, out[HALF:], out[:HALF])


def spread_near_kernel(first_own, second_own, from_d, from_u, dq, w_mine, send, grads):
    side, flip, _, head = position()
    first = first_own[...] + from_d[...].astype(F32)
    second = second_own[...] + from_u[...].astype(F32)
    grads[:, :HD] = dq[...]
    grads[:HALF, HD:] = jnp.where(flip == 1, first, second).astype(BF)
    grads[HALF:, HD:] = jnp.where(flip == 1, second, first).astype(BF)
    spread(grads[...], w_mine, side, head ^ 1, send)


def spread_far_kernel(grads, w_mine, send):
    side, _, _, head = position()
    spread(grads[...], w_mine, side, head ^ 3, send)


def spread_keep_kernel(grads, w_mine, near, far):
    side, _, _, head = position()
    spread(grads[...], w_mine, side, head, near)
    spread(grads[...], w_mine, side, head ^ 2, far)


def body(features, w_qkv, block_links, d_out, n_ctx, n_head):
    n_group = n_ctx // 2

    def across(value, flip_ctx, flip_head):
        pairs = [
            (c * n_head + h, (c ^ flip_ctx) * n_head + (h ^ flip_head))
            for c in range(n_ctx)
            for h in range(n_head)
        ]
        return lax.ppermute(value, ("ctx", "head"), pairs)

    def chain(value, back):
        pairs = []
        for ctx in range(n_ctx):
            group, side = divmod(ctx, 2)
            for h in range(n_head):
                to = group + (1 if h % 2 == back else -1)
                inside = 0 <= to < n_group
                target = (2 * to + side) * n_head + h if inside else ctx * n_head + (h ^ 1)
                pairs.append((ctx * n_head + h, target))
        return lax.ppermute(value, ("ctx", "head"), pairs)

    f = features
    sx = across(f, 0, 2)
    sy = across(f, 1, 0)
    sd = across(f, 1, 2)
    w = jnp.transpose(w_qkv, (1, 0, 2))

    def call(kernel, name, outs, ins, mebibytes, flops, scratch=()):
        specs = [SMEM if v.dtype == jnp.int32 else VMEM for v in ins]
        if kernel is begin_kernel:
            specs = [pl.BlockSpec(memory_space=pltpu.HBM)] * 2
            ins = [pltpu.with_memory_space_constraint(v, pltpu.HBM) for v in ins]
        return pl.pallas_call(
            kernel,
            name=name,
            out_shape=outs,
            in_specs=specs,
            out_specs=[SMEM if v.dtype == jnp.int32 else VMEM for v in outs],
            scratch_shapes=list(scratch),
            **params(flops, 2 << 20, mebibytes),
        )(*ins)

    def out(rows, cols, kind=BF):
        return jax.ShapeDtypeStruct((rows, cols), kind)

    def held(rows, cols, kind=BF):
        return pltpu.VMEM((rows, cols), kind)

    product = 2 * ROWS * f.shape[1] * 3 * HD
    attention = 2 * GROUP * 9 * BLK * BLK * 2 * HD
    w_mine, fm, total = call(
        begin_kernel,
        "begin",
        [held(w.shape[1], 3 * HD), held(*f.shape), held(HALF, 3 * HD, F32)],
        (f, w),
        4,
        product,
        [pltpu.SemaphoreType.DMA((4,))],
    )
    (early,) = call(pack_kernel, "pack_early", [out(ROWS, f.shape[1])], (fm, sd), 4, 0)
    other_early = across(early, 0, 1)
    (late,) = call(pack_kernel, "pack_late", [out(ROWS, f.shape[1])], (sy, sx), 4, 0)
    other_late = across(late, 0, 1)
    (total,) = call(
        project_rest_kernel,
        "project_rest",
        [held(ROWS, 3 * HD, F32)],
        (total, early, late, other_early, w_mine),
        4,
        product,
    )
    first, second = call(
        project_kv_kernel, "project_kv", [out(HALF, 2 * HD)] * 2, (other_late, total, w_mine), 4, product
    )

    u1 = chain(first, 0)
    d1 = chain(second, 1)
    u2 = chain(second, 0)
    d2 = chain(first, 1)
    u3 = chain(u1, 0)
    d3 = chain(d1, 1)
    rows, slots = block_links.shape
    link_rows = jnp.pad(block_links.astype(BF), ((0, 16 - rows), (0, HD - slots)))
    (payload,) = call(payload_kernel, "payload", [out(HALF + 16, HD)], (d_out, link_rows, late), 4, 0)
    d_other = across(payload, 1, 0)
    (q,) = call(project_q_kernel, "project_q", [held(ROWS, HD)], (other_late, total, w_mine, u1, d1), 4, product)
    other_links = d_other[HALF : HALF + rows, :slots].astype(jnp.int32)
    (links,) = call(
        links_kernel, "links", [pltpu.SMEM((GROUP + 1, slots), jnp.int32)], (block_links, other_links, q), 4, 0
    )
    links = pltpu.with_memory_space_constraint(links, pltpu.SMEM)
    window = pltpu.VMEM((WINDOW * BLK, 2 * HD), BF)
    sums = pltpu.VMEM((WINDOW * BLK, 2 * HD), F32)
    run = SPAN * BLK
    pairs, terms, prob_grads, stats = call(
        near_scores_kernel,
        "near_scores",
        [
            held(GROUP * 2 * BLK, 2 * HD),
            held(GROUP * 2 * run, BLK, F32),
            held(GROUP * 2 * run, BLK, F32),
            held(GROUP * 3 * 8, BLK, F32),
        ],
        (links, q, first, second, u1, d1, u2, d2, d_out, d_other),
        6,
        attention,
        [window],
    )
    far_mixed, edges, far_u_grad, far_d_grad, scales = call(
        far_grads_kernel,
        "far_grads",
        [
            held(GROUP * run, 2 * HD),
            held(2 * OWN, 2 * HD, F32),
            out(HALF, 2 * HD),
            out(HALF, 2 * HD),
            held(GROUP * 2 * 8, BLK, F32),
        ],
        (links, pairs, stats, u1, d1, u2, u3, d2, d3),
        6,
        attention,
        [window],
    )
    near_mixed, first_own, second_own, u2_grad, d2_grad, u3_grad, d3_grad = call(
        near_grads_kernel,
        "near_grads",
        [held(GROUP * 2 * run, 2 * HD)] + [held(HALF, 2 * HD, F32)] * 2 + [out(HALF, 2 * HD)] * 4,
        (links, pairs, terms, prob_grads, scales, edges),
        4,
        attention,
        [sums],
    )
    att_own, att_other, dq = call(
        outputs_kernel,
        "outputs",
        [out(HALF, HD), out(HALF, HD), held(ROWS, HD)],
        (links, near_mixed, far_mixed, first, second, u1, d1, u2, u3, d2, d3),
        4,
        attention,
        [window, pltpu.VMEM((ROWS, HD), BF)],
    )

    back_d = chain(far_d_grad, 1)
    back_u = chain(far_u_grad, 0)
    d2_back = chain(d2_grad, 1)
    u2_back = chain(u2_grad, 0)

    def merge(one, two, name):
        return call(merge_kernel, name, [out(HALF, 2 * HD)], (one, two, dq), 4, 0)[0]

    from_d = chain(merge(d3_grad, back_d, "merge_d"), 1)
    from_u = chain(merge(u3_grad, back_u, "merge_u"), 0)
    first_own, second_own = call(
        gather_kernel, "gather", [held(HALF, 2 * HD, F32)] * 2, (first_own, second_own, d2_back, u2_back), 4, 0
    )
    near_send, grads = call(
        spread_near_kernel,
        "spread_near",
        [out(ROWS, 2 * HD), held(ROWS, 3 * HD)],
        (first_own, second_own, from_d, from_u, dq, w_mine),
        4,
        product,
    )
    near_arrived = across(near_send, 0, 1)
    (far_send,) = call(spread_far_kernel, "spread_far", [out(ROWS, 2 * HD)], (grads, w_mine), 4, product)
    far_arrived = across(far_send, 0, 1)
    near, far = call(spread_keep_kernel, "spread_keep", [held(ROWS, 2 * HD)] * 2, (grads, w_mine), 4, product)
    mine, to_y = call(
        chip_sum_near_kernel,
        "chip_sum_near",
        [out(HALF, 2 * HD), out(HALF + BLK, 2 * HD)],
        (near, near_arrived, att_other),
        4,
        0,
    )
    gy = across(to_y, 1, 0)
    to_x, to_d = call(chip_sum_far_kernel, "chip_sum_far", [out(HALF, 2 * HD)] * 2, (far, far_arrived), 4, 0)
    gd = across(to_d, 1, 2)
    gx = across(to_x, 0, 2)
    attended, grad_features = call(
        finish_kernel, "finish", [out(HALF, 2 * HD)] * 2, (mine, gd, gx, gy, att_own), 4, 0
    )
    return attended, grad_features


def solution(mesh):
    sizes = dict(mesh.shape)
    return jax.shard_map(
        functools.partial(body, n_ctx=sizes["ctx"], n_head=sizes["head"]),
        mesh=mesh,
        in_specs=(P("ctx", "head"), P(None, None, "head"), P("ctx", None), P("ctx", "head")),
        out_specs=(P("ctx", "head"), P("ctx", "head")),
        check_vma=False,
    )
```

```python
import functools

import jax
import jax.numpy as jnp
from jax import lax
from jax.experimental import pallas as pl
from jax.experimental.pallas import tpu as pltpu
from jax.sharding import PartitionSpec as P

HD = 128
BLK = 128
REACH = 6
SPAN = 3
LOG2E = 1.4426950408889634
DEAD = -1e30
BF = jnp.bfloat16
F32 = jnp.float32

GROUP = 4
ROWS = GROUP * BLK
HALF = ROWS // 2
WINDOW = GROUP + 2 * REACH
NEAR_LEFT = (REACH - GROUP) * BLK
OWN = REACH * BLK
NEAR_RIGHT = OWN + ROWS
FAR_RIGHT = NEAR_RIGHT + ROWS


def params(flops, moved, mebibytes):
    return dict(
        compiler_params=pltpu.CompilerParams(vmem_limit_bytes=mebibytes * 1024 * 1024),
        cost_estimate=pl.CostEstimate(flops=flops, bytes_accessed=moved, transcendentals=0),
    )


VMEM = pl.BlockSpec(memory_space=pltpu.VMEM)
SMEM = pl.BlockSpec(memory_space=pltpu.SMEM)


def dot(a, b, dims):
    return lax.dot_general(a, b, (dims, ((), ())), preferred_element_type=F32)


def position():
    ctx, head = lax.axis_index("ctx"), lax.axis_index("head")
    return ctx % 2, head % 2, ctx // 2 * GROUP, head


def begin_kernel(f, w, w_mine, fm, total, sems):
    side, _, _, head = position()
    copies = [pltpu.make_async_copy(f, fm, sems.at[3])]
    for g in range(3):
        cols = pl.ds(pl.multiple_of(side * HD, HD), HD)
        copies.append(pltpu.make_async_copy(w.at[g, :, cols], w_mine.at[:, pl.ds(g * HD, HD)], sems.at[g]))
    for copy in copies:
        copy.start()
    for copy in copies:
        copy.wait()
    total[...] = dot(fm[...], weight_rows(w_mine, head, fm.shape[1]), ((1,), (0,)))


def weight_rows(w_mine, source, width):
    return w_mine[pl.ds(pl.multiple_of(source * width, width), width), :]


def pack_kernel(one, two, out):
    out[:HALF, :] = one[...]
    out[HALF:, :] = two[...]


def project_rest_kernel(before, early, late, other_early, w_mine, total):
    head = position()[3]
    width = early.shape[1]
    mine, across_x, sibling, across_both = (weight_rows(w_mine, head ^ k, width) for k in (0, 2, 1, 3))
    own = before[...] + dot(late[HALF:, :], across_x, ((1,), (0,)))
    total[:HALF, :] = own + dot(other_early[:HALF, :], sibling, ((1,), (0,)))
    partner = dot(late[:HALF, :], mine, ((1,), (0,))) + dot(early[HALF:, :], across_x, ((1,), (0,)))
    total[HALF:, :] = partner + dot(other_early[HALF:, :], across_both, ((1,), (0,)))


def last_product(head, other_late, w_mine, cols, group):
    width = other_late.shape[1]
    rows = pl.ds(pl.multiple_of((head ^ (3 if group == 0 else 1)) * width, width), width)
    piece = other_late[HALF:, :] if group == 0 else other_late[:HALF, :]
    return dot(piece, w_mine[rows, cols], ((1,), (0,)))


def project_kv_kernel(other_late, before, w_mine, first_out, second_out):
    side, flip, _, head = position()
    own, partner = (
        (before[g * HALF : (g + 1) * HALF, HD:] + last_product(head, other_late, w_mine, slice(HD, 3 * HD), g)).astype(BF)
        for g in range(2)
    )
    near_first = side ^ (1 - flip) == 0
    first_out[...] = jnp.where(near_first, own, partner)
    second_out[...] = jnp.where(near_first, partner, own)


def merge_kernel(one, two, dq, out):
    del dq
    out[...] = (one[...].astype(F32) + two[...].astype(F32)).astype(BF)


def gather_kernel(first_own, second_own, d, u, first_out, second_out):
    first_out[...] = first_own[...] + u[...].astype(F32)
    second_out[...] = second_own[...] + d[...].astype(F32)


def chip_sum_kernel(keep, arrived, att_other, mine, to_x, to_y, to_d):
    for index, target in enumerate((mine, to_x, to_y, to_d)):
        rows = slice(index * HALF, (index + 1) * HALF)
        target[:HALF, :] = (keep[rows, :].astype(F32) + arrived[rows, :].astype(F32)).astype(BF)
    for half in range(2):
        to_y[HALF:, half * HD : (half + 1) * HD] = att_other[half * BLK : (half + 1) * BLK, :]


def finish_kernel(mine, gd, gx, from_y, att_own, attended, grad_features):
    total = mine[...].astype(F32) + gd[...].astype(F32) + gx[...].astype(F32) + from_y[:HALF, :].astype(F32)
    grad_features[...] = total.astype(BF)
    side = position()[0]
    att_other = jnp.concatenate([from_y[HALF:, :HD], from_y[HALF:, HD:]], axis=0)
    for half in range(2):
        cols = slice(half * HD, (half + 1) * HD)
        attended[:, cols] = jnp.where(side == half, att_own[...], att_other)


def project_q_kernel(other_late, before, w_mine, u1, d1, q_out):
    del u1, d1
    side, _, _, head = position()
    for g in range(2):
        part = before[g * HALF : (g + 1) * HALF, :HD] + last_product(head, other_late, w_mine, slice(0, HD), g)
        q_out[pl.ds(pl.multiple_of((side ^ g) * HALF, HALF), HALF), :] = part.astype(BF)


def payload_kernel(d_own, link_rows, late, payload):
    del late
    side = position()[0]
    payload[:HALF, :] = jnp.where(side == 0, d_own[:, HD:], d_own[:, :HD])
    payload[HALF:, :] = link_rows[...]


def links_kernel(own, other, q, links):
    del q
    side, _, first, _ = position()
    for i in range(GROUP):
        for k in range(3 * SPAN):
            links[i, k] = jnp.where(side == i // 2, own[i % 2, k], other[i % 2, k])
        for t in (1, 2):
            base = jnp.int32(-(1 << 20))
            for j in range(SPAN):
                entry = links[i, SPAN * t + j]
                base = jnp.maximum(base, jnp.where(entry >= 0, entry - j, -(1 << 20)))
            base = jnp.where(base > -(1 << 19), base - first + REACH, i + 1 if t == 1 else i + REACH + SPAN)
            lowest = i if t == 1 else i + REACH + SPAN - 1
            links[GROUP, 2 * i + t - 1] = jnp.clip(base, lowest, lowest + 2) * BLK


def regions(flip):
    left_lo, left_hi = NEAR_LEFT, NEAR_LEFT + HALF
    right_lo, right_hi = NEAR_RIGHT, NEAR_RIGHT + HALF
    pick = lambda plain, flipped: pl.multiple_of((1 - flip) * plain + flip * flipped, HALF)
    return (
        pick(OWN + HALF, OWN),
        pick(OWN, OWN + HALF),
        pick(left_hi, right_lo),
        pick(right_lo, left_hi),
        pick(left_lo, right_hi),
        pick(0, FAR_RIGHT),
        pick(right_hi, left_lo),
        pick(FAR_RIGHT, 0),
    )


def start_of(links, i, t):
    if t == 0:
        return (REACH + i - 1) * BLK
    return pl.multiple_of(links[GROUP, 2 * i + t - 1], BLK)


def far_run(i):
    return 1 if i < GROUP // 2 else 2


def near_runs(i):
    return tuple(t for t in range(3) if t != far_run(i))


def near_rows(i, index, j):
    first = ((2 * i + index) * SPAN + j) * BLK
    return slice(first, first + BLK)


def far_rows(i):
    return slice(i * SPAN * BLK, (i + 1) * SPAN * BLK)


def run_scores(links, rows, pair, i, t):
    product = dot(rows, pair, ((1,), (1,)))
    blocks = []
    for j in range(SPAN):
        block = product[j * BLK : (j + 1) * BLK]
        bias = jnp.where(links[i, SPAN * t + j] >= 0, 0.0, DEAD).astype(F32)
        blocks.append((block[:, :BLK], block[:, BLK:], bias))
    return blocks


def fold(block):
    return block.reshape(BLK // 8, 8, BLK)


def largest_of(blocks):
    best = None
    for score, _, bias in blocks:
        peak = jnp.max(fold(score), axis=0) + bias
        best = peak if best is None else jnp.maximum(best, peak)
    return jnp.max(best, axis=0, keepdims=True)


def exponentials(blocks, largest):
    terms = []
    total = jnp.zeros((8, BLK), F32)
    weighted = jnp.zeros((8, BLK), F32)
    for score, prob_grad, bias in blocks:
        term = jnp.exp2((score - (largest - bias)) * (HD ** -0.5 * LOG2E))
        terms.append(term)
        total = total + jnp.sum(fold(term), axis=0)
        weighted = weighted + jnp.sum(fold(term * prob_grad), axis=0)
    return terms, jnp.sum(total, axis=0, keepdims=True), jnp.sum(weighted, axis=0, keepdims=True)


def mix(share, prob_grad, row_dot):
    grad = share * (prob_grad - row_dot)
    return jnp.concatenate([grad.astype(BF), share.astype(BF)], axis=1)


def side_factor():
    scale = HD ** -0.5
    return jnp.where(lax.broadcasted_iota(jnp.int32, (1, 2 * HD), 1) < HD, scale, 1.0).astype(F32)


def near_scores_kernel(
    links, q, first_kv, second_kv, u1, d1, u2, d2, d_own, d_other,
    pairs, terms_out, prob_grads_out, stats, win,
):
    side, flip, _, _ = position()
    places = regions(flip)
    for at, half in zip(places[:5] + places[6:7], (first_kv, second_kv, u1, d1, u2, d2)):
        win[pl.ds(at, HALF), :] = half[...]
    zeros = jnp.zeros((BLK, HD), BF)
    own_cols = pl.ds(pl.multiple_of(side * HD, HD), HD)
    for i in range(GROUP):
        rows = slice(i * BLK, (i + 1) * BLK)
        here = slice((i % 2) * BLK, (i % 2 + 1) * BLK)
        d_blk = jnp.where(side == i // 2, d_own[here, own_cols], d_other[here, :])
        pair = jnp.concatenate(
            [
                jnp.concatenate([q[rows, :], zeros], axis=1),
                jnp.concatenate([zeros, d_blk], axis=1),
            ],
            axis=0,
        )
        pairs[2 * i * BLK : 2 * (i + 1) * BLK, :] = pair
        blocks = []
        for t in near_runs(i):
            blocks += run_scores(links, win[pl.ds(start_of(links, i, t), SPAN * BLK), :], pair, i, t)
        largest = largest_of(blocks)
        terms, total, weighted = exponentials(blocks, largest)
        for n, term in enumerate(terms):
            terms_out[near_rows(i, 0, n), :] = term
            prob_grads_out[near_rows(i, 0, n), :] = blocks[n][1]
        for n, row in enumerate((largest, total, weighted)):
            stats[8 * (3 * i + n) : 8 * (3 * i + n + 1), :] = jnp.broadcast_to(row, (8, BLK))


def far_grads_kernel(links, pairs, stats, near, middle, far, after, mixed, edge, far_out, scales, win, chain):
    del after
    flip = position()[1]
    right = flip if chain == 0 else 1 - flip
    at_far = pl.multiple_of(right * ROWS, HALF)
    win[pl.ds(at_far, HALF), :] = far[...]
    win[HALF : 2 * HALF, :] = middle[...]
    win[pl.ds(pl.multiple_of(ROWS - right * ROWS, HALF), HALF), :] = near[...]
    edge[...] = jnp.zeros_like(edge)
    scale = HD ** -0.5 * LOG2E
    span = range(GROUP // 2)
    query = [2 * right + k for k in span]
    starts = [
        pl.multiple_of(links[GROUP, 2 * query[k] + right] - right * NEAR_RIGHT, BLK) for k in span
    ]
    pair = [pairs[pl.ds(pl.multiple_of(2 * query[k] * BLK, 2 * BLK), 2 * BLK), :] for k in span]
    known = [
        [stats[pl.ds(pl.multiple_of(8 * (3 * query[k] + n), 8), 8), :][:1] for n in range(3)] for k in span
    ]
    blocks = [
        run_scores(links, win[pl.ds(starts[k], SPAN * BLK), :], pair[k], query[k], 1 + right) for k in span
    ]
    largest = [jnp.maximum(known[k][0], largest_of(blocks[k])) for k in span]
    found = [exponentials(blocks[k], largest[k]) for k in span]
    parts = []
    for k in span:
        terms, total, weighted = found[k]
        near_scale = jnp.exp2((known[k][0] - largest[k]) * scale)
        inverse = 1.0 / (total + near_scale * known[k][1])
        row_dot = (weighted + near_scale * known[k][2]) * inverse
        for n, row in enumerate((near_scale * inverse, row_dot)):
            scales[8 * (2 * k + n) : 8 * (2 * k + n + 1), :] = jnp.broadcast_to(row, (8, BLK))
        parts.append(
            jnp.concatenate([mix(term * inverse, block[1], row_dot) for term, block in zip(terms, blocks[k])], axis=0)
        )
    for k in span:
        mixed[far_rows(k), :] = parts[k]
        edge[pl.ds(starts[k], SPAN * BLK), :] += dot(parts[k], pair[k], ((1,), (0,)))
    far_out[...] = (edge[pl.ds(at_far, HALF), :] * side_factor()).astype(BF)


def by_side(i, from_u, from_d):
    left = i < GROUP // 2
    return jnp.where((position()[1] == 0) == left, from_u, from_d)


def near_grads_kernel(
    links, pairs, terms, prob_grads, u_scales, d_scales, u_edge, d_edge, mixed, first_own, second_own,
    u2_out, d2_out, u3_out, d3_out, acc,
):
    acc[NEAR_LEFT:OWN, :] = by_side(0, u_edge[NEAR_LEFT:OWN, :], d_edge[NEAR_LEFT:OWN, :])
    acc[OWN:NEAR_RIGHT, :] = jnp.zeros((ROWS, 2 * HD), F32)
    acc[NEAR_RIGHT:FAR_RIGHT, :] = by_side(GROUP - 1, u_edge[:ROWS, :], d_edge[:ROWS, :])
    for i in range(GROUP):
        pair = pairs[2 * i * BLK : 2 * (i + 1) * BLK, :]
        at = [8 * (2 * (i % 2) + n) for n in range(2)]
        scale, row_dot = (by_side(i, u_scales[r : r + 1, :], d_scales[r : r + 1, :]) for r in at)
        for index, t in enumerate(near_runs(i)):
            parts = []
            for j in range(SPAN):
                rows = near_rows(i, index, j)
                parts.append(mix(terms[rows, :] * scale, prob_grads[rows, :], row_dot))
                mixed[rows, :] = parts[-1]
            at = pl.ds(start_of(links, i, t), SPAN * BLK)
            acc[at, :] += dot(jnp.concatenate(parts, axis=0), pair, ((1,), (0,)))
    factor = side_factor()
    first, second, u1, d1, u2, _, d2, _ = regions(position()[1])
    first_own[...] = acc[pl.ds(first, HALF), :] * factor
    second_own[...] = acc[pl.ds(second, HALF), :] * factor
    for target, at in ((u2_out, d2), (d2_out, u2), (u3_out, d1), (d3_out, u1)):
        target[...] = (acc[pl.ds(at, HALF), :] * factor).astype(BF)


def outputs_kernel(
    links, near_mixed, u_mixed, d_mixed, first_kv, second_kv, u1, d1, u2, u3, d2, d3,
    att_own, att_other, dq_out, win, att,
):
    side, flip, _, _ = position()
    for at, half in zip(regions(flip), (first_kv, second_kv, u1, d1, u2, u3, d2, d3)):
        win[pl.ds(at, HALF), :] = half[...]
    for i in range(GROUP):
        rows = slice(i * BLK, (i + 1) * BLK)
        out = dot(
            by_side(i, u_mixed[far_rows(i % 2), :], d_mixed[far_rows(i % 2), :]), win[pl.ds(start_of(links, i, far_run(i)), SPAN * BLK), :], ((0,), (0,))
        )
        for index, t in enumerate(near_runs(i)):
            part = near_mixed[near_rows(i, index, 0).start : near_rows(i, index, SPAN - 1).stop, :]
            out = out + dot(part, win[pl.ds(start_of(links, i, t), SPAN * BLK), :], ((0,), (0,)))
        att[rows, :] = out[BLK:, HD:].astype(BF)
        dq_out[rows, :] = (out[:BLK, :HD] * (HD ** -0.5)).astype(BF)
    att_own[...] = att[pl.ds(pl.multiple_of(side * HALF, HALF), HALF), :]
    att_other[...] = att[pl.ds(pl.multiple_of((1 - side) * HALF, HALF), HALF), :]


def spread(grads, w_mine, side, head, target):
    for step in range(2):
        out = dot(grads, weight_rows(w_mine, head ^ (2 * step), 2 * HD), ((1,), (1,))).astype(BF)
        for group in range(2):
            index = 2 * group + step
            part = jnp.where(side == group, out[:HALF], out[HALF:])
            target[index * HALF : (index + 1) * HALF, :] = part


def spread_send_kernel(first_own, second_own, from_d, from_u, dq, w_mine, send, grads):
    side, flip, _, head = position()
    first = first_own[...] + from_d[...].astype(F32)
    second = second_own[...] + from_u[...].astype(F32)
    grads[:, :HD] = dq[...]
    grads[:HALF, HD:] = jnp.where(flip == 1, first, second).astype(BF)
    grads[HALF:, HD:] = jnp.where(flip == 1, second, first).astype(BF)
    spread(grads[...], w_mine, side, head ^ 1, send)


def spread_keep_kernel(grads, w_mine, keep):
    side, _, _, head = position()
    spread(grads[...], w_mine, side, head, keep)


def body(features, w_qkv, block_links, d_out, n_ctx, n_head):
    n_group = n_ctx // 2

    def across(value, flip_ctx, flip_head):
        pairs = [
            (c * n_head + h, (c ^ flip_ctx) * n_head + (h ^ flip_head))
            for c in range(n_ctx)
            for h in range(n_head)
        ]
        return lax.ppermute(value, ("ctx", "head"), pairs)

    def chain(value, back):
        pairs = []
        for ctx in range(n_ctx):
            group, side = divmod(ctx, 2)
            for h in range(n_head):
                to = group + (1 if h % 2 == back else -1)
                inside = 0 <= to < n_group
                target = (2 * to + side) * n_head + h if inside else ctx * n_head + (h ^ 1)
                pairs.append((ctx * n_head + h, target))
        return lax.ppermute(value, ("ctx", "head"), pairs)

    f = features
    sx = across(f, 0, 2)
    sy = across(f, 1, 0)
    sd = across(f, 1, 2)
    w = jnp.transpose(w_qkv, (1, 0, 2))

    def call(kernel, name, outs, ins, mebibytes, flops, scratch=()):
        specs = [SMEM if v.dtype == jnp.int32 else VMEM for v in ins]
        if kernel is begin_kernel:
            specs = [pl.BlockSpec(memory_space=pltpu.HBM)] * 2
            ins = [pltpu.with_memory_space_constraint(v, pltpu.HBM) for v in ins]
        return pl.pallas_call(
            kernel,
            name=name,
            out_shape=outs,
            in_specs=specs,
            out_specs=[SMEM if v.dtype == jnp.int32 else VMEM for v in outs],
            scratch_shapes=list(scratch),
            **params(flops, 2 << 20, mebibytes),
        )(*ins)

    def out(rows, cols, kind=BF):
        return jax.ShapeDtypeStruct((rows, cols), kind)

    def held(rows, cols, kind=BF):
        return pltpu.VMEM((rows, cols), kind)

    product = 2 * ROWS * f.shape[1] * 3 * HD
    attention = 2 * GROUP * 9 * BLK * BLK * 2 * HD
    w_mine, fm, total = call(
        begin_kernel,
        "begin",
        [held(w.shape[1], 3 * HD), held(*f.shape), held(HALF, 3 * HD, F32)],
        (f, w),
        4,
        product,
        [pltpu.SemaphoreType.DMA((4,))],
    )
    (early,) = call(pack_kernel, "pack_early", [out(ROWS, f.shape[1])], (fm, sd), 4, 0)
    other_early = across(early, 0, 1)
    (late,) = call(pack_kernel, "pack_late", [out(ROWS, f.shape[1])], (sy, sx), 4, 0)
    other_late = across(late, 0, 1)
    (total,) = call(
        project_rest_kernel,
        "project_rest",
        [held(ROWS, 3 * HD, F32)],
        (total, early, late, other_early, w_mine),
        4,
        product,
    )
    first, second = call(
        project_kv_kernel, "project_kv", [out(HALF, 2 * HD)] * 2, (other_late, total, w_mine), 4, product
    )

    u1 = chain(first, 0)
    d1 = chain(second, 1)
    u2 = chain(second, 0)
    d2 = chain(first, 1)
    u3 = chain(u1, 0)
    d3 = chain(d1, 1)
    rows, slots = block_links.shape
    link_rows = jnp.pad(block_links.astype(BF), ((0, 16 - rows), (0, HD - slots)))
    (payload,) = call(payload_kernel, "payload", [out(HALF + 16, HD)], (d_out, link_rows, late), 4, 0)
    d_other = across(payload, 1, 0)
    (q,) = call(project_q_kernel, "project_q", [held(ROWS, HD)], (other_late, total, w_mine, u1, d1), 4, product)
    other_links = d_other[HALF : HALF + rows, :slots].astype(jnp.int32)
    (links,) = call(
        links_kernel, "links", [pltpu.SMEM((GROUP + 1, slots), jnp.int32)], (block_links, other_links, q), 4, 0
    )
    links = pltpu.with_memory_space_constraint(links, pltpu.SMEM)
    window = pltpu.VMEM((WINDOW * BLK, 2 * HD), BF)
    sums = pltpu.VMEM((WINDOW * BLK, 2 * HD), F32)
    run = SPAN * BLK
    pairs, terms, prob_grads, stats = call(
        near_scores_kernel,
        "near_scores",
        [
            held(GROUP * 2 * BLK, 2 * HD),
            held(GROUP * 2 * run, BLK, F32),
            held(GROUP * 2 * run, BLK, F32),
            held(GROUP * 3 * 8, BLK, F32),
        ],
        (links, q, first, second, u1, d1, u2, d2, d_out, d_other),
        6,
        attention,
        [window],
    )
    def far_grads(near, middle, far, after, which, name):
        return call(
            functools.partial(far_grads_kernel, chain=which),
            name,
            [
                held(GROUP // 2 * run, 2 * HD),
                held(OWN, 2 * HD, F32),
                out(HALF, 2 * HD),
                held(GROUP * 8, BLK, F32),
            ],
            (links, pairs, stats, near, middle, far, after),
            4,
            attention // 2,
            [pltpu.VMEM((OWN, 2 * HD), BF)],
        )

    u_mixed, u_edge, far_d_grad, u_scales = far_grads(u1, u2, u3, stats, 0, "far_grads_u")
    d_mixed, d_edge, far_u_grad, d_scales = far_grads(d1, d2, d3, far_d_grad, 1, "far_grads_d")
    near_mixed, first_own, second_own, u2_grad, d2_grad, u3_grad, d3_grad = call(
        near_grads_kernel,
        "near_grads",
        [held(GROUP * 2 * run, 2 * HD)] + [held(HALF, 2 * HD, F32)] * 2 + [out(HALF, 2 * HD)] * 4,
        (links, pairs, terms, prob_grads, u_scales, d_scales, u_edge, d_edge),
        4,
        attention,
        [sums],
    )
    att_own, att_other, dq = call(
        outputs_kernel,
        "outputs",
        [out(HALF, HD), out(HALF, HD), held(ROWS, HD)],
        (links, near_mixed, u_mixed, d_mixed, first, second, u1, d1, u2, u3, d2, d3),
        4,
        attention,
        [window, pltpu.VMEM((ROWS, HD), BF)],
    )

    back_d = chain(far_d_grad, 1)
    back_u = chain(far_u_grad, 0)
    d2_back = chain(d2_grad, 1)
    u2_back = chain(u2_grad, 0)

    def merge(one, two, name):
        return call(merge_kernel, name, [out(HALF, 2 * HD)], (one, two, dq), 4, 0)[0]

    from_d = chain(merge(d3_grad, back_d, "merge_d"), 1)
    from_u = chain(merge(u3_grad, back_u, "merge_u"), 0)
    first_own, second_own = call(
        gather_kernel, "gather", [held(HALF, 2 * HD, F32)] * 2, (first_own, second_own, d2_back, u2_back), 4, 0
    )
    send, grads = call(
        spread_send_kernel,
        "spread_send",
        [out(4 * HALF, 2 * HD), held(ROWS, 3 * HD)],
        (first_own, second_own, from_d, from_u, dq, w_mine),
        4,
        product,
    )
    (keep,) = call(spread_keep_kernel, "spread_keep", [held(4 * HALF, 2 * HD)], (grads, w_mine), 4, product)
    arrived = across(send, 0, 1)
    mine, to_x, to_y, to_d = call(
        chip_sum_kernel,
        "chip_sum",
        [out(HALF, 2 * HD)] * 2 + [out(HALF + BLK, 2 * HD), out(HALF, 2 * HD)],
        (keep, arrived, att_other),
        4,
        0,
    )
    gd = across(to_d, 1, 2)
    gy = across(to_y, 1, 0)
    gx = across(to_x, 0, 2)
    attended, grad_features = call(
        finish_kernel, "finish", [out(HALF, 2 * HD)] * 2, (mine, gd, gx, gy, att_own), 4, 0
    )
    return attended, grad_features


def solution(mesh):
    sizes = dict(mesh.shape)
    return jax.shard_map(
        functools.partial(body, n_ctx=sizes["ctx"], n_head=sizes["head"]),
        mesh=mesh,
        in_specs=(P("ctx", "head"), P(None, None, "head"), P("ctx", None), P("ctx", "head")),
        out_specs=(P("ctx", "head"), P("ctx", "head")),
        check_vma=False,
    )
```

```python
import functools

import jax
import jax.numpy as jnp
from jax import lax
from jax.experimental import pallas as pl
from jax.experimental.pallas import tpu as pltpu
from jax.sharding import PartitionSpec as P

HD = 128
BLK = 128
REACH = 6
SPAN = 3
LOG2E = 1.4426950408889634
DEAD = -1e30
BF = jnp.bfloat16
F32 = jnp.float32

GROUP = 4
ROWS = GROUP * BLK
HALF = ROWS // 2
WINDOW = GROUP + 2 * REACH
NEAR_LEFT = (REACH - GROUP) * BLK
OWN = REACH * BLK
NEAR_RIGHT = OWN + ROWS
FAR_RIGHT = NEAR_RIGHT + ROWS


def params(flops, moved, mebibytes):
    return dict(
        compiler_params=pltpu.CompilerParams(vmem_limit_bytes=mebibytes * 1024 * 1024),
        cost_estimate=pl.CostEstimate(flops=flops, bytes_accessed=moved, transcendentals=0),
    )


VMEM = pl.BlockSpec(memory_space=pltpu.VMEM)
SMEM = pl.BlockSpec(memory_space=pltpu.SMEM)


def dot(a, b, dims):
    return lax.dot_general(a, b, (dims, ((), ())), preferred_element_type=F32)


def position():
    ctx, head = lax.axis_index("ctx"), lax.axis_index("head")
    return ctx % 2, head % 2, ctx // 2 * GROUP, head


def begin_kernel(f, w, w_mine, fm, total, sems):
    side, _, _, head = position()
    copies = [pltpu.make_async_copy(f, fm, sems.at[3])]
    for g in range(3):
        cols = pl.ds(pl.multiple_of(side * HD, HD), HD)
        copies.append(pltpu.make_async_copy(w.at[g, :, cols], w_mine.at[:, pl.ds(g * HD, HD)], sems.at[g]))
    for copy in copies:
        copy.start()
    for copy in copies:
        copy.wait()
    total[...] = dot(fm[...], weight_rows(w_mine, head, fm.shape[1]), ((1,), (0,)))


def weight_rows(w_mine, source, width):
    return w_mine[pl.ds(pl.multiple_of(source * width, width), width), :]


def pack_kernel(one, two, out):
    out[:HALF, :] = one[...]
    out[HALF:, :] = two[...]


def project_rest_kernel(before, early, late, other_early, w_mine, total):
    head = position()[3]
    width = early.shape[1]
    mine, across_x, sibling, across_both = (weight_rows(w_mine, head ^ k, width) for k in (0, 2, 1, 3))
    own = before[...] + dot(late[HALF:, :], across_x, ((1,), (0,)))
    total[:HALF, :] = own + dot(other_early[:HALF, :], sibling, ((1,), (0,)))
    partner = dot(late[:HALF, :], mine, ((1,), (0,))) + dot(early[HALF:, :], across_x, ((1,), (0,)))
    total[HALF:, :] = partner + dot(other_early[HALF:, :], across_both, ((1,), (0,)))


def last_product(head, other_late, w_mine, cols, group):
    width = other_late.shape[1]
    rows = pl.ds(pl.multiple_of((head ^ (3 if group == 0 else 1)) * width, width), width)
    piece = other_late[HALF:, :] if group == 0 else other_late[:HALF, :]
    return dot(piece, w_mine[rows, cols], ((1,), (0,)))


def project_kv_kernel(other_late, before, w_mine, first_out, second_out):
    side, flip, _, head = position()
    own, partner = (
        (before[g * HALF : (g + 1) * HALF, HD:] + last_product(head, other_late, w_mine, slice(HD, 3 * HD), g)).astype(BF)
        for g in range(2)
    )
    near_first = side ^ (1 - flip) == 0
    first_out[...] = jnp.where(near_first, own, partner)
    second_out[...] = jnp.where(near_first, partner, own)


def merge_kernel(one, two, out):
    out[...] = (one[...].astype(F32) + two[...].astype(F32)).astype(BF)


def gather_kernel(first_own, second_own, d, u, first_out, second_out):
    first_out[...] = first_own[...] + u[...].astype(F32)
    second_out[...] = second_own[...] + d[...].astype(F32)


def chip_sum_near_kernel(keep, arrived, att_other, mine, to_y):
    total = (keep[...].astype(F32) + arrived[...].astype(F32)).astype(BF)
    mine[...] = total[:HALF]
    to_y[:HALF, :] = total[HALF:]
    for half in range(2):
        to_y[HALF:, half * HD : (half + 1) * HD] = att_other[half * BLK : (half + 1) * BLK, :]


def chip_sum_far_kernel(keep, arrived, to_x, to_d):
    total = (keep[...].astype(F32) + arrived[...].astype(F32)).astype(BF)
    to_x[...] = total[:HALF]
    to_d[...] = total[HALF:]


def finish_kernel(mine, gd, gx, from_y, att_own, attended, grad_features):
    total = mine[...].astype(F32) + gd[...].astype(F32) + gx[...].astype(F32) + from_y[:HALF, :].astype(F32)
    grad_features[...] = total.astype(BF)
    side = position()[0]
    att_other = jnp.concatenate([from_y[HALF:, :HD], from_y[HALF:, HD:]], axis=0)
    for half in range(2):
        cols = slice(half * HD, (half + 1) * HD)
        attended[:, cols] = jnp.where(side == half, att_own[...], att_other)


def project_q_kernel(other_late, before, w_mine, u1, d1, q_out):
    del u1, d1
    side, _, _, head = position()
    for g in range(2):
        part = before[g * HALF : (g + 1) * HALF, :HD] + last_product(head, other_late, w_mine, slice(0, HD), g)
        q_out[pl.ds(pl.multiple_of((side ^ g) * HALF, HALF), HALF), :] = part.astype(BF)


def payload_kernel(d_own, link_rows, late, payload):
    del late
    side = position()[0]
    payload[:HALF, :] = jnp.where(side == 0, d_own[:, HD:], d_own[:, :HD])
    payload[HALF:, :] = link_rows[...]


def links_kernel(own, other, q, links):
    del q
    side, _, first, _ = position()
    for i in range(GROUP):
        for k in range(3 * SPAN):
            links[i, k] = jnp.where(side == i // 2, own[i % 2, k], other[i % 2, k])
        for t in (1, 2):
            base = jnp.int32(-(1 << 20))
            for j in range(SPAN):
                entry = links[i, SPAN * t + j]
                base = jnp.maximum(base, jnp.where(entry >= 0, entry - j, -(1 << 20)))
            base = jnp.where(base > -(1 << 19), base - first + REACH, i + 1 if t == 1 else i + REACH + SPAN)
            lowest = i if t == 1 else i + REACH + SPAN - 1
            links[GROUP, 2 * i + t - 1] = jnp.clip(base, lowest, lowest + 2) * BLK


def regions(flip):
    left_lo, left_hi = NEAR_LEFT, NEAR_LEFT + HALF
    right_lo, right_hi = NEAR_RIGHT, NEAR_RIGHT + HALF
    pick = lambda plain, flipped: pl.multiple_of((1 - flip) * plain + flip * flipped, HALF)
    return (
        pick(OWN + HALF, OWN),
        pick(OWN, OWN + HALF),
        pick(left_hi, right_lo),
        pick(right_lo, left_hi),
        pick(left_lo, right_hi),
        pick(0, FAR_RIGHT),
        pick(right_hi, left_lo),
        pick(FAR_RIGHT, 0),
    )


def start_of(links, i, t):
    if t == 0:
        return (REACH + i - 1) * BLK
    return pl.multiple_of(links[GROUP, 2 * i + t - 1], BLK)


def far_run(i):
    return 1 if i < GROUP // 2 else 2


def near_runs(i):
    return tuple(t for t in range(3) if t != far_run(i))


def near_rows(i, index, j):
    first = ((2 * i + index) * SPAN + j) * BLK
    return slice(first, first + BLK)


def far_rows(i):
    return slice(i * SPAN * BLK, (i + 1) * SPAN * BLK)


def run_scores(links, rows, pair, i, t):
    product = dot(rows, pair, ((1,), (1,)))
    blocks = []
    for j in range(SPAN):
        block = product[j * BLK : (j + 1) * BLK]
        bias = jnp.where(links[i, SPAN * t + j] >= 0, 0.0, DEAD).astype(F32)
        blocks.append((block[:, :BLK], block[:, BLK:], bias))
    return blocks


def fold(block):
    return block.reshape(BLK // 8, 8, BLK)


def largest_of(blocks):
    best = None
    for score, _, bias in blocks:
        peak = jnp.max(fold(score), axis=0) + bias
        best = peak if best is None else jnp.maximum(best, peak)
    return jnp.max(best, axis=0, keepdims=True)


def exponentials(blocks, largest):
    terms = []
    total = jnp.zeros((8, BLK), F32)
    weighted = jnp.zeros((8, BLK), F32)
    for score, prob_grad, bias in blocks:
        term = jnp.exp2((score - (largest - bias)) * (HD ** -0.5 * LOG2E))
        terms.append(term)
        total = total + jnp.sum(fold(term), axis=0)
        weighted = weighted + jnp.sum(fold(term * prob_grad), axis=0)
    return terms, jnp.sum(total, axis=0, keepdims=True), jnp.sum(weighted, axis=0, keepdims=True)


def mix(share, prob_grad, row_dot):
    grad = share * (prob_grad - row_dot)
    return jnp.concatenate([grad.astype(BF), share.astype(BF)], axis=1)


def side_factor():
    scale = HD ** -0.5
    return jnp.where(lax.broadcasted_iota(jnp.int32, (1, 2 * HD), 1) < HD, scale, 1.0).astype(F32)


def near_scores_kernel(
    links, q, first_kv, second_kv, u1, d1, u2, d2, d_own, d_other,
    pairs, terms_out, prob_grads_out, stats, win,
):
    side, flip, _, _ = position()
    places = regions(flip)
    for at, half in zip(places[:5] + places[6:7], (first_kv, second_kv, u1, d1, u2, d2)):
        win[pl.ds(at, HALF), :] = half[...]
    zeros = jnp.zeros((BLK, HD), BF)
    own_cols = pl.ds(pl.multiple_of(side * HD, HD), HD)
    for i in range(GROUP):
        rows = slice(i * BLK, (i + 1) * BLK)
        here = slice((i % 2) * BLK, (i % 2 + 1) * BLK)
        d_blk = jnp.where(side == i // 2, d_own[here, own_cols], d_other[here, :])
        pair = jnp.concatenate(
            [
                jnp.concatenate([q[rows, :], zeros], axis=1),
                jnp.concatenate([zeros, d_blk], axis=1),
            ],
            axis=0,
        )
        pairs[2 * i * BLK : 2 * (i + 1) * BLK, :] = pair
        blocks = []
        for t in near_runs(i):
            blocks += run_scores(links, win[pl.ds(start_of(links, i, t), SPAN * BLK), :], pair, i, t)
        largest = largest_of(blocks)
        terms, total, weighted = exponentials(blocks, largest)
        for n, term in enumerate(terms):
            terms_out[near_rows(i, 0, n), :] = term
            prob_grads_out[near_rows(i, 0, n), :] = blocks[n][1]
        for n, row in enumerate((largest, total, weighted)):
            stats[8 * (3 * i + n) : 8 * (3 * i + n + 1), :] = jnp.broadcast_to(row, (8, BLK))


def far_grads_kernel(links, pairs, stats, near, middle, far, after, mixed, edge, far_out, scales, win, chain):
    del after
    flip = position()[1]
    right = flip if chain == 0 else 1 - flip
    at_far = pl.multiple_of(right * ROWS, HALF)
    win[pl.ds(at_far, HALF), :] = far[...]
    win[HALF : 2 * HALF, :] = middle[...]
    win[pl.ds(pl.multiple_of(ROWS - right * ROWS, HALF), HALF), :] = near[...]
    edge[...] = jnp.zeros_like(edge)
    scale = HD ** -0.5 * LOG2E
    span = range(GROUP // 2)
    query = [2 * right + k for k in span]
    starts = [
        pl.multiple_of(links[GROUP, 2 * query[k] + right] - right * NEAR_RIGHT, BLK) for k in span
    ]
    pair = [pairs[pl.ds(pl.multiple_of(2 * query[k] * BLK, 2 * BLK), 2 * BLK), :] for k in span]
    known = [
        [stats[pl.ds(pl.multiple_of(8 * (3 * query[k] + n), 8), 8), :][:1] for n in range(3)] for k in span
    ]
    blocks = [
        run_scores(links, win[pl.ds(starts[k], SPAN * BLK), :], pair[k], query[k], 1 + right) for k in span
    ]
    largest = [jnp.maximum(known[k][0], largest_of(blocks[k])) for k in span]
    found = [exponentials(blocks[k], largest[k]) for k in span]
    parts = []
    for k in span:
        terms, total, weighted = found[k]
        near_scale = jnp.exp2((known[k][0] - largest[k]) * scale)
        inverse = 1.0 / (total + near_scale * known[k][1])
        row_dot = (weighted + near_scale * known[k][2]) * inverse
        for n, row in enumerate((near_scale * inverse, row_dot)):
            scales[8 * (2 * k + n) : 8 * (2 * k + n + 1), :] = jnp.broadcast_to(row, (8, BLK))
        parts.append(
            jnp.concatenate([mix(term * inverse, block[1], row_dot) for term, block in zip(terms, blocks[k])], axis=0)
        )
    for k in span:
        mixed[far_rows(k), :] = parts[k]
        edge[pl.ds(starts[k], SPAN * BLK), :] += dot(parts[k], pair[k], ((1,), (0,)))
    far_out[...] = (edge[pl.ds(at_far, HALF), :] * side_factor()).astype(BF)


def by_side(i, from_u, from_d):
    left = i < GROUP // 2
    return jnp.where((position()[1] == 0) == left, from_u, from_d)


def near_grads_kernel(
    links, pairs, terms, prob_grads, u_scales, d_scales, u_edge, d_edge, mixed, first_own, second_own,
    u2_out, d2_out, u3_out, d3_out, acc,
):
    acc[NEAR_LEFT:OWN, :] = by_side(0, u_edge[NEAR_LEFT:OWN, :], d_edge[NEAR_LEFT:OWN, :])
    acc[OWN:NEAR_RIGHT, :] = jnp.zeros((ROWS, 2 * HD), F32)
    acc[NEAR_RIGHT:FAR_RIGHT, :] = by_side(GROUP - 1, u_edge[:ROWS, :], d_edge[:ROWS, :])
    for i in range(GROUP):
        pair = pairs[2 * i * BLK : 2 * (i + 1) * BLK, :]
        at = [8 * (2 * (i % 2) + n) for n in range(2)]
        scale, row_dot = (by_side(i, u_scales[r : r + 1, :], d_scales[r : r + 1, :]) for r in at)
        for index, t in enumerate(near_runs(i)):
            parts = []
            for j in range(SPAN):
                rows = near_rows(i, index, j)
                parts.append(mix(terms[rows, :] * scale, prob_grads[rows, :], row_dot))
                mixed[rows, :] = parts[-1]
            at = pl.ds(start_of(links, i, t), SPAN * BLK)
            acc[at, :] += dot(jnp.concatenate(parts, axis=0), pair, ((1,), (0,)))
    factor = side_factor()
    first, second, u1, d1, u2, _, d2, _ = regions(position()[1])
    first_own[...] = acc[pl.ds(first, HALF), :] * factor
    second_own[...] = acc[pl.ds(second, HALF), :] * factor
    for target, at in ((u2_out, d2), (d2_out, u2), (u3_out, d1), (d3_out, u1)):
        target[...] = (acc[pl.ds(at, HALF), :] * factor).astype(BF)


def outputs_kernel(
    links, near_mixed, u_mixed, d_mixed, first_kv, second_kv, u1, d1, u2, u3, d2, d3,
    att_own, att_other, dq_out, win, att,
):
    side, flip, _, _ = position()
    for at, half in zip(regions(flip), (first_kv, second_kv, u1, d1, u2, u3, d2, d3)):
        win[pl.ds(at, HALF), :] = half[...]
    for i in range(GROUP):
        rows = slice(i * BLK, (i + 1) * BLK)
        out = dot(
            by_side(i, u_mixed[far_rows(i % 2), :], d_mixed[far_rows(i % 2), :]), win[pl.ds(start_of(links, i, far_run(i)), SPAN * BLK), :], ((0,), (0,))
        )
        for index, t in enumerate(near_runs(i)):
            part = near_mixed[near_rows(i, index, 0).start : near_rows(i, index, SPAN - 1).stop, :]
            out = out + dot(part, win[pl.ds(start_of(links, i, t), SPAN * BLK), :], ((0,), (0,)))
        att[rows, :] = out[BLK:, HD:].astype(BF)
        dq_out[rows, :] = (out[:BLK, :HD] * (HD ** -0.5)).astype(BF)
    att_own[...] = att[pl.ds(pl.multiple_of(side * HALF, HALF), HALF), :]
    att_other[...] = att[pl.ds(pl.multiple_of((1 - side) * HALF, HALF), HALF), :]


def spread(grads, w_mine, side, head, target):
    out = dot(grads, weight_rows(w_mine, head, 2 * HD), ((1,), (1,))).astype(BF)
    target[:HALF, :] = jnp.where(side == 0, out[:HALF], out[HALF:])
    target[HALF:, :] = jnp.where(side == 0, out[HALF:], out[:HALF])


def spread_near_kernel(first_own, second_own, from_d, from_u, dq, w_mine, send, grads):
    side, flip, _, head = position()
    first = first_own[...] + from_d[...].astype(F32)
    second = second_own[...] + from_u[...].astype(F32)
    grads[:, :HD] = dq[...]
    grads[:HALF, HD:] = jnp.where(flip == 1, first, second).astype(BF)
    grads[HALF:, HD:] = jnp.where(flip == 1, second, first).astype(BF)
    spread(grads[...], w_mine, side, head ^ 1, send)


def spread_far_kernel(grads, w_mine, send):
    side, _, _, head = position()
    spread(grads[...], w_mine, side, head ^ 3, send)


def spread_keep_kernel(grads, w_mine, near, far):
    side, _, _, head = position()
    spread(grads[...], w_mine, side, head, near)
    spread(grads[...], w_mine, side, head ^ 2, far)


def body(features, w_qkv, block_links, d_out, n_ctx, n_head):
    n_group = n_ctx // 2

    def across(value, flip_ctx, flip_head):
        pairs = [
            (c * n_head + h, (c ^ flip_ctx) * n_head + (h ^ flip_head))
            for c in range(n_ctx)
            for h in range(n_head)
        ]
        return lax.ppermute(value, ("ctx", "head"), pairs)

    def chain(value, back):
        pairs = []
        for ctx in range(n_ctx):
            group, side = divmod(ctx, 2)
            for h in range(n_head):
                to = group + (1 if h % 2 == back else -1)
                inside = 0 <= to < n_group
                target = (2 * to + side) * n_head + h if inside else ctx * n_head + (h ^ 1)
                pairs.append((ctx * n_head + h, target))
        return lax.ppermute(value, ("ctx", "head"), pairs)

    f = features
    sx = across(f, 0, 2)
    sy = across(f, 1, 0)
    sd = across(f, 1, 2)
    w = jnp.transpose(w_qkv, (1, 0, 2))

    def call(kernel, name, outs, ins, mebibytes, flops, scratch=()):
        specs = [SMEM if v.dtype == jnp.int32 else VMEM for v in ins]
        if kernel is begin_kernel:
            specs = [pl.BlockSpec(memory_space=pltpu.HBM)] * 2
            ins = [pltpu.with_memory_space_constraint(v, pltpu.HBM) for v in ins]
        return pl.pallas_call(
            kernel,
            name=name,
            out_shape=outs,
            in_specs=specs,
            out_specs=[SMEM if v.dtype == jnp.int32 else VMEM for v in outs],
            scratch_shapes=list(scratch),
            **params(flops, 2 << 20, mebibytes),
        )(*ins)

    def out(rows, cols, kind=BF):
        return jax.ShapeDtypeStruct((rows, cols), kind)

    def held(rows, cols, kind=BF):
        return pltpu.VMEM((rows, cols), kind)

    product = 2 * ROWS * f.shape[1] * 3 * HD
    attention = 2 * GROUP * 9 * BLK * BLK * 2 * HD
    w_mine, fm, total = call(
        begin_kernel,
        "begin",
        [held(w.shape[1], 3 * HD), held(*f.shape), held(HALF, 3 * HD, F32)],
        (f, w),
        4,
        product,
        [pltpu.SemaphoreType.DMA((4,))],
    )
    (early,) = call(pack_kernel, "pack_early", [out(ROWS, f.shape[1])], (fm, sd), 4, 0)
    other_early = across(early, 0, 1)
    (late,) = call(pack_kernel, "pack_late", [out(ROWS, f.shape[1])], (sy, sx), 4, 0)
    other_late = across(late, 0, 1)
    (total,) = call(
        project_rest_kernel,
        "project_rest",
        [held(ROWS, 3 * HD, F32)],
        (total, early, late, other_early, w_mine),
        4,
        product,
    )
    first, second = call(
        project_kv_kernel, "project_kv", [out(HALF, 2 * HD)] * 2, (other_late, total, w_mine), 4, product
    )

    u1 = chain(first, 0)
    d1 = chain(second, 1)
    u2 = chain(second, 0)
    d2 = chain(first, 1)
    u3 = chain(u1, 0)
    d3 = chain(d1, 1)
    rows, slots = block_links.shape
    link_rows = jnp.pad(block_links.astype(BF), ((0, 16 - rows), (0, HD - slots)))
    (payload,) = call(payload_kernel, "payload", [out(HALF + 16, HD)], (d_out, link_rows, late), 4, 0)
    d_other = across(payload, 1, 0)
    (q,) = call(project_q_kernel, "project_q", [held(ROWS, HD)], (other_late, total, w_mine, u1, d1), 4, product)
    other_links = d_other[HALF : HALF + rows, :slots].astype(jnp.int32)
    (links,) = call(
        links_kernel, "links", [pltpu.SMEM((GROUP + 1, slots), jnp.int32)], (block_links, other_links, q), 4, 0
    )
    links = pltpu.with_memory_space_constraint(links, pltpu.SMEM)
    window = pltpu.VMEM((WINDOW * BLK, 2 * HD), BF)
    sums = pltpu.VMEM((WINDOW * BLK, 2 * HD), F32)
    run = SPAN * BLK
    pairs, terms, prob_grads, stats = call(
        near_scores_kernel,
        "near_scores",
        [
            held(GROUP * 2 * BLK, 2 * HD),
            held(GROUP * 2 * run, BLK, F32),
            held(GROUP * 2 * run, BLK, F32),
            held(GROUP * 3 * 8, BLK, F32),
        ],
        (links, q, first, second, u1, d1, u2, d2, d_out, d_other),
        6,
        attention,
        [window],
    )
    def far_grads(near, middle, far, after, which, name):
        return call(
            functools.partial(far_grads_kernel, chain=which),
            name,
            [
                held(GROUP // 2 * run, 2 * HD),
                held(OWN, 2 * HD, F32),
                out(HALF, 2 * HD),
                held(GROUP * 8, BLK, F32),
            ],
            (links, pairs, stats, near, middle, far, after),
            4,
            attention // 2,
            [pltpu.VMEM((OWN, 2 * HD), BF)],
        )

    u_mixed, u_edge, far_d_grad, u_scales = far_grads(u1, u2, u3, stats, 0, "far_grads_u")
    d_mixed, d_edge, far_u_grad, d_scales = far_grads(d1, d2, d3, far_d_grad, 1, "far_grads_d")
    near_mixed, first_own, second_own, u2_grad, d2_grad, u3_grad, d3_grad = call(
        near_grads_kernel,
        "near_grads",
        [held(GROUP * 2 * run, 2 * HD)] + [held(HALF, 2 * HD, F32)] * 2 + [out(HALF, 2 * HD)] * 4,
        (links, pairs, terms, prob_grads, u_scales, d_scales, u_edge, d_edge),
        4,
        attention,
        [sums],
    )
    att_own, att_other, dq = call(
        outputs_kernel,
        "outputs",
        [out(HALF, HD), out(HALF, HD), held(ROWS, HD)],
        (links, near_mixed, u_mixed, d_mixed, first, second, u1, d1, u2, u3, d2, d3),
        4,
        attention,
        [window, pltpu.VMEM((ROWS, HD), BF)],
    )

    back_d = chain(far_d_grad, 1)
    back_u = chain(far_u_grad, 0)
    d2_back = chain(d2_grad, 1)
    u2_back = chain(u2_grad, 0)

    def merge(one, two, name):
        return call(merge_kernel, name, [out(HALF, 2 * HD)], (one, two), 4, 0)[0]

    from_d = chain(merge(d3_grad, back_d, "merge_d"), 1)
    from_u = chain(merge(u3_grad, back_u, "merge_u"), 0)
    first_own, second_own = call(
        gather_kernel, "gather", [held(HALF, 2 * HD, F32)] * 2, (first_own, second_own, d2_back, u2_back), 4, 0
    )
    near_send, grads = call(
        spread_near_kernel,
        "spread_near",
        [out(ROWS, 2 * HD), held(ROWS, 3 * HD)],
        (first_own, second_own, from_d, from_u, dq, w_mine),
        4,
        product,
    )
    near_arrived = across(near_send, 0, 1)
    (far_send,) = call(spread_far_kernel, "spread_far", [out(ROWS, 2 * HD)], (grads, w_mine), 4, product)
    far_arrived = across(far_send, 0, 1)
    near, far = call(spread_keep_kernel, "spread_keep", [held(ROWS, 2 * HD)] * 2, (grads, w_mine), 4, product)
    mine, to_y = call(
        chip_sum_near_kernel,
        "chip_sum_near",
        [out(HALF, 2 * HD), out(HALF + BLK, 2 * HD)],
        (near, near_arrived, att_other),
        4,
        0,
    )
    gy = across(to_y, 1, 0)
    to_x, to_d = call(chip_sum_far_kernel, "chip_sum_far", [out(HALF, 2 * HD)] * 2, (far, far_arrived), 4, 0)
    gd = across(to_d, 1, 2)
    gx = across(to_x, 0, 2)
    attended, grad_features = call(
        finish_kernel, "finish", [out(HALF, 2 * HD)] * 2, (mine, gd, gx, gy, att_own), 4, 0
    )
    return attended, grad_features


def solution(mesh):
    sizes = dict(mesh.shape)
    return jax.shard_map(
        functools.partial(body, n_ctx=sizes["ctx"], n_head=sizes["head"]),
        mesh=mesh,
        in_specs=(P("ctx", "head"), P(None, None, "head"), P("ctx", None), P("ctx", "head")),
        out_specs=(P("ctx", "head"), P("ctx", "head")),
        check_vma=False,
    )
```

```python
import functools

import jax
import jax.numpy as jnp
from jax import lax
from jax.experimental import pallas as pl
from jax.experimental.pallas import tpu as pltpu
from jax.sharding import PartitionSpec as P

HD = 128
BLK = 128
REACH = 6
SPAN = 3
LOG2E = 1.4426950408889634
DEAD = -1e30
BF = jnp.bfloat16
F32 = jnp.float32

GROUP = 4
ROWS = GROUP * BLK
HALF = ROWS // 2
WINDOW = GROUP + 2 * REACH
NEAR_LEFT = (REACH - GROUP) * BLK
OWN = REACH * BLK
NEAR_RIGHT = OWN + ROWS
FAR_RIGHT = NEAR_RIGHT + ROWS


def params(flops, moved, mebibytes):
    return dict(
        compiler_params=pltpu.CompilerParams(vmem_limit_bytes=mebibytes * 1024 * 1024),
        cost_estimate=pl.CostEstimate(flops=flops, bytes_accessed=moved, transcendentals=0),
    )


VMEM = pl.BlockSpec(memory_space=pltpu.VMEM)
SMEM = pl.BlockSpec(memory_space=pltpu.SMEM)


def dot(a, b, dims):
    return lax.dot_general(a, b, (dims, ((), ())), preferred_element_type=F32)


def position():
    ctx, head = lax.axis_index("ctx"), lax.axis_index("head")
    return ctx % 2, head % 2, ctx // 2 * GROUP, head


def begin_kernel(f, w, w_mine, fm, total, sems):
    side, _, _, head = position()
    copies = [pltpu.make_async_copy(f, fm, sems.at[3])]
    for g in range(3):
        cols = pl.ds(pl.multiple_of(side * HD, HD), HD)
        copies.append(pltpu.make_async_copy(w.at[g, :, cols], w_mine.at[:, pl.ds(g * HD, HD)], sems.at[g]))
    for copy in copies:
        copy.start()
    for copy in copies:
        copy.wait()
    total[...] = dot(fm[...], weight_rows(w_mine, head, fm.shape[1]), ((1,), (0,)))


def weight_rows(w_mine, source, width):
    return w_mine[pl.ds(pl.multiple_of(source * width, width), width), :]


def pack_kernel(one, two, out):
    out[:HALF, :] = one[...]
    out[HALF:, :] = two[...]


def project_rest_kernel(before, early, late, other_early, w_mine, total):
    head = position()[3]
    width = early.shape[1]
    mine, across_x, sibling, across_both = (weight_rows(w_mine, head ^ k, width) for k in (0, 2, 1, 3))
    own = before[...] + dot(late[HALF:, :], across_x, ((1,), (0,)))
    total[:HALF, :] = own + dot(other_early[:HALF, :], sibling, ((1,), (0,)))
    partner = dot(late[:HALF, :], mine, ((1,), (0,))) + dot(early[HALF:, :], across_x, ((1,), (0,)))
    total[HALF:, :] = partner + dot(other_early[HALF:, :], across_both, ((1,), (0,)))


def last_product(head, other_late, w_mine, cols, group):
    width = other_late.shape[1]
    rows = pl.ds(pl.multiple_of((head ^ (3 if group == 0 else 1)) * width, width), width)
    piece = other_late[HALF:, :] if group == 0 else other_late[:HALF, :]
    return dot(piece, w_mine[rows, cols], ((1,), (0,)))


def project_kv_kernel(other_late, before, w_mine, first_out, second_out):
    side, flip, _, head = position()
    own, partner = (
        (before[g * HALF : (g + 1) * HALF, HD:] + last_product(head, other_late, w_mine, slice(HD, 3 * HD), g)).astype(BF)
        for g in range(2)
    )
    near_first = side ^ (1 - flip) == 0
    first_out[...] = jnp.where(near_first, own, partner)
    second_out[...] = jnp.where(near_first, partner, own)


def merge_kernel(one, two, out):
    out[...] = (one[...].astype(F32) + two[...].astype(F32)).astype(BF)


def gather_kernel(first_own, second_own, d, u, first_out, second_out):
    first_out[...] = first_own[...] + u[...].astype(F32)
    second_out[...] = second_own[...] + d[...].astype(F32)


def chip_sum_near_kernel(keep, arrived, att_other, mine, to_y):
    total = (keep[...].astype(F32) + arrived[...].astype(F32)).astype(BF)
    mine[...] = total[:HALF]
    to_y[:HALF, :] = total[HALF:]
    for half in range(2):
        to_y[HALF:, half * HD : (half + 1) * HD] = att_other[half * BLK : (half + 1) * BLK, :]


def chip_sum_far_kernel(keep, arrived, to_x, to_d):
    total = (keep[...].astype(F32) + arrived[...].astype(F32)).astype(BF)
    to_x[...] = total[:HALF]
    to_d[...] = total[HALF:]


def finish_kernel(mine, gx, gd, from_y, att_own, attended, grad_features):
    total = mine[...].astype(F32) + gd[...].astype(F32) + gx[...].astype(F32) + from_y[:HALF, :].astype(F32)
    grad_features[...] = total.astype(BF)
    side = position()[0]
    att_other = jnp.concatenate([from_y[HALF:, :HD], from_y[HALF:, HD:]], axis=0)
    for half in range(2):
        cols = slice(half * HD, (half + 1) * HD)
        attended[:, cols] = jnp.where(side == half, att_own[...], att_other)


def project_q_kernel(other_late, before, w_mine, u1, d1, q_out):
    del u1, d1
    side, _, _, head = position()
    for g in range(2):
        part = before[g * HALF : (g + 1) * HALF, :HD] + last_product(head, other_late, w_mine, slice(0, HD), g)
        q_out[pl.ds(pl.multiple_of((side ^ g) * HALF, HALF), HALF), :] = part.astype(BF)


def payload_kernel(d_own, link_rows, late, payload):
    del late
    side = position()[0]
    payload[:HALF, :] = jnp.where(side == 0, d_own[:, HD:], d_own[:, :HD])
    payload[HALF:, :] = link_rows[...]


def links_kernel(own, other, q, links):
    del q
    side, _, first, _ = position()
    for i in range(GROUP):
        for k in range(3 * SPAN):
            links[i, k] = jnp.where(side == i // 2, own[i % 2, k], other[i % 2, k])
        for t in (1, 2):
            base = jnp.int32(-(1 << 20))
            for j in range(SPAN):
                entry = links[i, SPAN * t + j]
                base = jnp.maximum(base, jnp.where(entry >= 0, entry - j, -(1 << 20)))
            base = jnp.where(base > -(1 << 19), base - first + REACH, i + 1 if t == 1 else i + REACH + SPAN)
            lowest = i if t == 1 else i + REACH + SPAN - 1
            links[GROUP, 2 * i + t - 1] = jnp.clip(base, lowest, lowest + 2) * BLK


def regions(flip):
    left_lo, left_hi = NEAR_LEFT, NEAR_LEFT + HALF
    right_lo, right_hi = NEAR_RIGHT, NEAR_RIGHT + HALF
    pick = lambda plain, flipped: pl.multiple_of((1 - flip) * plain + flip * flipped, HALF)
    return (
        pick(OWN + HALF, OWN),
        pick(OWN, OWN + HALF),
        pick(left_hi, right_lo),
        pick(right_lo, left_hi),
        pick(left_lo, right_hi),
        pick(0, FAR_RIGHT),
        pick(right_hi, left_lo),
        pick(FAR_RIGHT, 0),
    )


def start_of(links, i, t):
    if t == 0:
        return (REACH + i - 1) * BLK
    return pl.multiple_of(links[GROUP, 2 * i + t - 1], BLK)


def far_run(i):
    return 1 if i < GROUP // 2 else 2


def near_runs(i):
    return tuple(t for t in range(3) if t != far_run(i))


def near_rows(i, index, j):
    first = ((2 * i + index) * SPAN + j) * BLK
    return slice(first, first + BLK)


def far_rows(i):
    return slice(i * SPAN * BLK, (i + 1) * SPAN * BLK)


def run_scores(links, rows, pair, i, t):
    product = dot(rows, pair, ((1,), (1,)))
    blocks = []
    for j in range(SPAN):
        block = product[j * BLK : (j + 1) * BLK]
        bias = jnp.where(links[i, SPAN * t + j] >= 0, 0.0, DEAD).astype(F32)
        blocks.append((block[:, :BLK], block[:, BLK:], bias))
    return blocks


def fold(block):
    return block.reshape(BLK // 8, 8, BLK)


def largest_of(blocks):
    best = None
    for score, _, bias in blocks:
        peak = jnp.max(fold(score), axis=0) + bias
        best = peak if best is None else jnp.maximum(best, peak)
    return jnp.max(best, axis=0, keepdims=True)


def exponentials(blocks, largest):
    terms = []
    total = jnp.zeros((8, BLK), F32)
    weighted = jnp.zeros((8, BLK), F32)
    for score, prob_grad, bias in blocks:
        term = jnp.exp2((score - (largest - bias)) * (HD ** -0.5 * LOG2E))
        terms.append(term)
        total = total + jnp.sum(fold(term), axis=0)
        weighted = weighted + jnp.sum(fold(term * prob_grad), axis=0)
    return terms, jnp.sum(total, axis=0, keepdims=True), jnp.sum(weighted, axis=0, keepdims=True)


def mix(share, prob_grad, row_dot):
    grad = share * (prob_grad - row_dot)
    return jnp.concatenate([grad.astype(BF), share.astype(BF)], axis=1)


def side_factor():
    scale = HD ** -0.5
    return jnp.where(lax.broadcasted_iota(jnp.int32, (1, 2 * HD), 1) < HD, scale, 1.0).astype(F32)


def near_scores_kernel(
    links, q, first_kv, second_kv, u1, d1, u2, d2, d_own, d_other,
    pairs, terms_out, prob_grads_out, stats, win,
):
    side, flip, _, _ = position()
    places = regions(flip)
    for at, half in zip(places[:5] + places[6:7], (first_kv, second_kv, u1, d1, u2, d2)):
        win[pl.ds(at, HALF), :] = half[...]
    zeros = jnp.zeros((BLK, HD), BF)
    own_cols = pl.ds(pl.multiple_of(side * HD, HD), HD)
    for i in range(GROUP):
        rows = slice(i * BLK, (i + 1) * BLK)
        here = slice((i % 2) * BLK, (i % 2 + 1) * BLK)
        d_blk = jnp.where(side == i // 2, d_own[here, own_cols], d_other[here, :])
        pair = jnp.concatenate(
            [
                jnp.concatenate([q[rows, :], zeros], axis=1),
                jnp.concatenate([zeros, d_blk], axis=1),
            ],
            axis=0,
        )
        pairs[2 * i * BLK : 2 * (i + 1) * BLK, :] = pair
        blocks = []
        for t in near_runs(i):
            blocks += run_scores(links, win[pl.ds(start_of(links, i, t), SPAN * BLK), :], pair, i, t)
        largest = largest_of(blocks)
        terms, total, weighted = exponentials(blocks, largest)
        for n, term in enumerate(terms):
            terms_out[near_rows(i, 0, n), :] = term
            prob_grads_out[near_rows(i, 0, n), :] = blocks[n][1]
        for n, row in enumerate((largest, total, weighted)):
            stats[8 * (3 * i + n) : 8 * (3 * i + n + 1), :] = jnp.broadcast_to(row, (8, BLK))


def far_grads_kernel(links, pairs, stats, near, middle, far, after, mixed, edge, far_out, scales, win, chain):
    del after
    flip = position()[1]
    right = flip if chain == 0 else 1 - flip
    at_far = pl.multiple_of(right * ROWS, HALF)
    win[pl.ds(at_far, HALF), :] = far[...]
    win[HALF : 2 * HALF, :] = middle[...]
    win[pl.ds(pl.multiple_of(ROWS - right * ROWS, HALF), HALF), :] = near[...]
    edge[...] = jnp.zeros_like(edge)
    scale = HD ** -0.5 * LOG2E
    span = range(GROUP // 2)
    query = [2 * right + k for k in span]
    starts = [
        pl.multiple_of(links[GROUP, 2 * query[k] + right] - right * NEAR_RIGHT, BLK) for k in span
    ]
    pair = [pairs[pl.ds(pl.multiple_of(2 * query[k] * BLK, 2 * BLK), 2 * BLK), :] for k in span]
    known = [
        [stats[pl.ds(pl.multiple_of(8 * (3 * query[k] + n), 8), 8), :][:1] for n in range(3)] for k in span
    ]
    blocks = [
        run_scores(links, win[pl.ds(starts[k], SPAN * BLK), :], pair[k], query[k], 1 + right) for k in span
    ]
    largest = [jnp.maximum(known[k][0], largest_of(blocks[k])) for k in span]
    found = [exponentials(blocks[k], largest[k]) for k in span]
    parts = []
    for k in span:
        terms, total, weighted = found[k]
        near_scale = jnp.exp2((known[k][0] - largest[k]) * scale)
        inverse = 1.0 / (total + near_scale * known[k][1])
        row_dot = (weighted + near_scale * known[k][2]) * inverse
        for n, row in enumerate((near_scale * inverse, row_dot)):
            scales[8 * (2 * k + n) : 8 * (2 * k + n + 1), :] = jnp.broadcast_to(row, (8, BLK))
        parts.append(
            jnp.concatenate([mix(term * inverse, block[1], row_dot) for term, block in zip(terms, blocks[k])], axis=0)
        )
    for k in span:
        mixed[far_rows(k), :] = parts[k]
        edge[pl.ds(starts[k], SPAN * BLK), :] += dot(parts[k], pair[k], ((1,), (0,)))
    far_out[...] = (edge[pl.ds(at_far, HALF), :] * side_factor()).astype(BF)


def by_side(i, from_u, from_d):
    left = i < GROUP // 2
    return jnp.where((position()[1] == 0) == left, from_u, from_d)


def near_grads_kernel(
    links, pairs, terms, prob_grads, u_scales, d_scales, u_edge, d_edge, mixed, first_own, second_own,
    u2_out, d2_out, u3_out, d3_out, acc,
):
    acc[NEAR_LEFT:OWN, :] = by_side(0, u_edge[NEAR_LEFT:OWN, :], d_edge[NEAR_LEFT:OWN, :])
    acc[OWN:NEAR_RIGHT, :] = jnp.zeros((ROWS, 2 * HD), F32)
    acc[NEAR_RIGHT:FAR_RIGHT, :] = by_side(GROUP - 1, u_edge[:ROWS, :], d_edge[:ROWS, :])
    for i in range(GROUP):
        pair = pairs[2 * i * BLK : 2 * (i + 1) * BLK, :]
        at = [8 * (2 * (i % 2) + n) for n in range(2)]
        scale, row_dot = (by_side(i, u_scales[r : r + 1, :], d_scales[r : r + 1, :]) for r in at)
        for index, t in enumerate(near_runs(i)):
            parts = []
            for j in range(SPAN):
                rows = near_rows(i, index, j)
                parts.append(mix(terms[rows, :] * scale, prob_grads[rows, :], row_dot))
                mixed[rows, :] = parts[-1]
            at = pl.ds(start_of(links, i, t), SPAN * BLK)
            acc[at, :] += dot(jnp.concatenate(parts, axis=0), pair, ((1,), (0,)))
    factor = side_factor()
    first, second, u1, d1, u2, _, d2, _ = regions(position()[1])
    first_own[...] = acc[pl.ds(first, HALF), :] * factor
    second_own[...] = acc[pl.ds(second, HALF), :] * factor
    for target, at in ((u2_out, d2), (d2_out, u2), (u3_out, d1), (d3_out, u1)):
        target[...] = (acc[pl.ds(at, HALF), :] * factor).astype(BF)


def outputs_kernel(
    links, near_mixed, u_mixed, d_mixed, first_kv, second_kv, u1, d1, u2, u3, d2, d3,
    att_own, att_other, dq_out, win, att,
):
    side, flip, _, _ = position()
    for at, half in zip(regions(flip), (first_kv, second_kv, u1, d1, u2, u3, d2, d3)):
        win[pl.ds(at, HALF), :] = half[...]
    for i in range(GROUP):
        rows = slice(i * BLK, (i + 1) * BLK)
        out = dot(
            by_side(i, u_mixed[far_rows(i % 2), :], d_mixed[far_rows(i % 2), :]), win[pl.ds(start_of(links, i, far_run(i)), SPAN * BLK), :], ((0,), (0,))
        )
        for index, t in enumerate(near_runs(i)):
            part = near_mixed[near_rows(i, index, 0).start : near_rows(i, index, SPAN - 1).stop, :]
            out = out + dot(part, win[pl.ds(start_of(links, i, t), SPAN * BLK), :], ((0,), (0,)))
        att[rows, :] = out[BLK:, HD:].astype(BF)
        dq_out[rows, :] = (out[:BLK, :HD] * (HD ** -0.5)).astype(BF)
    att_own[...] = att[pl.ds(pl.multiple_of(side * HALF, HALF), HALF), :]
    att_other[...] = att[pl.ds(pl.multiple_of((1 - side) * HALF, HALF), HALF), :]


def spread(grads, w_mine, side, head, target):
    out = dot(grads, weight_rows(w_mine, head, 2 * HD), ((1,), (1,))).astype(BF)
    target[:HALF, :] = jnp.where(side == 0, out[:HALF], out[HALF:])
    target[HALF:, :] = jnp.where(side == 0, out[HALF:], out[:HALF])


def spread_near_kernel(first_own, second_own, from_d, from_u, dq, w_mine, send, grads):
    side, flip, _, head = position()
    first = first_own[...] + from_d[...].astype(F32)
    second = second_own[...] + from_u[...].astype(F32)
    grads[:, :HD] = dq[...]
    grads[:HALF, HD:] = jnp.where(flip == 1, first, second).astype(BF)
    grads[HALF:, HD:] = jnp.where(flip == 1, second, first).astype(BF)
    spread(grads[...], w_mine, side, head ^ 1, send)


def spread_far_kernel(grads, w_mine, send):
    side, _, _, head = position()
    spread(grads[...], w_mine, side, head ^ 3, send)


def spread_keep_kernel(grads, w_mine, near, far):
    side, _, _, head = position()
    spread(grads[...], w_mine, side, head, near)
    spread(grads[...], w_mine, side, head ^ 2, far)


def body(features, w_qkv, block_links, d_out, n_ctx, n_head):
    n_group = n_ctx // 2

    def across(value, flip_ctx, flip_head):
        pairs = [
            (c * n_head + h, (c ^ flip_ctx) * n_head + (h ^ flip_head))
            for c in range(n_ctx)
            for h in range(n_head)
        ]
        return lax.ppermute(value, ("ctx", "head"), pairs)

    def chain(value, back):
        pairs = []
        for ctx in range(n_ctx):
            group, side = divmod(ctx, 2)
            for h in range(n_head):
                to = group + (1 if h % 2 == back else -1)
                inside = 0 <= to < n_group
                target = (2 * to + side) * n_head + h if inside else ctx * n_head + (h ^ 1)
                pairs.append((ctx * n_head + h, target))
        return lax.ppermute(value, ("ctx", "head"), pairs)

    f = features
    sx = across(f, 0, 2)
    sy = across(f, 1, 0)
    sd = across(f, 1, 2)
    w = jnp.transpose(w_qkv, (1, 0, 2))

    def call(kernel, name, outs, ins, mebibytes, flops, scratch=()):
        specs = [SMEM if v.dtype == jnp.int32 else VMEM for v in ins]
        if kernel is begin_kernel:
            specs = [pl.BlockSpec(memory_space=pltpu.HBM)] * 2
            ins = [pltpu.with_memory_space_constraint(v, pltpu.HBM) for v in ins]
        return pl.pallas_call(
            kernel,
            name=name,
            out_shape=outs,
            in_specs=specs,
            out_specs=[SMEM if v.dtype == jnp.int32 else VMEM for v in outs],
            scratch_shapes=list(scratch),
            **params(flops, 2 << 20, mebibytes),
        )(*ins)

    def out(rows, cols, kind=BF):
        return jax.ShapeDtypeStruct((rows, cols), kind)

    def held(rows, cols, kind=BF):
        return pltpu.VMEM((rows, cols), kind)

    product = 2 * ROWS * f.shape[1] * 3 * HD
    attention = 2 * GROUP * 9 * BLK * BLK * 2 * HD
    w_mine, fm, total = call(
        begin_kernel,
        "begin",
        [held(w.shape[1], 3 * HD), held(*f.shape), held(HALF, 3 * HD, F32)],
        (f, w),
        4,
        product,
        [pltpu.SemaphoreType.DMA((4,))],
    )
    (early,) = call(pack_kernel, "pack_early", [out(ROWS, f.shape[1])], (fm, sd), 4, 0)
    other_early = across(early, 0, 1)
    (late,) = call(pack_kernel, "pack_late", [out(ROWS, f.shape[1])], (sy, sx), 4, 0)
    other_late = across(late, 0, 1)
    (total,) = call(
        project_rest_kernel,
        "project_rest",
        [held(ROWS, 3 * HD, F32)],
        (total, early, late, other_early, w_mine),
        4,
        product,
    )
    first, second = call(
        project_kv_kernel, "project_kv", [out(HALF, 2 * HD)] * 2, (other_late, total, w_mine), 4, product
    )

    u1 = chain(first, 0)
    d1 = chain(second, 1)
    u2 = chain(second, 0)
    d2 = chain(first, 1)
    u3 = chain(u1, 0)
    d3 = chain(d1, 1)
    rows, slots = block_links.shape
    link_rows = jnp.pad(block_links.astype(BF), ((0, 16 - rows), (0, HD - slots)))
    (payload,) = call(payload_kernel, "payload", [out(HALF + 16, HD)], (d_out, link_rows, late), 4, 0)
    d_other = across(payload, 1, 0)
    (q,) = call(project_q_kernel, "project_q", [held(ROWS, HD)], (other_late, total, w_mine, u1, d1), 4, product)
    other_links = d_other[HALF : HALF + rows, :slots].astype(jnp.int32)
    (links,) = call(
        links_kernel, "links", [pltpu.SMEM((GROUP + 1, slots), jnp.int32)], (block_links, other_links, q), 4, 0
    )
    links = pltpu.with_memory_space_constraint(links, pltpu.SMEM)
    window = pltpu.VMEM((WINDOW * BLK, 2 * HD), BF)
    sums = pltpu.VMEM((WINDOW * BLK, 2 * HD), F32)
    run = SPAN * BLK
    pairs, terms, prob_grads, stats = call(
        near_scores_kernel,
        "near_scores",
        [
            held(GROUP * 2 * BLK, 2 * HD),
            held(GROUP * 2 * run, BLK, F32),
            held(GROUP * 2 * run, BLK, F32),
            held(GROUP * 3 * 8, BLK, F32),
        ],
        (links, q, first, second, u1, d1, u2, d2, d_out, d_other),
        6,
        attention,
        [window],
    )
    def far_grads(near, middle, far, after, which, name):
        return call(
            functools.partial(far_grads_kernel, chain=which),
            name,
            [
                held(GROUP // 2 * run, 2 * HD),
                held(OWN, 2 * HD, F32),
                out(HALF, 2 * HD),
                held(GROUP * 8, BLK, F32),
            ],
            (links, pairs, stats, near, middle, far, after),
            4,
            attention // 2,
            [pltpu.VMEM((OWN, 2 * HD), BF)],
        )

    u_mixed, u_edge, far_d_grad, u_scales = far_grads(u1, u2, u3, stats, 0, "far_grads_u")
    d_mixed, d_edge, far_u_grad, d_scales = far_grads(d1, d2, d3, far_d_grad, 1, "far_grads_d")
    near_mixed, first_own, second_own, u2_grad, d2_grad, u3_grad, d3_grad = call(
        near_grads_kernel,
        "near_grads",
        [held(GROUP * 2 * run, 2 * HD)] + [held(HALF, 2 * HD, F32)] * 2 + [out(HALF, 2 * HD)] * 4,
        (links, pairs, terms, prob_grads, u_scales, d_scales, u_edge, d_edge),
        4,
        attention,
        [sums],
    )
    att_own, att_other, dq = call(
        outputs_kernel,
        "outputs",
        [out(HALF, HD), out(HALF, HD), held(ROWS, HD)],
        (links, near_mixed, u_mixed, d_mixed, first, second, u1, d1, u2, u3, d2, d3),
        4,
        attention,
        [window, pltpu.VMEM((ROWS, HD), BF)],
    )

    back_d = chain(far_d_grad, 1)
    back_u = chain(far_u_grad, 0)
    d2_back = chain(d2_grad, 1)
    u2_back = chain(u2_grad, 0)

    def merge(one, two, name):
        return call(merge_kernel, name, [out(HALF, 2 * HD)], (one, two), 4, 0)[0]

    from_d = chain(merge(d3_grad, back_d, "merge_d"), 1)
    from_u = chain(merge(u3_grad, back_u, "merge_u"), 0)
    first_own, second_own = call(
        gather_kernel, "gather", [held(HALF, 2 * HD, F32)] * 2, (first_own, second_own, d2_back, u2_back), 4, 0
    )
    near_send, grads = call(
        spread_near_kernel,
        "spread_near",
        [out(ROWS, 2 * HD), held(ROWS, 3 * HD)],
        (first_own, second_own, from_d, from_u, dq, w_mine),
        4,
        product,
    )
    near_arrived = across(near_send, 0, 1)
    (far_send,) = call(spread_far_kernel, "spread_far", [out(ROWS, 2 * HD)], (grads, w_mine), 4, product)
    far_arrived = across(far_send, 0, 1)
    near, far = call(spread_keep_kernel, "spread_keep", [held(ROWS, 2 * HD)] * 2, (grads, w_mine), 4, product)
    mine, to_y = call(
        chip_sum_near_kernel,
        "chip_sum_near",
        [out(HALF, 2 * HD), out(HALF + BLK, 2 * HD)],
        (near, near_arrived, att_other),
        4,
        0,
    )
    gy = across(to_y, 1, 0)
    to_x, to_d = call(chip_sum_far_kernel, "chip_sum_far", [out(HALF, 2 * HD)] * 2, (far, far_arrived), 4, 0)
    gd = across(to_d, 1, 2)
    gx = across(to_x, 0, 2)
    attended, grad_features = call(
        finish_kernel, "finish", [out(HALF, 2 * HD)] * 2, (mine, gx, gd, gy, att_own), 4, 0
    )
    return attended, grad_features


def solution(mesh):
    sizes = dict(mesh.shape)
    return jax.shard_map(
        functools.partial(body, n_ctx=sizes["ctx"], n_head=sizes["head"]),
        mesh=mesh,
        in_specs=(P("ctx", "head"), P(None, None, "head"), P("ctx", None), P("ctx", "head")),
        out_specs=(P("ctx", "head"), P("ctx", "head")),
        check_vma=False,
    )
```

```python
import functools

import jax
import jax.numpy as jnp
from jax import lax
from jax.experimental import pallas as pl
from jax.experimental.pallas import tpu as pltpu
from jax.sharding import PartitionSpec as P

HD = 128
BLK = 128
REACH = 6
SPAN = 3
LOG2E = 1.4426950408889634
DEAD = -1e30
BF = jnp.bfloat16
F32 = jnp.float32

GROUP = 4
ROWS = GROUP * BLK
HALF = ROWS // 2
WINDOW = GROUP + 2 * REACH
NEAR_LEFT = (REACH - GROUP) * BLK
OWN = REACH * BLK
NEAR_RIGHT = OWN + ROWS
FAR_RIGHT = NEAR_RIGHT + ROWS


def params(flops, moved, mebibytes):
    return dict(
        compiler_params=pltpu.CompilerParams(vmem_limit_bytes=mebibytes * 1024 * 1024),
        cost_estimate=pl.CostEstimate(flops=flops, bytes_accessed=moved, transcendentals=0),
    )


VMEM = pl.BlockSpec(memory_space=pltpu.VMEM)
SMEM = pl.BlockSpec(memory_space=pltpu.SMEM)


def dot(a, b, dims):
    return lax.dot_general(a, b, (dims, ((), ())), preferred_element_type=F32)


def position():
    ctx, head = lax.axis_index("ctx"), lax.axis_index("head")
    return ctx % 2, head % 2, ctx // 2 * GROUP, head


def begin_kernel(f, w, w_mine, fm, total, sems):
    side, _, _, head = position()
    copies = [pltpu.make_async_copy(f, fm, sems.at[3])]
    for g in range(3):
        cols = pl.ds(pl.multiple_of(side * HD, HD), HD)
        copies.append(pltpu.make_async_copy(w.at[g, :, cols], w_mine.at[:, pl.ds(g * HD, HD)], sems.at[g]))
    for copy in copies:
        copy.start()
    for copy in copies:
        copy.wait()
    total[...] = dot(fm[...], weight_rows(w_mine, head, fm.shape[1]), ((1,), (0,)))


def weight_rows(w_mine, source, width):
    return w_mine[pl.ds(pl.multiple_of(source * width, width), width), :]


def pack_kernel(one, two, out):
    out[:HALF, :] = one[...]
    out[HALF:, :] = two[...]


def project_rest_kernel(before, early, late, other_early, w_mine, total):
    head = position()[3]
    width = early.shape[1]
    mine, across_x, sibling, across_both = (weight_rows(w_mine, head ^ k, width) for k in (0, 2, 1, 3))
    own = before[...] + dot(late[HALF:, :], across_x, ((1,), (0,)))
    total[:HALF, :] = own + dot(other_early[:HALF, :], sibling, ((1,), (0,)))
    partner = dot(late[:HALF, :], mine, ((1,), (0,))) + dot(early[HALF:, :], across_x, ((1,), (0,)))
    total[HALF:, :] = partner + dot(other_early[HALF:, :], across_both, ((1,), (0,)))


def last_product(head, other_late, w_mine, cols, group):
    width = other_late.shape[1]
    rows = pl.ds(pl.multiple_of((head ^ (3 if group == 0 else 1)) * width, width), width)
    piece = other_late[HALF:, :] if group == 0 else other_late[:HALF, :]
    return dot(piece, w_mine[rows, cols], ((1,), (0,)))


def project_kv_kernel(other_late, before, w_mine, first_out, second_out):
    side, flip, _, head = position()
    own, partner = (
        (before[g * HALF : (g + 1) * HALF, HD:] + last_product(head, other_late, w_mine, slice(HD, 3 * HD), g)).astype(BF)
        for g in range(2)
    )
    near_first = side ^ (1 - flip) == 0
    first_out[...] = jnp.where(near_first, own, partner)
    second_out[...] = jnp.where(near_first, partner, own)


def merge_kernel(one, two, out):
    out[...] = (one[...].astype(F32) + two[...].astype(F32)).astype(BF)


def gather_kernel(first_own, second_own, d, u, first_out, second_out):
    first_out[...] = first_own[...] + u[...].astype(F32)
    second_out[...] = second_own[...] + d[...].astype(F32)


def chip_sum_near_kernel(keep, arrived, att_other, mine, to_y):
    total = (keep[...].astype(F32) + arrived[...].astype(F32)).astype(BF)
    mine[...] = total[:HALF]
    to_y[:HALF, :] = total[HALF:]
    for half in range(2):
        to_y[HALF:, half * HD : (half + 1) * HD] = att_other[half * BLK : (half + 1) * BLK, :]


def chip_sum_far_kernel(keep, arrived, to_x, to_d):
    total = (keep[...].astype(F32) + arrived[...].astype(F32)).astype(BF)
    to_x[...] = total[:HALF]
    to_d[...] = total[HALF:]


def finish_kernel(mine, gd, gx, from_y, att_own, attended, grad_features):
    total = mine[...].astype(F32) + gd[...].astype(F32) + gx[...].astype(F32) + from_y[:HALF, :].astype(F32)
    grad_features[...] = total.astype(BF)
    side = position()[0]
    att_other = jnp.concatenate([from_y[HALF:, :HD], from_y[HALF:, HD:]], axis=0)
    for half in range(2):
        cols = slice(half * HD, (half + 1) * HD)
        attended[:, cols] = jnp.where(side == half, att_own[...], att_other)


def project_q_kernel(other_late, before, w_mine, u1, d1, q_out):
    del u1, d1
    side, _, _, head = position()
    for g in range(2):
        part = before[g * HALF : (g + 1) * HALF, :HD] + last_product(head, other_late, w_mine, slice(0, HD), g)
        q_out[pl.ds(pl.multiple_of((side ^ g) * HALF, HALF), HALF), :] = part.astype(BF)


def payload_kernel(d_own, link_rows, late, payload):
    del late
    side = position()[0]
    payload[:HALF, :] = jnp.where(side == 0, d_own[:, HD:], d_own[:, :HD])
    payload[HALF:, :] = link_rows[...]


def links_kernel(own, other, q, links):
    del q
    side, _, first, _ = position()
    for i in range(GROUP):
        for k in range(3 * SPAN):
            links[i, k] = jnp.where(side == i // 2, own[i % 2, k], other[i % 2, k])
        for t in (1, 2):
            base = jnp.int32(-(1 << 20))
            for j in range(SPAN):
                entry = links[i, SPAN * t + j]
                base = jnp.maximum(base, jnp.where(entry >= 0, entry - j, -(1 << 20)))
            base = jnp.where(base > -(1 << 19), base - first + REACH, i + 1 if t == 1 else i + REACH + SPAN)
            lowest = i if t == 1 else i + REACH + SPAN - 1
            links[GROUP, 2 * i + t - 1] = jnp.clip(base, lowest, lowest + 2) * BLK


def regions(flip):
    left_lo, left_hi = NEAR_LEFT, NEAR_LEFT + HALF
    right_lo, right_hi = NEAR_RIGHT, NEAR_RIGHT + HALF
    pick = lambda plain, flipped: pl.multiple_of((1 - flip) * plain + flip * flipped, HALF)
    return (
        pick(OWN + HALF, OWN),
        pick(OWN, OWN + HALF),
        pick(left_hi, right_lo),
        pick(right_lo, left_hi),
        pick(left_lo, right_hi),
        pick(0, FAR_RIGHT),
        pick(right_hi, left_lo),
        pick(FAR_RIGHT, 0),
    )


def start_of(links, i, t):
    if t == 0:
        return (REACH + i - 1) * BLK
    return pl.multiple_of(links[GROUP, 2 * i + t - 1], BLK)


def far_run(i):
    return 1 if i < GROUP // 2 else 2


def near_runs(i):
    return tuple(t for t in range(3) if t != far_run(i))


def near_rows(i, index, j):
    first = ((2 * i + index) * SPAN + j) * BLK
    return slice(first, first + BLK)


def far_rows(i):
    return slice(i * SPAN * BLK, (i + 1) * SPAN * BLK)


def run_scores(links, rows, pair, i, t):
    product = dot(rows, pair, ((1,), (1,)))
    blocks = []
    for j in range(SPAN):
        block = product[j * BLK : (j + 1) * BLK]
        bias = jnp.where(links[i, SPAN * t + j] >= 0, 0.0, DEAD).astype(F32)
        blocks.append((block[:, :BLK], block[:, BLK:], bias))
    return blocks


def fold(block):
    return block.reshape(BLK // 8, 8, BLK)


def largest_of(blocks):
    best = None
    for score, _, bias in blocks:
        peak = jnp.max(fold(score), axis=0) + bias
        best = peak if best is None else jnp.maximum(best, peak)
    return jnp.max(best, axis=0, keepdims=True)


def exponentials(blocks, largest):
    terms = []
    total = jnp.zeros((8, BLK), F32)
    weighted = jnp.zeros((8, BLK), F32)
    for score, prob_grad, bias in blocks:
        term = jnp.exp2((score - (largest - bias)) * (HD ** -0.5 * LOG2E))
        terms.append(term)
        total = total + jnp.sum(fold(term), axis=0)
        weighted = weighted + jnp.sum(fold(term * prob_grad), axis=0)
    return terms, jnp.sum(total, axis=0, keepdims=True), jnp.sum(weighted, axis=0, keepdims=True)


def mix(share, prob_grad, row_dot):
    grad = share * (prob_grad - row_dot)
    return jnp.concatenate([grad.astype(BF), share.astype(BF)], axis=1)


def side_factor():
    scale = HD ** -0.5
    return jnp.where(lax.broadcasted_iota(jnp.int32, (1, 2 * HD), 1) < HD, scale, 1.0).astype(F32)


def near_scores_kernel(
    links, q, first_kv, second_kv, u1, d1, u2, d2, d_own, d_other,
    pairs, terms_out, prob_grads_out, stats, win,
):
    side, flip, _, _ = position()
    places = regions(flip)
    for at, half in zip(places[:5] + places[6:7], (first_kv, second_kv, u1, d1, u2, d2)):
        win[pl.ds(at, HALF), :] = half[...]
    zeros = jnp.zeros((BLK, HD), BF)
    own_cols = pl.ds(pl.multiple_of(side * HD, HD), HD)
    for i in range(GROUP):
        rows = slice(i * BLK, (i + 1) * BLK)
        here = slice((i % 2) * BLK, (i % 2 + 1) * BLK)
        d_blk = jnp.where(side == i // 2, d_own[here, own_cols], d_other[here, :])
        pair = jnp.concatenate(
            [
                jnp.concatenate([q[rows, :], zeros], axis=1),
                jnp.concatenate([zeros, d_blk], axis=1),
            ],
            axis=0,
        )
        pairs[2 * i * BLK : 2 * (i + 1) * BLK, :] = pair
        blocks = []
        for t in near_runs(i):
            blocks += run_scores(links, win[pl.ds(start_of(links, i, t), SPAN * BLK), :], pair, i, t)
        largest = largest_of(blocks)
        terms, total, weighted = exponentials(blocks, largest)
        for n, term in enumerate(terms):
            terms_out[near_rows(i, 0, n), :] = term
            prob_grads_out[near_rows(i, 0, n), :] = blocks[n][1]
        for n, row in enumerate((largest, total, weighted)):
            stats[8 * (3 * i + n) : 8 * (3 * i + n + 1), :] = jnp.broadcast_to(row, (8, BLK))


def far_grads_kernel(links, pairs, stats, near, middle, far, after, mixed, edge, far_out, scales, win, chain):
    del after
    flip = position()[1]
    right = flip if chain == 0 else 1 - flip
    at_far = pl.multiple_of(right * ROWS, HALF)
    win[pl.ds(at_far, HALF), :] = far[...]
    win[HALF : 2 * HALF, :] = middle[...]
    win[pl.ds(pl.multiple_of(ROWS - right * ROWS, HALF), HALF), :] = near[...]
    edge[...] = jnp.zeros_like(edge)
    scale = HD ** -0.5 * LOG2E
    span = range(GROUP // 2)
    query = [2 * right + k for k in span]
    starts = [
        pl.multiple_of(links[GROUP, 2 * query[k] + right] - right * NEAR_RIGHT, BLK) for k in span
    ]
    pair = [pairs[pl.ds(pl.multiple_of(2 * query[k] * BLK, 2 * BLK), 2 * BLK), :] for k in span]
    known = [
        [stats[pl.ds(pl.multiple_of(8 * (3 * query[k] + n), 8), 8), :][:1] for n in range(3)] for k in span
    ]
    blocks = [
        run_scores(links, win[pl.ds(starts[k], SPAN * BLK), :], pair[k], query[k], 1 + right) for k in span
    ]
    largest = [jnp.maximum(known[k][0], largest_of(blocks[k])) for k in span]
    found = [exponentials(blocks[k], largest[k]) for k in span]
    parts = []
    for k in span:
        terms, total, weighted = found[k]
        near_scale = jnp.exp2((known[k][0] - largest[k]) * scale)
        inverse = 1.0 / (total + near_scale * known[k][1])
        row_dot = (weighted + near_scale * known[k][2]) * inverse
        for n, row in enumerate((near_scale * inverse, row_dot)):
            scales[8 * (2 * k + n) : 8 * (2 * k + n + 1), :] = jnp.broadcast_to(row, (8, BLK))
        parts.append(
            jnp.concatenate([mix(term * inverse, block[1], row_dot) for term, block in zip(terms, blocks[k])], axis=0)
        )
    for k in span:
        mixed[far_rows(k), :] = parts[k]
        edge[pl.ds(starts[k], SPAN * BLK), :] += dot(parts[k], pair[k], ((1,), (0,)))
    far_out[...] = (edge[pl.ds(at_far, HALF), :] * side_factor()).astype(BF)


def by_side(i, from_u, from_d):
    left = i < GROUP // 2
    return jnp.where((position()[1] == 0) == left, from_u, from_d)


def near_grads_kernel(
    links, pairs, terms, prob_grads, u_scales, d_scales, u_edge, d_edge, mixed, first_own, second_own,
    u2_out, d2_out, u3_out, d3_out, acc,
):
    acc[NEAR_LEFT:OWN, :] = by_side(0, u_edge[NEAR_LEFT:OWN, :], d_edge[NEAR_LEFT:OWN, :])
    acc[OWN:NEAR_RIGHT, :] = jnp.zeros((ROWS, 2 * HD), F32)
    acc[NEAR_RIGHT:FAR_RIGHT, :] = by_side(GROUP - 1, u_edge[:ROWS, :], d_edge[:ROWS, :])
    runs = []
    for i in range(GROUP):
        at = [8 * (2 * (i % 2) + n) for n in range(2)]
        scale, row_dot = (by_side(i, u_scales[r : r + 1, :], d_scales[r : r + 1, :]) for r in at)
        for index, t in enumerate(near_runs(i)):
            parts = []
            for j in range(SPAN):
                rows = near_rows(i, index, j)
                parts.append(mix(terms[rows, :] * scale, prob_grads[rows, :], row_dot))
                mixed[rows, :] = parts[-1]
            runs.append((i, t, jnp.concatenate(parts, axis=0)))
    for i, t, part in runs:
        at = pl.ds(start_of(links, i, t), SPAN * BLK)
        acc[at, :] += dot(part, pairs[2 * i * BLK : 2 * (i + 1) * BLK, :], ((1,), (0,)))
    factor = side_factor()
    first, second, u1, d1, u2, _, d2, _ = regions(position()[1])
    first_own[...] = acc[pl.ds(first, HALF), :] * factor
    second_own[...] = acc[pl.ds(second, HALF), :] * factor
    for target, at in ((u2_out, d2), (d2_out, u2), (u3_out, d1), (d3_out, u1)):
        target[...] = (acc[pl.ds(at, HALF), :] * factor).astype(BF)


def outputs_kernel(
    links, near_mixed, u_mixed, d_mixed, first_kv, second_kv, u1, d1, u2, u3, d2, d3,
    att_own, att_other, dq_out, win, att,
):
    side, flip, _, _ = position()
    for at, half in zip(regions(flip), (first_kv, second_kv, u1, d1, u2, u3, d2, d3)):
        win[pl.ds(at, HALF), :] = half[...]
    for i in range(GROUP):
        rows = slice(i * BLK, (i + 1) * BLK)
        out = dot(
            by_side(i, u_mixed[far_rows(i % 2), :], d_mixed[far_rows(i % 2), :]), win[pl.ds(start_of(links, i, far_run(i)), SPAN * BLK), :], ((0,), (0,))
        )
        for index, t in enumerate(near_runs(i)):
            part = near_mixed[near_rows(i, index, 0).start : near_rows(i, index, SPAN - 1).stop, :]
            out = out + dot(part, win[pl.ds(start_of(links, i, t), SPAN * BLK), :], ((0,), (0,)))
        att[rows, :] = out[BLK:, HD:].astype(BF)
        dq_out[rows, :] = (out[:BLK, :HD] * (HD ** -0.5)).astype(BF)
    att_own[...] = att[pl.ds(pl.multiple_of(side * HALF, HALF), HALF), :]
    att_other[...] = att[pl.ds(pl.multiple_of((1 - side) * HALF, HALF), HALF), :]


def spread(grads, w_mine, side, head, target):
    out = dot(grads, weight_rows(w_mine, head, 2 * HD), ((1,), (1,))).astype(BF)
    target[:HALF, :] = jnp.where(side == 0, out[:HALF], out[HALF:])
    target[HALF:, :] = jnp.where(side == 0, out[HALF:], out[:HALF])


def spread_near_kernel(first_own, second_own, from_d, from_u, dq, w_mine, send, grads):
    side, flip, _, head = position()
    first = first_own[...] + from_d[...].astype(F32)
    second = second_own[...] + from_u[...].astype(F32)
    grads[:, :HD] = dq[...]
    grads[:HALF, HD:] = jnp.where(flip == 1, first, second).astype(BF)
    grads[HALF:, HD:] = jnp.where(flip == 1, second, first).astype(BF)
    spread(grads[...], w_mine, side, head ^ 1, send)


def spread_far_kernel(grads, w_mine, send):
    side, _, _, head = position()
    spread(grads[...], w_mine, side, head ^ 3, send)


def spread_keep_kernel(grads, w_mine, near, far):
    side, _, _, head = position()
    spread(grads[...], w_mine, side, head, near)
    spread(grads[...], w_mine, side, head ^ 2, far)


def body(features, w_qkv, block_links, d_out, n_ctx, n_head):
    n_group = n_ctx // 2

    def across(value, flip_ctx, flip_head):
        pairs = [
            (c * n_head + h, (c ^ flip_ctx) * n_head + (h ^ flip_head))
            for c in range(n_ctx)
            for h in range(n_head)
        ]
        return lax.ppermute(value, ("ctx", "head"), pairs)

    def chain(value, back):
        pairs = []
        for ctx in range(n_ctx):
            group, side = divmod(ctx, 2)
            for h in range(n_head):
                to = group + (1 if h % 2 == back else -1)
                inside = 0 <= to < n_group
                target = (2 * to + side) * n_head + h if inside else ctx * n_head + (h ^ 1)
                pairs.append((ctx * n_head + h, target))
        return lax.ppermute(value, ("ctx", "head"), pairs)

    f = features
    sx = across(f, 0, 2)
    sy = across(f, 1, 0)
    sd = across(f, 1, 2)
    w = jnp.transpose(w_qkv, (1, 0, 2))

    def call(kernel, name, outs, ins, mebibytes, flops, scratch=()):
        specs = [SMEM if v.dtype == jnp.int32 else VMEM for v in ins]
        if kernel is begin_kernel:
            specs = [pl.BlockSpec(memory_space=pltpu.HBM)] * 2
            ins = [pltpu.with_memory_space_constraint(v, pltpu.HBM) for v in ins]
        return pl.pallas_call(
            kernel,
            name=name,
            out_shape=outs,
            in_specs=specs,
            out_specs=[SMEM if v.dtype == jnp.int32 else VMEM for v in outs],
            scratch_shapes=list(scratch),
            **params(flops, 2 << 20, mebibytes),
        )(*ins)

    def out(rows, cols, kind=BF):
        return jax.ShapeDtypeStruct((rows, cols), kind)

    def held(rows, cols, kind=BF):
        return pltpu.VMEM((rows, cols), kind)

    product = 2 * ROWS * f.shape[1] * 3 * HD
    attention = 2 * GROUP * 9 * BLK * BLK * 2 * HD
    w_mine, fm, total = call(
        begin_kernel,
        "begin",
        [held(w.shape[1], 3 * HD), held(*f.shape), held(HALF, 3 * HD, F32)],
        (f, w),
        4,
        product,
        [pltpu.SemaphoreType.DMA((4,))],
    )
    (early,) = call(pack_kernel, "pack_early", [out(ROWS, f.shape[1])], (fm, sd), 4, 0)
    other_early = across(early, 0, 1)
    (late,) = call(pack_kernel, "pack_late", [out(ROWS, f.shape[1])], (sy, sx), 4, 0)
    other_late = across(late, 0, 1)
    (total,) = call(
        project_rest_kernel,
        "project_rest",
        [held(ROWS, 3 * HD, F32)],
        (total, early, late, other_early, w_mine),
        4,
        product,
    )
    first, second = call(
        project_kv_kernel, "project_kv", [out(HALF, 2 * HD)] * 2, (other_late, total, w_mine), 4, product
    )

    u1 = chain(first, 0)
    d1 = chain(second, 1)
    u2 = chain(second, 0)
    d2 = chain(first, 1)
    u3 = chain(u1, 0)
    d3 = chain(d1, 1)
    rows, slots = block_links.shape
    link_rows = jnp.pad(block_links.astype(BF), ((0, 16 - rows), (0, HD - slots)))
    (payload,) = call(payload_kernel, "payload", [out(HALF + 16, HD)], (d_out, link_rows, late), 4, 0)
    d_other = across(payload, 1, 0)
    (q,) = call(project_q_kernel, "project_q", [held(ROWS, HD)], (other_late, total, w_mine, u1, d1), 4, product)
    other_links = d_other[HALF : HALF + rows, :slots].astype(jnp.int32)
    (links,) = call(
        links_kernel, "links", [pltpu.SMEM((GROUP + 1, slots), jnp.int32)], (block_links, other_links, q), 4, 0
    )
    links = pltpu.with_memory_space_constraint(links, pltpu.SMEM)
    window = pltpu.VMEM((WINDOW * BLK, 2 * HD), BF)
    sums = pltpu.VMEM((WINDOW * BLK, 2 * HD), F32)
    run = SPAN * BLK
    pairs, terms, prob_grads, stats = call(
        near_scores_kernel,
        "near_scores",
        [
            held(GROUP * 2 * BLK, 2 * HD),
            held(GROUP * 2 * run, BLK, F32),
            held(GROUP * 2 * run, BLK, F32),
            held(GROUP * 3 * 8, BLK, F32),
        ],
        (links, q, first, second, u1, d1, u2, d2, d_out, d_other),
        6,
        attention,
        [window],
    )
    def far_grads(near, middle, far, after, which, name):
        return call(
            functools.partial(far_grads_kernel, chain=which),
            name,
            [
                held(GROUP // 2 * run, 2 * HD),
                held(OWN, 2 * HD, F32),
                out(HALF, 2 * HD),
                held(GROUP * 8, BLK, F32),
            ],
            (links, pairs, stats, near, middle, far, after),
            4,
            attention // 2,
            [pltpu.VMEM((OWN, 2 * HD), BF)],
        )

    u_mixed, u_edge, far_d_grad, u_scales = far_grads(u1, u2, u3, stats, 0, "far_grads_u")
    d_mixed, d_edge, far_u_grad, d_scales = far_grads(d1, d2, d3, far_d_grad, 1, "far_grads_d")
    near_mixed, first_own, second_own, u2_grad, d2_grad, u3_grad, d3_grad = call(
        near_grads_kernel,
        "near_grads",
        [held(GROUP * 2 * run, 2 * HD)] + [held(HALF, 2 * HD, F32)] * 2 + [out(HALF, 2 * HD)] * 4,
        (links, pairs, terms, prob_grads, u_scales, d_scales, u_edge, d_edge),
        8,
        attention,
        [sums],
    )
    att_own, att_other, dq = call(
        outputs_kernel,
        "outputs",
        [out(HALF, HD), out(HALF, HD), held(ROWS, HD)],
        (links, near_mixed, u_mixed, d_mixed, first, second, u1, d1, u2, u3, d2, d3),
        4,
        attention,
        [window, pltpu.VMEM((ROWS, HD), BF)],
    )

    back_d = chain(far_d_grad, 1)
    back_u = chain(far_u_grad, 0)
    d2_back = chain(d2_grad, 1)
    u2_back = chain(u2_grad, 0)

    def merge(one, two, name):
        return call(merge_kernel, name, [out(HALF, 2 * HD)], (one, two), 4, 0)[0]

    from_d = chain(merge(d3_grad, back_d, "merge_d"), 1)
    from_u = chain(merge(u3_grad, back_u, "merge_u"), 0)
    first_own, second_own = call(
        gather_kernel, "gather", [held(HALF, 2 * HD, F32)] * 2, (first_own, second_own, d2_back, u2_back), 4, 0
    )
    near_send, grads = call(
        spread_near_kernel,
        "spread_near",
        [out(ROWS, 2 * HD), held(ROWS, 3 * HD)],
        (first_own, second_own, from_d, from_u, dq, w_mine),
        4,
        product,
    )
    near_arrived = across(near_send, 0, 1)
    (far_send,) = call(spread_far_kernel, "spread_far", [out(ROWS, 2 * HD)], (grads, w_mine), 4, product)
    far_arrived = across(far_send, 0, 1)
    near, far = call(spread_keep_kernel, "spread_keep", [held(ROWS, 2 * HD)] * 2, (grads, w_mine), 4, product)
    mine, to_y = call(
        chip_sum_near_kernel,
        "chip_sum_near",
        [out(HALF, 2 * HD), out(HALF + BLK, 2 * HD)],
        (near, near_arrived, att_other),
        4,
        0,
    )
    gy = across(to_y, 1, 0)
    to_x, to_d = call(chip_sum_far_kernel, "chip_sum_far", [out(HALF, 2 * HD)] * 2, (far, far_arrived), 4, 0)
    gd = across(to_d, 1, 2)
    gx = across(to_x, 0, 2)
    attended, grad_features = call(
        finish_kernel, "finish", [out(HALF, 2 * HD)] * 2, (mine, gd, gx, gy, att_own), 4, 0
    )
    return attended, grad_features


def solution(mesh):
    sizes = dict(mesh.shape)
    return jax.shard_map(
        functools.partial(body, n_ctx=sizes["ctx"], n_head=sizes["head"]),
        mesh=mesh,
        in_specs=(P("ctx", "head"), P(None, None, "head"), P("ctx", None), P("ctx", "head")),
        out_specs=(P("ctx", "head"), P("ctx", "head")),
        check_vma=False,
    )
```
